256 devices in a mesh: dp: 16 (over z, x_lo), seq: 16 (over y, x_hi, core).
Axes of the slice: x: 4 (x_hi: 2, x_lo: 2; x = x_hi * 2 + x_lo), y: 4, z: 8, core: 2. Of those that a mesh axis runs over, the one named last changes fastest.
Arguments:
- inputs: bfloat16 [16, 2048, 768], P('dp', 'seq'), may hold values from -6 to 6
- convolution_weight: bfloat16 [5, 768, 768], replicated, may hold values from -0.09375 to 0.09375
- w_qkv: bfloat16 [768, 3072], replicated, may hold values from -0.21875 to 0.21875
- gain: float32 [768], replicated, may hold values from 0.5 to 1.5
- out_grad: bfloat16 [16, 2048, 1024], P('dp', 'seq'), may hold values from -6 to 6
Outputs:
- attended: bfloat16 [16, 2048, 1024], P('dp', 'seq')
- grad_input: bfloat16 [16, 2048, 768], P('dp', 'seq')
- grad_conv: float32 [5, 768, 768], P(None, None, 'seq')
- grad_qkv: float32 [768, 3072], P(None, 'seq')
The draws below stay inside these ranges and needn't reach their ends.
All inputs are finite; a program needn't handle non-finite values.
Results may differ from the reference program's by a relative error of at most 0.023.
Values may be sent and summed in bfloat16 or wider, within the bound.
A program may use at most 128 MiB of HBM per device.

```python
import jax
import jax.numpy as jnp
from jax import lax

CH = 768
HEADS = 8
HD = 128
KERNEL_TAPS = 5
TAP_SPACING = 16
LEN = 2048
BATCH = 16


def block_levels(key, shape, cuts, low, high):
    loudness, own = 1.0, jax.random.fold_in(key, 6)
    for dim, shards_of in cuts:
        draws = jnp.exp(jax.random.uniform(jax.random.fold_in(own, dim), (shards_of,), jnp.float32, low / len(cuts), high / len(cuts)))
        loudness = loudness * jnp.repeat(draws, shape[dim] // shards_of).reshape([-1 if axis == dim else 1 for axis in range(len(shape))])
    return loudness


def noise(rng, dims, spread, bound, pieces=(), dtype=jnp.bfloat16):
    level = block_levels(rng, dims, pieces, -0.22, 0.18) if pieces else 1.0
    values = jax.random.normal(rng, dims, jnp.float32) * spread * level
    return jnp.minimum(jnp.maximum(values, -bound), bound).astype(dtype)


def setup_inputs(seed: int = 0) -> dict:
    splits = jax.random.split(jax.random.key(seed), 6)
    inputs = noise(splits[0], (BATCH, LEN, CH), 1.0, 6.0, ((0, 16), (1, 16)))
    convolution_weight = noise(splits[1], (KERNEL_TAPS, CH, CH), (KERNEL_TAPS * CH) ** -0.5, 0.09375)
    w_qkv = noise(splits[2], (CH, 3 * HEADS * HD), CH ** -0.5, 0.21875)
    gain = jnp.clip(1.0 + 0.1 * jax.random.normal(splits[3], (CH,), jnp.float32), 0.5, 1.5)
    out_grad = noise(splits[4], (BATCH, LEN, HEADS * HD), 1.0, 6.0, ((0, 16), (1, 16)))
    return {"inputs": inputs, "convolution_weight": convolution_weight, "w_qkv": w_qkv, "gain": gain, "out_grad": out_grad}


def one_sequence(inputs, convolution_weight, w_qkv, gain, out_grad):
    sequence_length = inputs.shape[0]
    inner = HEADS * HD
    half_reach = KERNEL_TAPS // 2
    temper = HD ** (-0.5)
    local_in = inputs.astype(jnp.float32)
    acted, gelu_back = jax.vjp(jax.nn.gelu, local_in)
    activated_low_precision = acted.astype(jnp.bfloat16)
    padded_rows = jnp.pad(activated_low_precision, ((half_reach * TAP_SPACING, half_reach * TAP_SPACING), (0, 0)))
    convolved_output = jnp.zeros((sequence_length, CH), jnp.float32)
    for tap_number in range(KERNEL_TAPS):
        convolved_output = convolved_output + jnp.dot(padded_rows[tap_number * TAP_SPACING:tap_number * TAP_SPACING + sequence_length], convolution_weight[tap_number], preferred_element_type=jnp.float32)
    hidden = local_in + convolved_output
    inv_rms = lax.rsqrt(lax.optimization_barrier(jnp.mean(hidden * hidden, -1, keepdims=True)) + 1e-06)
    normed = hidden * inv_rms
    normed_bf = (normed * gain).astype(jnp.bfloat16)
    qkv = jnp.dot(normed_bf, w_qkv, preferred_element_type=jnp.float32).astype(jnp.bfloat16)
    query = qkv[:, :inner].reshape(sequence_length, HEADS, HD).astype(jnp.float32)
    keys = qkv[:, inner:2 * inner].reshape(sequence_length, HEADS, HD).astype(jnp.float32)
    values = qkv[:, 2 * inner:].reshape(sequence_length, HEADS, HD).astype(jnp.float32)
    scores = jnp.einsum('qhd,khd->hqk', query, keys) * temper
    highest = lax.optimization_barrier(jnp.max(scores, -1, keepdims=True))
    expo = jnp.exp(scores - highest)
    denom = lax.optimization_barrier(jnp.sum(expo, -1, keepdims=True))
    log_total = highest + jnp.log(denom)
    weights_bf = jnp.exp(scores - log_total).astype(jnp.bfloat16)
    attended = jnp.einsum('hqk,khd->qhd', weights_bf.astype(jnp.float32), values).astype(jnp.bfloat16)
    grad_heads = out_grad.reshape(sequence_length, HEADS, HD).astype(jnp.float32)
    back_weights = jnp.exp(scores - log_total)
    grad_weights = jnp.einsum('qhd,khd->hqk', grad_heads, values)
    row_dots = lax.optimization_barrier(jnp.sum(grad_heads * attended.astype(jnp.float32), -1)).T
    grad_scores = (back_weights * (grad_weights - row_dots[..., None])).astype(jnp.bfloat16).astype(jnp.float32)
    grad_query = (jnp.einsum('hqk,khd->qhd', grad_scores, keys) * temper).astype(jnp.bfloat16)
    grad_key = (jnp.einsum('hqk,qhd->khd', grad_scores, query) * temper).astype(jnp.bfloat16)
    grad_value = jnp.einsum('hqk,qhd->khd', back_weights.astype(jnp.bfloat16).astype(jnp.float32), grad_heads).astype(jnp.bfloat16)
    grad_rows = jnp.concatenate([grad_query.reshape(sequence_length, inner), grad_key.reshape(sequence_length, inner), grad_value.reshape(sequence_length, inner)], 1)
    grad_normed = jnp.dot(grad_rows, w_qkv.T, preferred_element_type=jnp.float32)
    scaled = grad_normed * gain
    grad_hidden = inv_rms * (scaled - normed * lax.optimization_barrier(jnp.mean(scaled * normed, -1, keepdims=True)))
    convolved_output_gradient = grad_hidden.astype(jnp.bfloat16)
    border_rows = jnp.pad(convolved_output_gradient, ((half_reach * TAP_SPACING, half_reach * TAP_SPACING), (0, 0)))
    grad_acted = jnp.zeros((sequence_length, CH), jnp.float32)
    for tap_number in range(KERNEL_TAPS):
        window_start = (KERNEL_TAPS - 1 - tap_number) * TAP_SPACING
        grad_acted = grad_acted + jnp.dot(border_rows[window_start:window_start + sequence_length], convolution_weight[tap_number].T, preferred_element_type=jnp.float32)
    grad_input = (grad_hidden + gelu_back(grad_acted)[0]).astype(jnp.bfloat16)
    qkv_part = jnp.dot(normed_bf.T, grad_rows, preferred_element_type=jnp.float32)
    convolved_partial = jnp.stack([jnp.dot(padded_rows[tap_number * TAP_SPACING:tap_number * TAP_SPACING + sequence_length].T, convolved_output_gradient, preferred_element_type=jnp.float32) for tap_number in range(KERNEL_TAPS)], 0)
    return (attended.reshape(sequence_length, inner), grad_input, convolved_partial, qkv_part)

def reference(inputs, convolution_weight, w_qkv, gain, out_grad):

    def single(pair):
        return one_sequence(pair[0], convolution_weight, w_qkv, gain, pair[1])
    results = lax.map(single, (inputs, out_grad))
    return (results[0], results[1], lax.optimization_barrier(jnp.sum(results[2], 0)), lax.optimization_barrier(jnp.sum(results[3], 0)))
```

```python
import functools

import jax
import jax.numpy as jnp
from jax import lax
from jax.experimental import pallas as pl
from jax.experimental.pallas import tpu as pltpu
from jax.sharding import PartitionSpec as P

CH = 768
HEADS = 8
HD = 128
TAPS = 5
GAP = 16
HALO = 32
ROWS = 128
SEQ = 16
DP = 16
CHIPS = 8
TILE = 256
TEMPER = HD ** (-0.5)
LOG2E = 1.4426950408889634
GELU_A = 0.7978845608028654
GELU_B = 0.044715
BF = jnp.bfloat16
F32 = jnp.float32
MESH = pl.DeviceIdType.MESH


def rcopy(src, dst, ss, rs, dev):
    return pltpu.make_async_remote_copy(
        src_ref=src, dst_ref=dst, send_sem=ss, recv_sem=rs, device_id=dev, device_id_type=MESH
    )


def dot(a, b):
    return jnp.dot(a, b, preferred_element_type=F32)


def dot_nt(a, b):
    return lax.dot_general(a, b, (((1,), (1,)), ((), ())), preferred_element_type=F32)


def flip(a):
    return a.astype(F32).T


def kernel(
    x_ref, gain_ref, og_ref, cw_hbm, w_hbm,
    att_ref, gi_ref, ct_out, gq_out,
    cwv, wfull, wh, act, normed_s, inv_s, nh, doh, qh, kv, kvt, s_ref, dkv, pr,
    odq, gsrc, gt, res, ah, gtf, gst, grcv, gown, gq, bext, bst, bh, bt, cg, cst, crcv, ct,
    rc, rq, cfin, gfin,
    wsem, hs, hr, dos, dor, nhs, nhr, kvs, kvr, ahs, ahr, os_, or_, ks, kr, prs, prr,
    gps, gpr, gus, gur, h2s, h2r, bs, br, cps, cpr, rcs, rcr, rqs, rqr, fcs, fcr, fqs, fqr,
):
    j = lax.axis_index("seq")
    d = lax.axis_index("dp")
    c = j // 2
    k = j % 2
    mate = {"seq": j + 1 - 2 * k}

    def same(chip):
        return {"seq": chip * 2 + k}

    order = (2, 0, 1, 3, 4)
    cw_copies = {t: pltpu.make_async_copy(cw_hbm.at[t], cwv.at[t], wsem.at[t]) for t in order}
    for t in order:
        cw_copies[t].start()
    col = pl.multiple_of(c * HD, HD)
    wh_copies = [
        pltpu.make_async_copy(
            w_hbm.at[:, pl.ds(p * HEADS * HD + col, HD)], wh.at[:, pl.ds(p * HD, HD)], wsem.at[5 + p]
        )
        for p in range(3)
    ]
    for cp in wh_copies:
        cp.start()
    wf_copy = pltpu.make_async_copy(w_hbm, wfull, wsem.at[8])
    wf_copy.start()

    barrier = pltpu.get_barrier_semaphore()

    def hello(i, carry):
        pl.semaphore_signal(barrier, inc=1, device_id={"seq": (j + i) % SEQ}, device_id_type=MESH)
        pl.semaphore_signal(barrier, inc=1, device_id={"dp": (d + i) % DP}, device_id_type=MESH)
        return carry

    lax.fori_loop(1, 16, hello, 0)

    x = x_ref[...].astype(F32)
    th = jnp.tanh(GELU_A * (x + GELU_B * x * x * x))
    act[HALO : HALO + ROWS, :] = (0.5 * x * (1.0 + th)).astype(BF)

    @pl.when(j == 0)
    def _():
        act[0:HALO, :] = jnp.zeros((HALO, CH), BF)
        bext[0:HALO, :] = jnp.zeros((HALO, CH), BF)

    @pl.when(j == SEQ - 1)
    def _():
        act[HALO + ROWS :, :] = jnp.zeros((HALO, CH), BF)
        bext[HALO + ROWS :, :] = jnp.zeros((HALO, CH), BF)

    pl.semaphore_wait(barrier, 30)

    def halo(buf, ss, rs):
        up = rcopy(buf.at[ROWS : ROWS + HALO], buf.at[0:HALO], ss.at[0], rs.at[0], {"seq": (j + 1) % SEQ})
        down = rcopy(
            buf.at[HALO : 2 * HALO], buf.at[HALO + ROWS : 2 * HALO + ROWS], ss.at[1], rs.at[1],
            {"seq": (j + SEQ - 1) % SEQ},
        )

        def start():
            pl.when(j < SEQ - 1)(up.start)
            pl.when(j > 0)(down.start)

        def wait_recv():
            pl.when(j > 0)(up.wait_recv)
            pl.when(j < SEQ - 1)(down.wait_recv)

        def wait_send():
            pl.when(j < SEQ - 1)(up.wait_send)
            pl.when(j > 0)(down.wait_send)

        return start, wait_recv, wait_send

    h_start, h_recv, h_send = halo(act, hs, hr)
    h_start()

    def do_copy(r):
        b = (c + r) % CHIPS
        src = og_ref.at[:, pl.ds(pl.multiple_of(b * HD, HD), HD)]
        return rcopy(src, doh.at[c], dos.at[b], dor.at[c], same(b))

    for r in range(1, CHIPS):
        do_copy(r).start()
    doh[c] = og_ref[:, pl.ds(col, HD)]

    cw_copies[2].wait()
    conv = dot(act[HALO : HALO + ROWS, :], cwv[2])
    h_recv()
    for t in (0, 1, 3, 4):
        cw_copies[t].wait()
        conv = conv + dot(act[t * GAP : t * GAP + ROWS, :], cwv[t])
    hidden = x_ref[...].astype(F32) + conv
    inv = lax.rsqrt(jnp.mean(hidden * hidden, -1, keepdims=True) + 1e-6)
    normed = hidden * inv
    normed_s[...] = normed
    inv_s[...] = jnp.broadcast_to(inv, (ROWS, HD))
    nh[c] = (normed * gain_ref[...]).astype(BF)

    def nh_copy(r):
        b = (c + r) % CHIPS
        return rcopy(nh.at[c], nh.at[c], nhs.at[b], nhr.at[c], same(b))

    def nh_wait(b):
        rcopy(nh.at[b], nh.at[b], nhs.at[b], nhr.at[b], same(b)).wait_recv()

    for r in range(1, CHIPS):
        nh_copy(r).start()

    for cp in wh_copies:
        cp.wait()

    def kv_copy(b):
        return rcopy(kv.at[k, b], kv.at[k, b], kvs.at[b], kvr.at[b], mate)

    def project(b):
        out = dot(nh[b], wh[...]).astype(BF)
        qh[b] = out[:, :HD]
        kv[k, b] = out[:, HD:]
        kv_copy(b).start()
        lane = pl.multiple_of(k * (CHIPS * ROWS) + b * ROWS, ROWS)
        kvt[0, :, pl.ds(lane, ROWS)] = flip(out[:, HD : 2 * HD]).astype(BF)
        kvt[1, :, pl.ds(lane, ROWS)] = flip(out[:, 2 * HD :]).astype(BF)

    project(c)

    def project_next(i, carry):
        b = (c + CHIPS - i) % CHIPS
        nh_wait(b)
        project(b)
        return carry

    lax.fori_loop(1, CHIPS, project_next, 0)

    mine = act.at[HALO : HALO + ROWS]

    def ah_copy(r):
        b = (c + r) % CHIPS
        return rcopy(mine, ah.at[c], ahs.at[b], ahr.at[c], same(b))

    for r in range(1, CHIPS):
        ah_copy(r).start()
    ah[c] = act[HALO : HALO + ROWS, :]

    dkv[...] = jnp.zeros_like(dkv)

    def other_keys(b, carry):
        rcopy(kv.at[1 - k, b], kv.at[1 - k, b], kvs.at[b], kvr.at[b], mate).wait_recv()
        lane = pl.multiple_of((1 - k) * (CHIPS * ROWS) + b * ROWS, ROWS)
        kvt[0, :, pl.ds(lane, ROWS)] = flip(kv[1 - k, b, :, :HD]).astype(BF)
        kvt[1, :, pl.ds(lane, ROWS)] = flip(kv[1 - k, b, :, HD:]).astype(BF)
        return carry

    lax.fori_loop(0, CHIPS, other_keys, 0)
    for r in range(1, CHIPS):
        b = (c + r) % CHIPS
        rcopy(doh.at[b], doh.at[b], dos.at[b], dor.at[b], same(b)).wait_recv()

    def chunk(i, half):
        two = kv[i // 4, (i % 4) * 2 : (i % 4) * 2 + 2, :, half * HD : (half + 1) * HD]
        return two.reshape(TILE, HD)

    def odq_copy(b):
        return rcopy(
            odq.at[:, b], res.at[0:2, :, pl.ds(col, HD)], os_.at[b], or_.at[c], same(b)
        )

    def tile(t, carry):
        b0 = (c + 1 + 2 * t) % CHIPS
        b1 = (c + 2 + 2 * t) % CHIPS
        q = jnp.concatenate([qh[b0], qh[b1]], axis=0)
        go = jnp.concatenate([doh[b0], doh[b1]], axis=0)
        qt = flip(q).astype(BF)
        got_f = flip(go)
        got = got_f.astype(BF)
        top = None
        for i in range(8):
            s = dot(chunk(i, 0), qt)
            s_ref[i * TILE : (i + 1) * TILE, :] = s
            part = jnp.max(s.reshape(TILE // 8, 8, TILE), axis=0)
            top = part if top is None else jnp.maximum(top, part)
        top = jnp.max(top, axis=0, keepdims=True) * (TEMPER * LOG2E)
        total = jnp.zeros((8, TILE), F32)
        for i in range(8):
            p = jnp.exp2(s_ref[i * TILE : (i + 1) * TILE, :] * (TEMPER * LOG2E) - top)
            s_ref[i * TILE : (i + 1) * TILE, :] = p
            total = total + jnp.sum(p.reshape(TILE // 8, 8, TILE), axis=0)
        rec = 1.0 / jnp.sum(total, axis=0, keepdims=True)
        ot = jnp.zeros((HD, TILE), F32)
        for i in range(8):
            w = s_ref[i * TILE : (i + 1) * TILE, :] * rec
            s_ref[i * TILE : (i + 1) * TILE, :] = w
            wb = w.astype(BF)
            ot = ot + dot(kvt[1, :, i * TILE : (i + 1) * TILE], wb)
            rows = pl.ds((i % 4) * TILE, TILE)
            dkv[i // 4, rows, HD:] = dkv[i // 4, rows, HD:] + dot(wb, go)
        otb = ot.astype(BF).astype(F32)
        dots = jnp.sum(got_f * otb, axis=0, keepdims=True)
        dqt = jnp.zeros((HD, TILE), F32)
        for i in range(8):
            gw = dot(chunk(i, 1), got)
            ds = (s_ref[i * TILE : (i + 1) * TILE, :] * (gw - dots)).astype(BF)
            dqt = dqt + dot(kvt[0, :, i * TILE : (i + 1) * TILE], ds)
            rows = pl.ds((i % 4) * TILE, TILE)
            dkv[i // 4, rows, :HD] = dkv[i // 4, rows, :HD] + dot(ds, q)
        dqt = dqt * TEMPER
        o = otb.T.astype(BF)
        dq = dqt.T.astype(BF)
        dqtb = dqt.astype(BF)
        odq[0, b0] = o[:ROWS]
        odq[0, b1] = o[ROWS:]
        odq[1, b0] = dq[:ROWS]
        odq[1, b1] = dq[ROWS:]
        gt[0:HD, pl.ds(pl.multiple_of(b0 * ROWS, ROWS), ROWS)] = dqtb[:, :ROWS]
        gt[0:HD, pl.ds(pl.multiple_of(b1 * ROWS, ROWS), ROWS)] = dqtb[:, ROWS:]
        odq_copy(b0).start()

        @pl.when(t < 3)
        def _():
            odq_copy(b1).start()

        return carry

    lax.fori_loop(0, 4, tile, 0)
    res[0, :, pl.ds(col, HD)] = odq[0, c]
    res[1, :, pl.ds(col, HD)] = odq[1, c]

    pr_copy = rcopy(dkv.at[1 - k], pr, prs.at[0], prr.at[0], mate)
    pr_copy.start()
    pr_copy.wait_recv()

    def dkv_copy(b):
        return rcopy(
            gsrc.at[:, b], res.at[2:4, :, pl.ds(col, HD)], ks.at[b], kr.at[c], same(b)
        )

    def give_back(i, carry):
        b = (c + 1 + i) % CHIPS
        rows = pl.ds(pl.multiple_of(b * ROWS, ROWS), ROWS)
        both = dkv[k, rows, :] + pr[rows, :]
        dk = both[:, :HD] * TEMPER
        dv = both[:, HD:]
        gsrc[0, b] = dk.astype(BF)
        gsrc[1, b] = dv.astype(BF)

        @pl.when(i < CHIPS - 1)
        def _():
            dkv_copy(b).start()

        gt[HD : 2 * HD, rows] = dk.T.astype(BF)
        gt[2 * HD :, rows] = dv.T.astype(BF)
        return carry

    lax.fori_loop(0, CHIPS, give_back, 0)
    res[2, :, pl.ds(col, HD)] = gsrc[0, c]
    res[3, :, pl.ds(col, HD)] = gsrc[1, c]

    gtf[...] = dot(gt[...], nh[...].reshape(CHIPS * ROWS, CH))
    for p in range(3):
        rows = pl.ds(pl.multiple_of(p * HD + (1 - k) * 64, 64), 64)
        gst[p] = gtf[rows, :].astype(BF).reshape(4, 16, CH)
    gp_copy = rcopy(gst, grcv, gps.at[0], gpr.at[0], mate)
    gp_copy.start()

    for r in range(1, CHIPS):
        b = (c + r) % CHIPS
        lanes = pl.ds(pl.multiple_of(b * HD, HD), HD)
        rcopy(odq.at[:, b], res.at[0:2, :, lanes], os_.at[b], or_.at[b], same(b)).wait_recv()
        rcopy(gsrc.at[:, b], res.at[2:4, :, lanes], ks.at[b], kr.at[b], same(b)).wait_recv()
    att_ref[...] = res[0]
    wf_copy.wait()
    inner = HEADS * HD
    gn = dot_nt(res[1], wfull[:, :inner])
    gn = gn + dot_nt(res[2], wfull[:, inner : 2 * inner])
    gn = gn + dot_nt(res[3], wfull[:, 2 * inner :])
    scaled = gn * gain_ref[...]
    nrm = normed_s[...]
    gh = inv_s[:, 0:1] * (scaled - nrm * jnp.mean(scaled * nrm, -1, keepdims=True))
    normed_s[...] = gh
    bext[HALO : HALO + ROWS, :] = gh.astype(BF)
    b_start, b_recv, b_send = halo(bext, h2s, h2r)
    b_start()

    gp_copy.wait_recv()
    for p in range(3):
        rows = pl.ds(pl.multiple_of(p * HD + k * 64, 64), 64)
        gown[p] = (gtf[rows, :].reshape(4, 16, CH) + grcv[p].astype(F32)).astype(BF)
        unit = SEQ * p + j
        owner = unit // 3
        slot = unit % 3

        @pl.when(owner == j)
        def _():
            gq[pl.ds(slot * 4, 4)] = gown[p]

        @pl.when(owner != j)
        def _():
            rcopy(gown.at[p], gq.at[pl.ds(slot * 4, 4)], gus.at[p], gur.at[slot], {"seq": owner}).start()

    b_recv()
    wide = bext[...].astype(F32)
    for b in range(CHIPS):
        turned = wide if b == 0 else pltpu.roll(wide, CH - 96 * b, 1)
        bst[b] = turned[:, :HD].astype(BF)

    def b_copy(r):
        b = (c + r) % CHIPS
        return rcopy(bst.at[b], bh.at[c], bs.at[b], br.at[c], same(b))

    for r in range(1, CHIPS):
        b_copy(r).start()
    bh[c] = bst[c]

    ga = dot_nt(bext[(TAPS - 1) * GAP : (TAPS - 1) * GAP + ROWS, :], cwv[0])
    for t in range(1, TAPS):
        lo = (TAPS - 1 - t) * GAP
        ga = ga + dot_nt(bext[lo : lo + ROWS, :], cwv[t])
    x = x_ref[...].astype(F32)
    th = jnp.tanh(GELU_A * (x + GELU_B * x * x * x))
    slope = 0.5 * (1.0 + th) + 0.5 * x * (1.0 - th * th) * GELU_A * (1.0 + 3.0 * GELU_B * x * x)
    gi_ref[...] = (normed_s[...] + slope * ga).astype(BF)

    for slot in range(3):
        @pl.when((3 * j + slot) % SEQ != j)
        def _():
            rcopy(gown.at[0], gq.at[pl.ds(slot * 4, 4)], gus.at[0], gur.at[slot], mate).wait_recv()

    def rq_copy(i):
        to = (d + i) % DP
        return rcopy(gq.at[jnp.minimum(15 - to, 11)], rq.at[d], rqs.at[to], rqr.at[d], {"dp": to}), to

    def rq_send(i, carry):
        cp, to = rq_copy(i)
        pl.when(to >= 4)(cp.start)
        return carry

    lax.fori_loop(1, DP, rq_send, 0)

    for r in range(1, CHIPS):
        b = (c + r) % CHIPS
        rcopy(ah.at[b], ah.at[b], ahs.at[b], ahr.at[b], same(b)).wait_recv()
        rcopy(bh.at[b], bh.at[b], bs.at[b], br.at[b], same(b)).wait_recv()
    for t in range(TAPS):
        lo = (TAPS - 1 - t) * GAP
        win = bh[:, lo : lo + ROWS, :].reshape(CHIPS * ROWS, HD)
        bt[t * 96 : (t + 1) * 96, :] = flip(win)[:96].astype(BF)
    cg[...] = dot(bt[...], ah[...].reshape(CHIPS * ROWS, CH))
    for t in range(TAPS):
        rows = pl.ds(pl.multiple_of(t * 96 + (1 - k) * 48, 48), 48)
        cst[t * 3 : t * 3 + 3] = cg[rows, :].astype(BF).reshape(3, 16, CH)
    cp_copy = rcopy(cst, crcv, cps.at[0], cpr.at[0], mate)
    cp_copy.start()

    def take(buf, ss, rs):
        def step(i, carry):
            frm = (d + i) % DP
            rcopy(buf.at[frm], buf.at[frm], ss.at[frm], rs.at[frm], {"dp": frm}).wait_recv()
            return carry

        lax.fori_loop(1, DP, step, 0)
        total = buf[0].astype(F32)
        for i in range(1, DP):
            total = total + buf[i].astype(F32)
        return total.astype(BF)

    def spread(buf, mine, ss, rs):
        def step(i, carry):
            to = (d + i) % DP
            rcopy(buf.at[mine], buf.at[mine], ss.at[to], rs.at[mine], {"dp": to}).start()
            return carry

        lax.fori_loop(1, DP, step, 0)

    @pl.when(d >= 4)
    def _():
        rq[d] = gq[15 - d]
        gfin[15 - d] = take(rq, rqs, rqr)
        spread(gfin, 15 - d, fqs, fqr)

    cp_copy.wait_recv()
    for t in range(TAPS):
        rows = pl.ds(pl.multiple_of(t * 96 + k * 48, 48), 48)
        own = cg[rows, :].reshape(3, 16, CH)
        ct[t * 3 : t * 3 + 3] = (own + crcv[t * 3 : t * 3 + 3].astype(F32)).astype(BF)

    def rc_copy(i):
        to = (d + i) % DP
        return rcopy(ct.at[jnp.minimum(to, 14)], rc.at[d], rcs.at[to], rcr.at[d], {"dp": to}), to

    def rc_send(i, carry):
        cp, to = rc_copy(i)
        pl.when(to < 15)(cp.start)
        return carry

    lax.fori_loop(1, DP, rc_send, 0)

    @pl.when(d < 15)
    def _():
        rc[d] = ct[d]
        cfin[d] = take(rc, rcs, rcr)
        spread(cfin, d, fcs, fcr)

    def land(i, carry):
        frm = (d + i) % DP

        @pl.when(frm >= 4)
        def _():
            m = 15 - frm
            rcopy(gfin.at[m], gfin.at[m], fqs.at[frm], fqr.at[m], {"dp": frm}).wait_recv()

        return carry

    lax.fori_loop(1, DP, land, 0)
    gq_out[...] = gfin[...].astype(F32).reshape(192, CH)

    def land_c(i, carry):
        frm = (d + i) % DP

        @pl.when(frm < 15)
        def _():
            rcopy(cfin.at[frm], cfin.at[frm], fcs.at[frm], fcr.at[frm], {"dp": frm}).wait_recv()

        return carry

    lax.fori_loop(1, DP, land_c, 0)
    ct_out[...] = cfin[...].astype(F32).reshape(240, CH)

    h_send()
    b_send()
    pr_copy.wait_send()
    gp_copy.wait_send()
    cp_copy.wait_send()
    for r in range(1, CHIPS):
        do_copy(r).wait_send()
        nh_copy(r).wait_send()
        ah_copy(r).wait_send()
        b_copy(r).wait_send()
        b = (c + r) % CHIPS
        odq_copy(b).wait_send()
        dkv_copy(b).wait_send()
    for b in range(CHIPS):
        kv_copy(b).wait_send()
    for p in range(3):
        unit = SEQ * p + j

        @pl.when(unit // 3 != j)
        def _():
            rcopy(gown.at[p], gq.at[pl.ds(0, 4)], gus.at[p], gur.at[0], {"seq": unit // 3}).wait_send()

    def drain(i, carry):
        cp, to = rq_copy(i)
        pl.when(to >= 4)(cp.wait_send)
        cp, to = rc_copy(i)
        pl.when(to < 15)(cp.wait_send)

        @pl.when(d >= 4)
        def _():
            rcopy(gfin.at[0], gfin.at[0], fqs.at[to], fqr.at[0], {"dp": to}).wait_send()

        @pl.when(d < 15)
        def _():
            rcopy(cfin.at[0], cfin.at[0], fcs.at[to], fcr.at[0], {"dp": to}).wait_send()

        return carry

    lax.fori_loop(1, DP, drain, 0)


def body(inputs, convolution_weight, w_qkv, gain, out_grad):
    vm = pl.BlockSpec(memory_space=pltpu.VMEM)
    hbm = pl.BlockSpec(memory_space=pl.ANY)
    V = pltpu.VMEM

    def sem(n):
        return pltpu.SemaphoreType.DMA((n,))

    half = CHIPS * ROWS
    scratch = [
        V((TAPS, CH, CH), BF),
        V((CH, 3 * HEADS * HD), BF),
        V((CH, 3 * HD), BF),
        V((ROWS + 2 * HALO, CH), BF),
        V((ROWS, CH), F32),
        V((ROWS, HD), F32),
        V((CHIPS, ROWS, CH), BF),
        V((CHIPS, ROWS, HD), BF),
        V((CHIPS, ROWS, HD), BF),
        V((2, CHIPS, ROWS, 2 * HD), BF),
        V((2, HD, 2 * half), BF),
        V((2 * half, TILE), F32),
        V((2, half, 2 * HD), F32),
        V((half, 2 * HD), F32),
        V((2, CHIPS, ROWS, HD), BF),
        V((2, CHIPS, ROWS, HD), BF),
        V((3 * HD, half), BF),
        V((4, ROWS, HEADS * HD), BF),
        V((CHIPS, ROWS, CH), BF),
        V((3 * HD, CH), F32),
        V((3, 4, 16, CH), BF),
        V((3, 4, 16, CH), BF),
        V((3, 4, 16, CH), BF),
        V((12, 16, CH), BF),
        V((ROWS + 2 * HALO, CH), BF),
        V((CHIPS, ROWS + 2 * HALO, HD), BF),
        V((CHIPS, ROWS + 2 * HALO, HD), BF),
        V((TAPS * 96, half), BF),
        V((TAPS * 96, CH), F32),
        V((15, 16, CH), BF),
        V((15, 16, CH), BF),
        V((15, 16, CH), BF),
        V((DP, 16, CH), BF),
        V((DP, 16, CH), BF),
        V((15, 16, CH), BF),
        V((12, 16, CH), BF),
        sem(9),
        sem(2), sem(2), sem(8), sem(8), sem(8), sem(8), sem(8), sem(8), sem(8), sem(8),
        sem(8), sem(8), sem(8), sem(8), sem(1), sem(1),
        sem(1), sem(1), sem(3), sem(3), sem(2), sem(2), sem(8), sem(8), sem(1), sem(1),
        sem(16), sem(16), sem(16), sem(16), sem(16), sem(16), sem(16), sem(16),
    ]
    att, gi, ct, gq = pl.pallas_call(
        kernel,
        out_shape=[
            jax.ShapeDtypeStruct((ROWS, HEADS * HD), BF),
            jax.ShapeDtypeStruct((ROWS, CH), BF),
            jax.ShapeDtypeStruct((240, CH), F32),
            jax.ShapeDtypeStruct((192, CH), F32),
        ],
        in_specs=[vm, vm, vm, hbm, hbm],
        out_specs=[vm, vm, vm, vm],
        scratch_shapes=scratch,
        compiler_params=pltpu.CompilerParams(
            collective_id=0, has_side_effects=True, vmem_limit_bytes=56 * 1024 * 1024
        ),
        cost_estimate=pl.CostEstimate(flops=8_000_000_000, bytes_accessed=15_000_000, transcendentals=2_200_000),
    )(inputs[0], gain[None, :], out_grad[0], convolution_weight, w_qkv)
    conv = ct.reshape(TAPS, 48, CH).transpose(0, 2, 1)
    return att[None], gi[None], conv, gq.T


def solution(mesh):
    in_specs = (P("dp", "seq", None), P(), P(), P(), P("dp", "seq", None))
    out_specs = (P("dp", "seq", None), P("dp", "seq", None), P(None, None, "seq"), P(None, "seq"))
    return jax.shard_map(body, mesh=mesh, in_specs=in_specs, out_specs=out_specs, check_vma=False)
```

```python
import jax
import jax.numpy as jnp
from jax import lax
from jax.experimental import pallas as pl
from jax.experimental.pallas import tpu as pltpu
from jax.sharding import PartitionSpec as P

CH = 768
HEADS = 8
HD = 128
INNER = HEADS * HD
TAPS = 5
GAP = 16
HALO = 32
ROWS = 128
SEQ = 16
DP = 16
CHIPS = 8
HALF = CHIPS * ROWS
TILE = 256
TILES = HALF // TILE
PART = 384
GROUPS = 3
WIDE = CH // GROUPS
TEMPER = HD ** (-0.5)
LOG2E = 1.4426950408889634
GELU_A = 0.7978845608028654
GELU_B = 0.044715
BF = jnp.bfloat16
F32 = jnp.float32
MESH = pl.DeviceIdType.MESH


def rcopy(src, dst, ss, rs, dev):
    return pltpu.make_async_remote_copy(
        src_ref=src, dst_ref=dst, send_sem=ss, recv_sem=rs, device_id=dev, device_id_type=MESH
    )


def dot(a, b):
    return jnp.dot(a, b, preferred_element_type=F32)


def dot_nt(a, b):
    return lax.dot_general(a, b, (((1,), (1,)), ((), ())), preferred_element_type=F32)


def flip(a):
    return a.astype(F32).T


def gelu_tanh(x):
    return jnp.tanh(GELU_A * (x + GELU_B * x * x * x))


def gelu(x):
    x = x.astype(F32)
    return (0.5 * x * (1.0 + gelu_tanh(x))).astype(BF)


def loop(n, step):
    lax.fori_loop(0, n, lambda i, carry: (step(i), carry)[1], 0)


def kernel(
    x_ref, gain_ref, og_ref, cw_hbm, w_hbm,
    att_ref, gi_ref, cfin, gfin,
    cwv, wfull, wh, xg, xhb, ag, acc_s, hbuf, hid_s, nh, doh, dot_s, qd, qt_s, kv, kt_s, vt_s,
    wts, stat_s, dor_s, dqt, dkvp, pr, obuf, dqb, gsrc, gt, res, gtf, gst, grcv, gown,
    rq, red, bext, bst, bh, bt, cg, cst, crcv, ct, rc,
    wsem, xs, xr, xhs, xhr, dos, dor, hds, hdr, kvs, kvr, os_, or_, dqs, dqr, ks, kr, prs, prr,
    gps, gpr, rqs, rqr, gus, gur, h2s, h2r, bs, br, cps, cpr, rcs, rcr, fcs, fcr,
):
    j = lax.axis_index("seq")
    d = lax.axis_index("dp")
    c = j // 2
    k = j % 2
    mate = {"seq": j + 1 - 2 * k}
    home = j // CHIPS
    slot = j % CHIPS
    col = pl.multiple_of(c * HD, HD)

    for t in range(TAPS):
        pltpu.make_async_copy(cw_hbm.at[t], cwv.at[t], wsem.at[t]).start()
    for p in range(3):
        pltpu.make_async_copy(
            w_hbm.at[:, pl.ds(p * INNER + col, HD)], wh.at[:, pl.ds(p * HD, HD)], wsem.at[5 + p]
        ).start()
    wf_copy = pltpu.make_async_copy(w_hbm, wfull, wsem.at[8])
    wf_copy.start()

    barrier = pltpu.get_barrier_semaphore()

    def hello(i):
        pl.semaphore_signal(barrier, inc=1, device_id={"seq": (j + i + 1) % SEQ}, device_id_type=MESH)
        pl.semaphore_signal(barrier, inc=1, device_id={"dp": (d + i + 1) % DP}, device_id_type=MESH)

    loop(15, hello)
    dqt[...] = jnp.zeros_like(dqt)
    pl.semaphore_wait(barrier, 30)

    def to_worker(copy, local):
        def step(i):
            chip = (c + CHIPS - 1 - i) % CHIPS
            dev = 2 * chip + home

            @pl.when(dev != j)
            def _():
                copy(chip, {"seq": dev}).start()

            if local is not None:
                pl.when(dev == j)(lambda: local(chip))

        loop(CHIPS, step)

    def to_worker_done(copy):
        def step(chip):
            dev = 2 * chip + home

            @pl.when(dev != j)
            def _():
                copy(chip, {"seq": dev}).wait_send()

        loop(CHIPS, step)

    def owner_of(b):
        return CHIPS * k + b

    def xh_copy(chip):
        start = pl.multiple_of(96 * (8 - j), HALO)
        return rcopy(
            x_ref.at[pl.ds(start, HALO)], xhb, xhs.at[chip], xhr.at[0], {"seq": 2 * chip + 8 - j}
        )

    @pl.when((j == 7) | (j == 8))
    def _():
        def step(i):
            chip = (c + CHIPS - 1 - i) % CHIPS

            @pl.when(chip != c)
            def _():
                xh_copy(chip).start()

        loop(CHIPS, step)

    pl.when(j == 7)(lambda: xhb.__setitem__(Ellipsis, x_ref[ROWS - HALO :, :]))
    pl.when(j == 8)(lambda: xhb.__setitem__(Ellipsis, x_ref[:HALO, :]))

    def x_copy(g):
        def copy(chip, dev):
            src = x_ref.at[:, g * WIDE : (g + 1) * WIDE]
            return rcopy(src, xg.at[g, slot], xs.at[g, chip], xr.at[g, slot], dev)

        return copy

    for g in range(GROUPS):
        def x_local(chip, g=g):
            xg[g, slot] = x_ref[:, g * WIDE : (g + 1) * WIDE]

        to_worker(x_copy(g), x_local)

    def do_copy(chip, dev):
        src = og_ref.at[:, pl.ds(pl.multiple_of(chip * HD, HD), HD)]
        return rcopy(src, doh.at[slot], dos.at[chip], dor.at[slot], dev)

    def do_local(chip):
        doh[slot] = og_ref[:, pl.ds(pl.multiple_of(chip * HD, HD), HD)]

    to_worker(do_copy, do_local)

    def wait_slot(buf, ss, rs, b):
        @pl.when(owner_of(b) != j)
        def _():
            rcopy(buf.at[b], buf.at[b], ss.at[0], rs.at[b], mate).wait_recv()

    def kv_copy(p):
        return rcopy(kv.at[k, p], kv.at[k, p], kvs.at[p], kvr.at[p], mate)

    def finish_rows(p, acc):
        inv = lax.rsqrt(jnp.mean(acc * acc, -1, keepdims=True) + 1e-6)

        @pl.when((k == c // 4) & (p == c % 4))
        def _():
            hbuf[...] = acc.reshape(2, ROWS, CH)

        rows_bf = (acc * inv * gain_ref[...]).astype(BF)
        nh[p] = rows_bf
        outb = dot(rows_bf, wh[...]).astype(BF)
        kv[k, p] = outb[:, HD:]
        kv_copy(p).start()
        qd[pl.ds(pl.multiple_of(p * TILE, TILE), TILE), :] = outb[:, :HD]
        outf = outb.astype(F32)
        qt_s[p] = outf[:, :HD].T.astype(BF)
        kt_s[k * TILES + p] = outf[:, HD : 2 * HD].T.astype(BF)
        vt_s[k * TILES + p] = outf[:, 2 * HD :].T.astype(BF)

    @pl.when((j != 7) & (j != 8))
    def _():
        rcopy(xhb, xhb, xhs.at[0], xhr.at[0], mate).wait_recv()

    edge = gelu(xhb[...])
    ag[0:HALO, :] = jnp.where(k == 1, edge, jnp.zeros_like(edge))
    ag[HALO + HALF :, :] = jnp.where(k == 0, edge, jnp.zeros_like(edge))
    for t in range(TAPS):
        pltpu.make_async_copy(cw_hbm.at[t], cwv.at[t], wsem.at[t]).wait()
    for p in range(3):
        pltpu.make_async_copy(
            w_hbm.at[:, pl.ds(p * INNER + col, HD)], wh.at[:, pl.ds(p * HD, HD)], wsem.at[5 + p]
        ).wait()
    for g in range(GROUPS):
        lanes = slice(g * WIDE, (g + 1) * WIDE)

        def arrive(p, g=g, lanes=lanes):
            for e in range(2):
                wait_slot(xg.at[g], xs.at[g], xr.at[g], 2 * p + e)
            block = xg[g, pl.ds(2 * p, 2)].reshape(TILE, WIDE)
            ag[pl.ds(pl.multiple_of(HALO + p * TILE, HALO), TILE), lanes] = gelu(block)
            if g == 0:
                acc_s[p] = jnp.zeros((TILE, CH), F32)
            acc_s[p, :, lanes] = acc_s[p, :, lanes] + block.astype(F32)

        loop(TILES, arrive)

        def convolve(p, g=g, lanes=lanes):
            part = None
            for t in range(TAPS):
                rows = pl.ds(pl.multiple_of(p * TILE + t * GAP, GAP), TILE)
                one = dot(ag[rows, lanes], cwv[t, lanes, :])
                part = one if part is None else part + one
            if g < GROUPS - 1:
                acc_s[p] = acc_s[p] + part
            else:
                finish_rows(p, acc_s[p] + part)

        loop(TILES, convolve)

    hd_copy = rcopy(hbuf.at[1 - k], hid_s, hds.at[0], hdr.at[0], mate)

    @pl.when(k == c // 4)
    def _():
        hd_copy.start()
        hid_s[...] = hbuf[k]

    def cotangents(t):
        for e in range(2):
            wait_slot(doh, dos, dor, 2 * t + e)
        dot_s[t] = flip(doh[pl.ds(2 * t, 2)].reshape(TILE, HD)).astype(BF)

    loop(TILES, cotangents)

    def other_keys(p):
        rcopy(kv.at[1 - k, p], kv.at[1 - k, p], kvs.at[p], kvr.at[p], mate).wait_recv()
        both = kv[1 - k, p].astype(F32)
        kt_s[(1 - k) * TILES + p] = both[:, :HD].T.astype(BF)
        vt_s[(1 - k) * TILES + p] = both[:, HD:].T.astype(BF)

    loop(TILES, other_keys)

    def give(copy, local, p):
        for e in range(2):
            b = 2 * p + e
            pl.when(owner_of(b) != j)(lambda b=b: copy(b).start())
            pl.when(owner_of(b) == j)(lambda b=b: local(b))

    def o_copy(b):
        return rcopy(
            obuf.at[b], att_ref.at[:, pl.ds(col, HD)], os_.at[b], or_.at[c], {"seq": owner_of(b)}
        )

    def o_local(b):
        att_ref[:, pl.ds(col, HD)] = obuf[b]

    def forward(t):
        qt = qt_s[t]
        top = None
        for i in range(2 * TILES):
            s = dot(kv[i // TILES, i % TILES, :, :HD], qt)
            part = jnp.max(s.reshape(TILE // 8, 8, TILE), axis=0)
            top = part if top is None else jnp.maximum(top, part)
        top = jnp.max(top, axis=0, keepdims=True) * (TEMPER * LOG2E)
        total = jnp.zeros((8, TILE), F32)
        ot = jnp.zeros((HD, TILE), F32)
        lanes = pl.ds(pl.multiple_of(t * TILE, TILE), TILE)
        for i in range(2 * TILES):
            s = dot(kv[i // TILES, i % TILES, :, :HD], qt)
            p = jnp.exp2(s * (TEMPER * LOG2E) - top)
            total = total + jnp.sum(p.reshape(TILE // 8, 8, TILE), axis=0)
            pb = p.astype(BF)
            wts[i, :, lanes] = pb
            ot = ot + dot(vt_s[i], pb)
        rec = 1.0 / jnp.sum(total, axis=0, keepdims=True)
        otb = (ot * rec).astype(BF).astype(F32)
        go = dot_s[t].astype(F32)
        dots = jnp.sum(go * otb, axis=0, keepdims=True)
        stat_s[0, :, lanes] = jnp.broadcast_to(rec, (8, TILE))
        stat_s[1, :, lanes] = jnp.broadcast_to(dots, (8, TILE))
        dor_s[lanes, :] = (go * rec).T.astype(BF)
        obuf[pl.ds(2 * t, 2)] = otb.T.astype(BF).reshape(2, ROWS, HD)
        give(o_copy, o_local, t)

    loop(TILES, forward)

    def backward(h, m):
        g = h * TILES + m
        vc = kv[h, m, :, HD:]
        w = wts[g]
        parts = []
        for t in range(TILES):
            lanes = slice(t * TILE, (t + 1) * TILE)
            gw = dot(vc, dot_s[t])
            slope = (gw - stat_s[1, 0:1, lanes]) * stat_s[0, 0:1, lanes]
            parts.append((w[:, lanes].astype(F32) * slope).astype(BF))
        ds = jnp.concatenate(parts, axis=1)
        dv = dot(w, dor_s[...])
        dk = dot(ds, qd[...])
        dqt[...] = dqt[...] + dot(kt_s[g], ds)
        return dk * TEMPER, dv

    def pr_copy(m):
        return rcopy(dkvp.at[m], pr.at[m], prs.at[m], prr.at[m], mate)

    def other_half(m):
        dk, dv = backward(1 - k, m)
        dkvp[m, 0] = dk
        dkvp[m, 1] = dv
        pr_copy(m).start()

    loop(TILES, other_half)

    def kv_back(b):
        return rcopy(
            gsrc.at[:, b], res.at[1:3, :, pl.ds(col, HD)], ks.at[b], kr.at[c], {"seq": owner_of(b)}
        )

    def kv_local(b):
        res[1, :, pl.ds(col, HD)] = gsrc[0, b]
        res[2, :, pl.ds(col, HD)] = gsrc[1, b]

    def own_half(m):
        dk, dv = backward(k, m)
        pr_copy(m).wait_recv()
        dk = dk + pr[m, 0]
        dv = dv + pr[m, 1]
        gsrc[0, pl.ds(2 * m, 2)] = dk.astype(BF).reshape(2, ROWS, HD)
        gsrc[1, pl.ds(2 * m, 2)] = dv.astype(BF).reshape(2, ROWS, HD)
        give(kv_back, kv_local, m)
        gt[m, HD : 2 * HD, :] = dk.T.astype(BF)
        gt[m, 2 * HD :, :] = dv.T.astype(BF)

    loop(TILES, own_half)

    def dq_copy(b):
        return rcopy(
            dqb.at[b], res.at[0, :, pl.ds(col, HD)], dqs.at[b], dqr.at[c], {"seq": owner_of(b)}
        )

    def dq_local(b):
        res[0, :, pl.ds(col, HD)] = dqb[b]

    def query_back(t):
        dq = dqt[:, pl.ds(pl.multiple_of(t * TILE, TILE), TILE)] * TEMPER
        dqb[pl.ds(2 * t, 2)] = dq.T.astype(BF).reshape(2, ROWS, HD)
        give(dq_copy, dq_local, t)
        gt[t, :HD, :] = dq.astype(BF)

    loop(TILES, query_back)

    for t in range(TILES):
        part = dot(gt[t], nh[t])
        gtf[...] = part if t == 0 else gtf[...] + part
    for p in range(3):
        rows = pl.ds(pl.multiple_of(p * HD + (1 - k) * 64, 64), 64)
        gst[p * 4 : p * 4 + 4] = gtf[rows, :].astype(BF).reshape(4, 16, CH)
    gp_copy = rcopy(gst, grcv, gps.at[0], gpr.at[0], mate)
    gp_copy.start()
    gp_copy.wait_recv()
    for p in range(3):
        rows = pl.ds(pl.multiple_of(p * HD + k * 64, 64), 64)
        own = gtf[rows, :].reshape(4, 16, CH)
        gown[p * 4 : p * 4 + 4] = (own + grcv[p * 4 : p * 4 + 4].astype(F32)).astype(BF)

    def rq_copy(to):
        return rcopy(gown.at[jnp.minimum(15 - to, 11)], rq.at[d], rqs.at[to], rqr.at[d], {"dp": to})

    def rq_send(i):
        to = (d + 1 + i) % DP
        pl.when(to >= 4)(lambda: rq_copy(to).start())

    loop(15, rq_send)

    @pl.when(k != c // 4)
    def _():
        hd_copy.wait_recv()

    def back(copy):
        def step(i):
            chip = (c + i) % CHIPS
            lanes = pl.ds(pl.multiple_of(chip * HD, HD), HD)
            pl.when(2 * chip + home != j)(lambda: copy(chip, lanes).wait_recv())

        loop(CHIPS, step)

    wf_copy.wait()
    back(lambda chip, lanes: rcopy(gsrc.at[:, 0], res.at[1:3, :, lanes], ks.at[0], kr.at[chip], mate))
    gn = dot_nt(res[1], wfull[:, INNER : 2 * INNER])
    gn = gn + dot_nt(res[2], wfull[:, 2 * INNER :])
    back(lambda chip, lanes: rcopy(dqb.at[0], res.at[0, :, lanes], dqs.at[0], dqr.at[chip], mate))
    gn = gn + dot_nt(res[0], wfull[:, :INNER])
    hidden = hid_s[...]
    inv = lax.rsqrt(jnp.mean(hidden * hidden, -1, keepdims=True) + 1e-6)
    normed = hidden * inv
    scaled = gn * gain_ref[...]
    gh = inv * (scaled - normed * jnp.mean(scaled * normed, -1, keepdims=True))
    hid_s[...] = gh
    ghb = gh.astype(BF)
    bext[HALO : HALO + ROWS, :] = ghb

    wide = ghb.astype(F32)
    for b in range(CHIPS):
        turned = wide if b == 0 else pltpu.roll(wide, CH - 96 * b, 1)
        bst[b] = turned[:, :HD].astype(BF)

    def b_copy(chip, dev):
        return rcopy(bst.at[chip], bh.at[slot], bs.at[chip], br.at[slot], dev)

    def b_local(chip):
        bh[slot] = bst[chip]

    to_worker(b_copy, b_local)

    up = rcopy(bext.at[ROWS : ROWS + HALO], bext.at[0:HALO], h2s.at[0], h2r.at[0], {"seq": (j + 1) % SEQ})
    down = rcopy(
        bext.at[HALO : 2 * HALO], bext.at[HALO + ROWS :], h2s.at[1], h2r.at[1], {"seq": (j + SEQ - 1) % SEQ}
    )
    pl.when(j < SEQ - 1)(lambda: up.start())
    pl.when(j > 0)(lambda: down.start())

    @pl.when(j == 0)
    def _():
        bext[0:HALO, :] = jnp.zeros((HALO, CH), BF)

    @pl.when(j == SEQ - 1)
    def _():
        bext[HALO + ROWS :, :] = jnp.zeros((HALO, CH), BF)

    def take(buf, ss, rs):
        def step(i):
            frm = (d + 1 + i) % DP
            rcopy(buf.at[frm], buf.at[frm], ss.at[frm], rs.at[frm], {"dp": frm}).wait_recv()

        loop(15, step)
        total = buf[0].astype(F32)
        for i in range(1, DP):
            total = total + buf[i].astype(F32)
        return total.astype(BF)

    mine = jnp.maximum(15 - d, 0)
    unit = SEQ * (mine // 4) + j
    owner = unit // 3
    row = (unit % 3) * 4 + mine % 4

    def red_copy(i):
        to = (d + i) % DP
        return rcopy(red, gfin.at[row], gus.at[to], gur.at[row], {"dp": to, "seq": owner})

    @pl.when(d >= 4)
    def _():
        rq[d] = gown[15 - d]
        red[...] = take(rq, rqs, rqr)
        loop(15, lambda i: red_copy(i + 1).start())
        pl.when(owner != j)(lambda: red_copy(0).start())

        @pl.when(owner == j)
        def _():
            gfin[row] = red[...]

    def b_wait(b):
        wait_slot(bh, bs, br, b)

    loop(CHIPS, b_wait)
    bt[...] = flip(bh[...].reshape(HALF, HD))[:96].astype(BF)

    def cp_copy(n):
        return rcopy(cst.at[n], crcv.at[n], cps.at[n], cpr.at[n], mate)

    for n in range(2):
        for t in range(TAPS):
            rows = slice(t * GAP, t * GAP + HALF)
            cg[n, t * 96 : t * 96 + 96, :] = dot(bt[...], ag[rows, n * PART : (n + 1) * PART])
        for t in range(TAPS):
            rows = pl.ds(pl.multiple_of(t * 96 + (1 - k) * 48, 48), 48)
            cst[n, t * 3 : t * 3 + 3] = cg[n, rows, :].astype(BF).reshape(3, 16, PART)
        cp_copy(n).start()

    def rc_copy(n, to):
        return rcopy(
            ct.at[n, jnp.minimum(to, 14)], rc.at[n, d], rcs.at[n, to], rcr.at[n, d], {"dp": to}
        )

    for n in range(2):
        cp_copy(n).wait_recv()
        for t in range(TAPS):
            rows = pl.ds(pl.multiple_of(t * 96 + k * 48, 48), 48)
            own = cg[n, rows, :].reshape(3, 16, PART)
            ct[n, t * 3 : t * 3 + 3] = (own + crcv[n, t * 3 : t * 3 + 3].astype(F32)).astype(BF)

        def rc_send(i, n=n):
            to = (d + 1 + i) % DP
            pl.when(to < 15)(lambda: rc_copy(n, to).start())

        loop(15, rc_send)

    pl.when(j > 0)(lambda: up.wait_recv())
    pl.when(j < SEQ - 1)(lambda: down.wait_recv())
    ga = jnp.zeros((ROWS, CH), F32)
    for t in range(TAPS):
        lo = (TAPS - 1 - t) * GAP
        ga = ga + dot_nt(bext[lo : lo + ROWS, :], cwv[t])
    x = x_ref[...].astype(F32)
    th = gelu_tanh(x)
    slope = 0.5 * (1.0 + th) + 0.5 * x * (1.0 - th * th) * GELU_A * (1.0 + 3.0 * GELU_B * x * x)
    gi_ref[...] = (hid_s[...] + slope * ga).astype(BF)

    def fc_copy(n, m, to):
        return rcopy(cfin.at[n, m], cfin.at[n, m], fcs.at[n, to], fcr.at[n, m], {"dp": to})

    @pl.when(d < 15)
    def _():
        for n in range(2):
            rc[n, d] = ct[n, d]
            cfin[n, d] = take(rc.at[n], rcs.at[n], rcr.at[n])
            loop(15, lambda i, n=n: fc_copy(n, d, (d + 1 + i) % DP).start())

    def o_wait(chip):
        @pl.when(2 * chip + home != j)
        def _():
            lanes = pl.ds(pl.multiple_of(chip * HD, HD), HD)
            rcopy(obuf.at[0], att_ref.at[:, lanes], os_.at[0], or_.at[chip], mate).wait_recv()

    loop(CHIPS, o_wait)

    for r in range(3):
        u = 3 * j + r
        for q in range(4):
            frm = u % SEQ
            at = 15 - (4 * (u // SEQ) + q)

            @pl.when((frm != j) | (at != d))
            def _(row=r * 4 + q):
                rcopy(red, gfin.at[row], gus.at[0], gur.at[row], mate).wait_recv()

    for n in range(2):
        def land_c(i, n=n):
            frm = (d + 1 + i) % DP
            pl.when(frm < 15)(lambda: fc_copy(n, frm, frm).wait_recv())

        loop(15, land_c)

    for g in range(GROUPS):
        to_worker_done(x_copy(g))
    to_worker_done(do_copy)
    to_worker_done(b_copy)

    @pl.when((j == 7) | (j == 8))
    def _():
        def step(chip):
            pl.when(chip != c)(lambda: xh_copy(chip).wait_send())

        loop(CHIPS, step)

    pl.when(k == c // 4)(lambda: hd_copy.wait_send())

    def mates(p):
        kv_copy(p).wait_send()
        pr_copy(p).wait_send()

    loop(TILES, mates)

    def given(b):
        @pl.when(owner_of(b) != j)
        def _():
            o_copy(b).wait_send()
            kv_back(b).wait_send()
            dq_copy(b).wait_send()

    loop(CHIPS, given)
    gp_copy.wait_send()

    @pl.when(d >= 4)
    def _():
        loop(15, lambda i: red_copy(i + 1).wait_send())
        pl.when(owner != j)(lambda: red_copy(0).wait_send())

    pl.when(j < SEQ - 1)(lambda: up.wait_send())
    pl.when(j > 0)(lambda: down.wait_send())
    for n in range(2):
        cp_copy(n).wait_send()

    def drain(i):
        to = (d + 1 + i) % DP
        pl.when(to >= 4)(lambda: rq_copy(to).wait_send())
        for n in range(2):
            pl.when(to < 15)(lambda n=n: rc_copy(n, to).wait_send())
            pl.when(d < 15)(lambda n=n: fc_copy(n, 0, to).wait_send())

    loop(15, drain)


def finish(att_ref, gi_ref, cfin, gfin, att_out, gi_out, cw_out, w_out, cbuf, gbuf, sem):
    copies = [pltpu.make_async_copy(att_ref, att_out, sem.at[0]), pltpu.make_async_copy(gi_ref, gi_out, sem.at[1])]
    for cp in copies:
        cp.start()
    gbuf[...] = gfin[...].astype(F32).reshape(192, CH).T
    copies.append(pltpu.make_async_copy(gbuf, w_out, sem.at[2]))
    copies[-1].start()
    for t in range(TAPS):
        for n in range(2):
            rows = cfin[n, t * 3 : t * 3 + 3].astype(F32).reshape(48, PART)
            cbuf[t, n * PART : (n + 1) * PART, :] = rows.T
    copies.append(pltpu.make_async_copy(cbuf, cw_out, sem.at[3]))
    copies[-1].start()
    for cp in copies:
        cp.wait()


def body(inputs, convolution_weight, w_qkv, gain, out_grad):
    vm = pl.BlockSpec(memory_space=pltpu.VMEM)
    hbm = pl.BlockSpec(memory_space=pl.ANY)
    V = pltpu.VMEM

    def sem(*n):
        return pltpu.SemaphoreType.DMA(n)

    scratch = [
        V((TAPS, CH, CH), BF),
        V((CH, 3 * INNER), BF),
        V((CH, 3 * HD), BF),
        V((GROUPS, CHIPS, ROWS, WIDE), BF),
        V((HALO, CH), BF),
        V((HALF + 2 * HALO, CH), BF),
        V((TILES, TILE, CH), F32),
        V((2, ROWS, CH), F32),
        V((ROWS, CH), F32),
        V((TILES, TILE, CH), BF),
        V((CHIPS, ROWS, HD), BF),
        V((TILES, HD, TILE), BF),
        V((HALF, HD), BF),
        V((TILES, HD, TILE), BF),
        V((2, TILES, TILE, 2 * HD), BF),
        V((2 * TILES, HD, TILE), BF),
        V((2 * TILES, HD, TILE), BF),
        V((2 * TILES, TILE, HALF), BF),
        V((2, 8, HALF), F32),
        V((HALF, HD), BF),
        V((HD, HALF), F32),
        V((TILES, 2, TILE, HD), F32),
        V((TILES, 2, TILE, HD), F32),
        V((CHIPS, ROWS, HD), BF),
        V((CHIPS, ROWS, HD), BF),
        V((2, CHIPS, ROWS, HD), BF),
        V((TILES, 3 * HD, TILE), BF),
        V((3, ROWS, INNER), BF),
        V((3 * HD, CH), F32),
        V((12, 16, CH), BF),
        V((12, 16, CH), BF),
        V((12, 16, CH), BF),
        V((DP, 16, CH), BF),
        V((16, CH), BF),
        V((ROWS + 2 * HALO, CH), BF),
        V((CHIPS, ROWS, HD), BF),
        V((CHIPS, ROWS, HD), BF),
        V((96, HALF), BF),
        V((2, TAPS * 96, PART), F32),
        V((2, 15, 16, PART), BF),
        V((2, 15, 16, PART), BF),
        V((2, 15, 16, PART), BF),
        V((2, DP, 16, PART), BF),
        sem(9),
        sem(3, 8), sem(3, 8), sem(8), sem(1), sem(8), sem(8), sem(1), sem(1),
        sem(4), sem(4), sem(8), sem(8), sem(8), sem(8), sem(8), sem(8), sem(4), sem(4),
        sem(1), sem(1), sem(16), sem(16), sem(16), sem(12),
        sem(2), sem(2), sem(8), sem(8), sem(2), sem(2),
        sem(2, 16), sem(2, 16), sem(2, 16), sem(2, 15),
    ]
    att, gi, cfin, gfin = pl.pallas_call(
        kernel,
        out_shape=[
            jax.ShapeDtypeStruct((ROWS, INNER), BF),
            jax.ShapeDtypeStruct((ROWS, CH), BF),
            jax.ShapeDtypeStruct((2, 15, 16, PART), BF),
            jax.ShapeDtypeStruct((12, 16, CH), BF),
        ],
        in_specs=[vm, vm, vm, hbm, hbm],
        out_specs=[vm, vm, vm, vm],
        scratch_shapes=scratch,
        compiler_params=pltpu.CompilerParams(
            collective_id=0, has_side_effects=True, vmem_limit_bytes=58 * 1024 * 1024
        ),
        cost_estimate=pl.CostEstimate(flops=14_000_000_000, bytes_accessed=15_000_000, transcendentals=3_000_000),
    )(inputs[0], gain.reshape(1, CH), out_grad[0], convolution_weight, w_qkv)
    att, gi, conv, qkv = pl.pallas_call(
        finish,
        out_shape=[
            jax.ShapeDtypeStruct((ROWS, INNER), BF),
            jax.ShapeDtypeStruct((ROWS, CH), BF),
            jax.ShapeDtypeStruct((TAPS, CH, 48), F32),
            jax.ShapeDtypeStruct((CH, 192), F32),
        ],
        in_specs=[vm, vm, vm, vm],
        out_specs=[hbm, hbm, hbm, hbm],
        scratch_shapes=[V((TAPS, CH, 48), F32), V((CH, 192), F32), sem(4)],
    )(att, gi, cfin, gfin)
    return att[None], gi[None], conv, qkv


def solution(mesh):
    in_specs = (P("dp", "seq", None), P(), P(), P(), P("dp", "seq", None))
    out_specs = (P("dp", "seq", None), P("dp", "seq", None), P(None, None, "seq"), P(None, "seq"))
    return jax.shard_map(body, mesh=mesh, in_specs=in_specs, out_specs=out_specs, check_vma=False)
```

```python
import jax
import jax.numpy as jnp
from jax import lax
from jax.experimental import pallas as pl
from jax.experimental.pallas import tpu as pltpu
from jax.sharding import PartitionSpec as P

CH = 768
HEADS = 8
HD = 128
INNER = HEADS * HD
TAPS = 5
GAP = 16
HALO = 32
PAD = 2 * HALO
ROWS = 128
SEQ = 16
DP = 16
ZS = 8
CHIPS = 8
HALF = CHIPS * ROWS
TILE = 256
TILES = HALF // TILE
PART = 384
GROUPS = 3
WIDE = CH // GROUPS
TEMPER = HD ** (-0.5)
LOG2E = 1.4426950408889634
GELU_A = 0.7978845608028654
GELU_B = 0.044715
BF = jnp.bfloat16
F32 = jnp.float32
MESH = pl.DeviceIdType.MESH


def rcopy(src, dst, ss, rs, dev):
    return pltpu.make_async_remote_copy(
        src_ref=src, dst_ref=dst, send_sem=ss, recv_sem=rs, device_id=dev, device_id_type=MESH
    )


def dot(a, b):
    return jnp.dot(a, b, preferred_element_type=F32)


def dot_nt(a, b):
    return lax.dot_general(a, b, (((1,), (1,)), ((), ())), preferred_element_type=F32)


def flip(a):
    return a.astype(F32).T


def gelu_tanh(x):
    return jnp.tanh(GELU_A * (x + GELU_B * x * x * x))


def gelu(x):
    x = x.astype(F32)
    return (0.5 * x * (1.0 + gelu_tanh(x))).astype(BF)


def loop(n, step):
    lax.fori_loop(0, n, lambda i, carry: (step(i), carry)[1], 0)


def kernel(
    x_hbm, gain_hbm, og_hbm, cw_hbm, w_hbm,
    att_ref, gi_ref, cfin, gfin,
    x_ref, gain_ref, og_ref, cwv, wfull, wh, xg, ag, apad, epad, acc_s, gn_s, hid_s, nh, doh, dot_s, qd, qt_s, kv, vt_s,
    wts, stat_s, ot_s, dor_s, dqt, dkvp, pr, obuf, dqb, gsrc, gt, res, gtf, gst, grcv, gown,
    rq, redp, redr, red, bext, bst, bh, bt, cg, cst, crcv, give_c, keep_c, px, zs, rc,
    wsem, xs, xr, xps, xhs, xhr, dos, dor, hds, hdr, kvs, kvr, os_, or_, dqs, dqr, ks, kr, prs, prr,
    gps, gpr, rqs, rqr, rps, rpr, gus, gur, h2s, h2r, bs, br, cps, cpr,
    pxs, pxr, rcs, rcr, fzs, fzr,
):
    j = lax.axis_index("seq")
    d = lax.axis_index("dp")
    c = j // 2
    k = j % 2
    mate = {"seq": j + 1 - 2 * k}
    home = j // CHIPS
    slot = j % CHIPS
    col = pl.multiple_of(c * HD, HD)

    barrier = pltpu.get_barrier_semaphore()

    def hello(i):
        pl.semaphore_signal(barrier, inc=1, device_id={"seq": (j + i + 1) % SEQ}, device_id_type=MESH)
        pl.semaphore_signal(barrier, inc=1, device_id={"dp": (d + i + 1) % DP}, device_id_type=MESH)

    loop(15, hello)
    x_in = pltpu.make_async_copy(x_hbm, x_ref, wsem.at[9])
    og_in = pltpu.make_async_copy(og_hbm, og_ref, wsem.at[10])
    gain_in = pltpu.make_async_copy(gain_hbm, gain_ref, wsem.at[11])
    x_in.start()
    og_in.start()
    gain_in.start()
    for t in range(TAPS):
        pltpu.make_async_copy(cw_hbm.at[t], cwv.at[t], wsem.at[t]).start()
    for p in range(3):
        pltpu.make_async_copy(
            w_hbm.at[:, pl.ds(p * INNER + col, HD)], wh.at[:, pl.ds(p * HD, HD)], wsem.at[5 + p]
        ).start()
    wf_copy = pltpu.make_async_copy(w_hbm, wfull, wsem.at[8])
    wf_copy.start()

    dqt[...] = jnp.zeros_like(dqt)
    acc_s[...] = jnp.zeros_like(acc_s)
    for p in range(TILES):
        apad[p, :PAD, :] = jnp.zeros((PAD, CH), BF)
        apad[p, PAD + TILE :, :] = jnp.zeros((PAD, CH), BF)
    epad[:PAD, :] = jnp.zeros((PAD, CH), BF)
    epad[PAD + HALO :, :] = jnp.zeros((PAD, CH), BF)

    @pl.when(k == 0)
    def _():
        ag[0:HALO, :] = jnp.zeros((HALO, CH), BF)

    @pl.when(k == 1)
    def _():
        ag[HALO + HALF :, :] = jnp.zeros((HALO, CH), BF)

    pl.semaphore_wait(barrier, 30)

    def to_worker(copy, local):
        def step(i):
            chip = (c + CHIPS - 1 - i) % CHIPS
            dev = 2 * chip + home

            @pl.when(dev != j)
            def _():
                copy(chip, {"seq": dev}).start()

            if local is not None:
                pl.when(dev == j)(lambda: local(chip))

        loop(CHIPS, step)

    def to_worker_done(copy):
        def step(chip):
            dev = 2 * chip + home

            @pl.when(dev != j)
            def _():
                copy(chip, {"seq": dev}).wait_send()

        loop(CHIPS, step)

    def owner_of(b):
        return CHIPS * k + b

    flip_x = c + 1 - 2 * (c % 2)
    near = (flip_x, (c + 2) % CHIPS, (c + 6) % CHIPS, (c + 4) % CHIPS, c)

    def x_copy(g, i):
        src = x_ref.at[:, g * WIDE : (g + 1) * WIDE]
        return rcopy(src, xg.at[g, slot], xs.at[g, i], xr.at[g, slot], {"seq": 2 * near[i] + home})

    def x_left(g):
        for i in range(4):
            x_copy(g, i).wait_send()

    def send_x(g):
        for i in range(4):
            x_copy(g, i).start()
        pl.when(home != k)(lambda: x_copy(g, 4).start())

        @pl.when(home == k)
        def _():
            xg[g, slot] = x_ref[:, g * WIDE : (g + 1) * WIDE]

    x_in.wait()
    send_x(0)
    x_left(0)
    send_x(1)

    inside = c // 4 == k
    passed = jnp.where(inside, flip_x, (c + 4) % CHIPS) - 4 * k

    def pass_copy(g, e, chip, i):
        b = 2 * passed + e
        return rcopy(xg.at[g, b], xg.at[g, b], xps.at[g, e, i], xr.at[g, b], {"seq": 2 * chip + k})

    def hand_on(g, e):
        b = 2 * passed + e
        rcopy(xg.at[g, b], xg.at[g, b], xps.at[g, e, 0], xr.at[g, b], mate).wait_recv()

        @pl.when(inside)
        def _():
            pass_copy(g, e, near[1], 0).start()
            pass_copy(g, e, near[2], 1).start()

        pl.when(c // 4 != k)(lambda: pass_copy(g, e, flip_x, 0).start())

    def relay(g):
        hand_on(g, 0)
        hand_on(g, 1)

    def wait_slot(buf, ss, rs, b):
        @pl.when(owner_of(b) != j)
        def _():
            rcopy(buf.at[b], buf.at[b], ss.at[0], rs.at[b], mate).wait_recv()

    def kv_copy(p):
        return rcopy(kv.at[k, p], kv.at[k, p], kvs.at[p], kvr.at[p], mate)

    def do_copy(chip, dev):
        src = og_ref.at[:, pl.ds(pl.multiple_of(chip * HD, HD), HD)]
        return rcopy(src, doh.at[slot], dos.at[chip], dor.at[slot], dev)

    def do_local(chip):
        doh[slot] = og_ref[:, pl.ds(pl.multiple_of(chip * HD, HD), HD)]

    edge_copy = rcopy(
        apad.at[3 - 3 * k, pl.ds(pl.multiple_of(PAD + (TILE - HALO) * (1 - k), HALO), HALO)],
        epad.at[pl.ds(PAD, HALO)], xhs.at[0], xhr.at[0], mate,
    )
    def unit(g, direct):
        lanes = slice(g * WIDE, (g + 1) * WIDE)
        low = c % 2 if direct else 1 - c % 2
        for q in range(2):
            p = low + 2 * q
            for e in range(2):
                b = 2 * p + e

                @pl.when((owner_of(b) != j) & (p != passed))
                def _(b=b):
                    rcopy(xg.at[g, b], xg.at[g, b], xps.at[g, 0, 0], xr.at[g, b], mate).wait_recv()

            rows = gelu(xg[g, pl.ds(2 * p, 2)].reshape(TILE, WIDE))
            apad[p, PAD : PAD + TILE, lanes] = rows
            ag[pl.ds(pl.multiple_of(HALO + p * TILE, HALO), TILE), lanes] = rows
        if g == GROUPS - 1 and not direct:
            edge_copy.start()
        weights = cwv[:, lanes, :].reshape(TAPS * WIDE, CH)
        for q in range(2):
            p = low + 2 * q
            windows = [apad[p, t * GAP : t * GAP + TILE + PAD, lanes] for t in range(TAPS)]
            rows = pl.ds(pl.multiple_of(p * TILE, TILE), TILE + PAD)
            acc_s[rows, :] = acc_s[rows, :] + dot(jnp.concatenate(windows, axis=1), weights)

    for t in range(TAPS):
        pltpu.make_async_copy(cw_hbm.at[t], cwv.at[t], wsem.at[t]).wait()
    relay(0)
    unit(0, True)
    x_left(1)
    send_x(2)
    relay(1)
    unit(1, True)
    unit(0, False)
    relay(2)
    og_in.wait()
    to_worker(do_copy, do_local)
    unit(2, True)
    unit(1, False)
    gain_in.wait()
    unit(2, False)

    for p in range(3):
        pltpu.make_async_copy(
            w_hbm.at[:, pl.ds(p * INNER + col, HD)], wh.at[:, pl.ds(p * HD, HD)], wsem.at[5 + p]
        ).wait()

    def finish_rows(p):
        rows = pl.ds(pl.multiple_of(HALO + p * 2 * TILE, HALO), 2 * TILE)
        x = jnp.concatenate([xg[g, pl.ds(4 * p, 4)].reshape(2 * TILE, WIDE) for g in range(GROUPS)], axis=1)
        acc = acc_s[rows, :] + x.astype(F32)
        acc_s[rows, :] = acc
        inv = lax.rsqrt(jnp.mean(acc * acc, -1, keepdims=True) + 1e-6)
        rows_bf = (acc * inv * gain_ref[...].reshape(1, CH)).astype(BF)
        nh[pl.ds(2 * p, 2)] = rows_bf.reshape(2, TILE, CH)
        outb = dot(rows_bf, wh[...]).astype(BF)
        kv[k, pl.ds(2 * p, 2)] = outb[:, HD:].reshape(2, TILE, 2 * HD)
        qd[pl.ds(pl.multiple_of(p * 2 * TILE, TILE), 2 * TILE), :] = outb[:, :HD]
        for e in range(2):
            qt_s[2 * p + e] = outb[e * TILE : (e + 1) * TILE, :HD].T
            vt_s[k * TILES + 2 * p + e] = outb[e * TILE : (e + 1) * TILE, 2 * HD :].T
        kv_copy(2 * p).start()
        kv_copy(2 * p + 1).start()

    finish_rows(k)
    edge_copy.wait_recv()
    ag[pl.ds(pl.multiple_of((HALF + HALO) * (1 - k), HALO), HALO), :] = epad[PAD : PAD + HALO, :]
    windows = [epad[pl.ds(pl.multiple_of((3 + k + q) * GAP, GAP), HALO), :] for q in range(2)]
    part = dot(jnp.concatenate(windows, axis=1), cwv[pl.ds(3 - 3 * k, 2)].reshape(2 * CH, CH))
    rows = pl.ds(pl.multiple_of(HALF - (HALF - HALO) * k, HALO), HALO)
    acc_s[rows, :] = acc_s[rows, :] + part
    finish_rows(1 - k)

    def hidden_rows(core):
        return acc_s.at[pl.ds(pl.multiple_of(HALO + (c % 4) * TILE + core * ROWS, HALO), ROWS)]

    hd_copy = rcopy(hidden_rows(1 - k), hid_s, hds.at[0], hdr.at[0], mate)

    @pl.when(k == c // 4)
    def _():
        hd_copy.start()
        hid_s[...] = hidden_rows(k)[...]

    def other_keys(p):
        rcopy(kv.at[1 - k, p], kv.at[1 - k, p], kvs.at[p], kvr.at[p], mate).wait_recv()
        vt_s[(1 - k) * TILES + p] = kv[1 - k, p, :, HD:].T

    loop(TILES, other_keys)

    def give(copy, local, p):
        for e in range(2):
            b = 2 * p + e
            pl.when(owner_of(b) != j)(lambda b=b: copy(b).start())
            pl.when(owner_of(b) == j)(lambda b=b: local(b))

    def o_copy(b):
        return rcopy(
            obuf.at[b], att_ref.at[:, pl.ds(col, HD)], os_.at[b], or_.at[c], {"seq": owner_of(b)}
        )

    def o_local(b):
        att_ref[:, pl.ds(col, HD)] = obuf[b]

    def forward(t):
        qt = qt_s[t]
        top = None
        for i in range(2 * TILES):
            s = dot(kv[i // TILES, i % TILES, :, :HD], qt)
            part = jnp.max(s.reshape(TILE // 8, 8, TILE), axis=0)
            top = part if top is None else jnp.maximum(top, part)
        top = jnp.max(top, axis=0, keepdims=True) * (TEMPER * LOG2E)
        total = jnp.zeros((8, TILE), F32)
        ot = jnp.zeros((HD, TILE), F32)
        lanes = pl.ds(pl.multiple_of(t * TILE, TILE), TILE)
        for i in range(2 * TILES):
            s = dot(kv[i // TILES, i % TILES, :, :HD], qt)
            p = jnp.exp2(s * (TEMPER * LOG2E) - top)
            total = total + jnp.sum(p.reshape(TILE // 8, 8, TILE), axis=0)
            pb = p.astype(BF)
            wts[i, :, lanes] = pb
            ot = ot + dot(vt_s[i], pb)
        rec = 1.0 / jnp.sum(total, axis=0, keepdims=True)
        otb = (ot * rec).astype(BF)
        ot_s[t] = otb
        stat_s[0, :, lanes] = jnp.broadcast_to(rec, (8, TILE))
        obuf[pl.ds(2 * t, 2)] = otb.T.reshape(2, ROWS, HD)

    def turn(i, core):
        return (c + i + core) % TILES

    def forward_two(i):
        forward(turn(2 * i, k))
        forward(turn(2 * i + 1, k))
        give(o_copy, o_local, turn(2 * i, k))
        give(o_copy, o_local, turn(2 * i + 1, k))

    loop(TILES // 2, forward_two)

    loop(CHIPS, lambda b: wait_slot(doh, dos, dor, b))
    for t in range(TILES):
        lanes = slice(t * TILE, (t + 1) * TILE)
        got = doh[2 * t : 2 * t + 2].reshape(TILE, HD).T
        dot_s[t] = got
        go = got.astype(F32)
        dots = jnp.sum(go * ot_s[t].astype(F32), axis=0, keepdims=True)
        stat_s[1, :, lanes] = jnp.broadcast_to(dots, (8, TILE))
        dor_s[lanes, :] = (go * stat_s[0, 0:1, lanes]).T.astype(BF)

    def backward(h, m):
        g = h * TILES + m
        vc = kv[h, m, :, HD:]
        w = wts[g]
        parts = []
        for t in range(TILES):
            lanes = slice(t * TILE, (t + 1) * TILE)
            gw = dot(vc, dot_s[t])
            slope = (gw - stat_s[1, 0:1, lanes]) * stat_s[0, 0:1, lanes]
            parts.append((w[:, lanes].astype(F32) * slope).astype(BF))
        ds = jnp.concatenate(parts, axis=1)
        dv = dot(w, dor_s[...])
        dk = dot(ds, qd[...])
        dqt[...] = dqt[...] + dot(kv[h, m, :, :HD].T, ds)
        return dk * TEMPER, dv

    def pr_copy(m):
        return rcopy(dkvp.at[m], pr.at[m], prs.at[m], prr.at[m], mate)

    early = turn(0, 1 - k)
    dk, dv = backward(1 - k, early)
    dkvp[early, 0] = dk
    dkvp[early, 1] = dv
    pr_copy(early).start()

    def kv_back(b):
        return rcopy(
            gsrc.at[b], res.at[c, 1:3], ks.at[b], kr.at[c], {"seq": owner_of(b)}
        )

    def kv_local(b):
        res[c, 1:3] = gsrc[b]

    def halves(i):
        m = turn(i, k)
        ahead = turn(i + 1, 1 - k)

        @pl.when(i < TILES - 1)
        def _():
            dk, dv = backward(1 - k, ahead)
            dkvp[ahead, 0] = dk
            dkvp[ahead, 1] = dv
            pr_copy(ahead).start()

        dk, dv = backward(k, m)
        pr_copy(m).wait_recv()
        dk = dk + pr[m, 0]
        dv = dv + pr[m, 1]
        for e in range(2):
            gsrc[2 * m + e, 0] = dk[e * ROWS : (e + 1) * ROWS].astype(BF)
            gsrc[2 * m + e, 1] = dv[e * ROWS : (e + 1) * ROWS].astype(BF)
        give(kv_back, kv_local, m)
        gt[m, HD : 2 * HD, :] = dk.T.astype(BF)
        gt[m, 2 * HD :, :] = dv.T.astype(BF)

    loop(TILES, halves)

    def dq_copy(b):
        return rcopy(
            dqb.at[b], res.at[c, 0], dqs.at[b], dqr.at[c], {"seq": owner_of(b)}
        )

    def dq_local(b):
        res[c, 0] = dqb[b]

    def query_back(i):
        t = turn(i, k)
        dq = dqt[:, pl.ds(pl.multiple_of(t * TILE, TILE), TILE)] * TEMPER
        dqb[pl.ds(2 * t, 2)] = dq.T.astype(BF).reshape(2, ROWS, HD)
        give(dq_copy, dq_local, t)
        gt[t, :HD, :] = dq.astype(BF)

    loop(TILES, query_back)

    gtf[...] = dot(jnp.concatenate([gt[t] for t in range(TILES)], axis=1), nh[...].reshape(HALF, CH))
    for p in range(3):
        rows = pl.ds(pl.multiple_of(p * HD + (1 - k) * 64, 64), 64)
        gst[p * 4 : p * 4 + 4] = gtf[rows, :].astype(BF).reshape(4, 16, CH)
    gp_copy = rcopy(gst, grcv, gps.at[0], gpr.at[0], mate)
    gp_copy.start()
    gp_copy.wait_recv()
    for p in range(3):
        rows = pl.ds(pl.multiple_of(p * HD + k * 64, 64), 64)
        own = gtf[rows, :].reshape(4, 16, CH)
        both = own + grcv[p * 4 : p * 4 + 4].astype(F32)
        for h in range(2):
            gown[8 * p + 4 * h : 8 * p + 4 * h + 4] = both[:, :, h * PART : (h + 1) * PART].astype(BF)

    z = d // 2
    xl = d % 2
    partner = {"dp": d + 1 - 2 * xl}

    def ring(off):
        zz = (z + off) % ZS
        return zz, {"dp": 2 * zz + xl}

    FAR = (4, 3, 5, 2, 6, 1, 7)

    def rq_copy(off):
        zz, dev = ring(off)
        return rcopy(gown.at[pl.ds(3 * zz, 3)], rq.at[z], rqs.at[zz], rqr.at[z], dev)

    for off in FAR:
        rq_copy(off).start()

    def back(copy):
        def step(i):
            chip = (c + i) % CHIPS
            pl.when(2 * chip + home != j)(lambda: copy(chip).wait_recv())

        loop(CHIPS, step)

    @pl.when(k != c // 4)
    def _():
        hd_copy.wait_recv()

    wf_copy.wait()

    def heads(i):
        return jnp.concatenate([res[h, i] for h in range(HEADS)], axis=1)

    back(lambda chip: rcopy(gsrc.at[0], res.at[chip, 1:3], ks.at[0], kr.at[chip], mate))
    gn_s[...] = dot_nt(jnp.concatenate([heads(1), heads(2)], axis=1), wfull[:, INNER:])
    back(lambda chip: rcopy(dqb.at[0], res.at[chip, 0], dqs.at[0], dqr.at[chip], mate))
    gn = gn_s[...] + dot_nt(heads(0), wfull[:, :INNER])
    hidden = hid_s[...]
    inv = lax.rsqrt(jnp.mean(hidden * hidden, -1, keepdims=True) + 1e-6)
    normed = hidden * inv
    scaled = gn * gain_ref[...].reshape(1, CH)
    gh = inv * (scaled - normed * jnp.mean(scaled * normed, -1, keepdims=True))
    hid_s[...] = gh
    ghb = gh.astype(BF)
    bext[HALO : HALO + ROWS, :] = ghb

    bst[...] = gh.T.astype(BF).reshape(CHIPS, 96, ROWS)

    def b_copy(chip, dev):
        return rcopy(bst.at[chip], bh.at[slot], bs.at[chip], br.at[slot], dev)

    def b_local(chip):
        bh[slot] = bst[chip]

    to_worker(b_copy, b_local)

    class Edges:
        def __init__(self, buf, ss, rs):
            self.up = rcopy(
                buf.at[ROWS : ROWS + HALO], buf.at[0:HALO], ss.at[0], rs.at[0], {"seq": (j + 1) % SEQ}
            )
            self.down = rcopy(
                buf.at[HALO : 2 * HALO], buf.at[HALO + ROWS :], ss.at[1], rs.at[1], {"seq": (j + SEQ - 1) % SEQ}
            )

        def start(self):
            pl.when(j < SEQ - 1)(lambda: self.up.start())
            pl.when(j > 0)(lambda: self.down.start())

        def wait_recv(self):
            pl.when(j > 0)(lambda: self.up.wait_recv())
            pl.when(j < SEQ - 1)(lambda: self.down.wait_recv())

        def wait_send(self):
            pl.when(j < SEQ - 1)(lambda: self.up.wait_send())
            pl.when(j > 0)(lambda: self.down.wait_send())

    edges = Edges(bext, h2s, h2r)
    edges.start()

    @pl.when(j == 0)
    def _():
        bext[0:HALO, :] = jnp.zeros((HALO, CH), BF)

    @pl.when(j == SEQ - 1)
    def _():
        bext[HALO + ROWS :, :] = jnp.zeros((HALO, CH), BF)

    def take(buf, ss, rs):
        for off in reversed(FAR):
            zz, dev = ring(off)
            rcopy(buf.at[zz], buf.at[zz], ss.at[zz], rs.at[zz], dev).wait_recv()
        total = buf[0].astype(F32)
        for i in range(1, ZS):
            total = total + buf[i].astype(F32)
        return total.astype(BF)

    rq[z] = gown[pl.ds(3 * z, 3)]
    redp[...] = take(rq, rqs, rqr)
    rp_copy = rcopy(redp, redr, rps.at[0], rpr.at[0], partner)
    rp_copy.start()

    rp_copy.wait_recv()
    red[...] = (redp[...].astype(F32) + redr[...].astype(F32)).astype(BF)

    def red_copy(i, off):
        hc = 3 * z + i
        unit = SEQ * (hc // 8) + j
        row = (unit % 3) * 8 + hc % 8
        zz = (z + off) % ZS
        dev = {"dp": 2 * zz + xl, "seq": unit // 3}
        return rcopy(red.at[i], gfin.at[row], gus.at[i, zz], gur.at[row], dev), unit // 3, row

    for i in range(3):
        for off in FAR:
            red_copy(i, off)[0].start()
        cp, owner, row = red_copy(i, 0)
        pl.when(owner != j)(cp.start)

        @pl.when(owner == j)
        def _(i=i, row=row):
            gfin[row] = red[i]

    def b_wait(b):
        wait_slot(bh, bs, br, b)

    loop(CHIPS, b_wait)
    for b in range(CHIPS):
        bt[:, b * ROWS : (b + 1) * ROWS] = bh[b]

    def cp_copy(o):
        return rcopy(cst.at[o], crcv.at[o], cps.at[o], cpr.at[o], mate)

    for o in range(2):
        n = 1 - xl if o == 0 else xl
        lanes = pl.ds(pl.multiple_of(n * PART, PART), PART)
        for t in range(TAPS):
            cg[o, t * 96 : t * 96 + 96, :] = dot(bt[...], ag[t * GAP : t * GAP + HALF, lanes])
        for t in range(TAPS):
            rows = pl.ds(pl.multiple_of(t * 96 + (1 - k) * 48, 48), 48)
            cst[o, t * 3 : t * 3 + 3] = cg[o, rows, :].astype(BF).reshape(3, 16, PART)
        cp_copy(o).start()

    give_c[15] = jnp.zeros((16, PART), BF)
    keep_c[15] = jnp.zeros((16, PART), F32)

    def with_mate(o):
        cp_copy(o).wait_recv()
        for t in range(TAPS):
            rows = pl.ds(pl.multiple_of(t * 96 + k * 48, 48), 48)
            own = cg[o, rows, :].reshape(3, 16, PART)
            both = own + crcv[o, t * 3 : t * 3 + 3].astype(F32)
            if o == 0:
                give_c[t * 3 : t * 3 + 3] = both.astype(BF)
            else:
                keep_c[t * 3 : t * 3 + 3] = both

    def px_copy(off):
        zz, _ = ring(off)
        return rcopy(give_c.at[pl.ds(2 * zz, 2)], px.at[zz], pxs.at[zz], pxr.at[zz], partner)

    with_mate(0)
    for off in FAR + (0,):
        px_copy(off).start()
    with_mate(1)

    def rc_copy(off):
        zz, dev = ring(off)
        return rcopy(zs.at[zz], rc.at[z], rcs.at[zz], rcr.at[z], dev)

    for off in FAR + (0,):
        zz, _ = ring(off)
        px_copy(off).wait_recv()
        both = (keep_c[pl.ds(2 * zz, 2)] + px[zz].astype(F32)).astype(BF)
        if off:
            zs[zz] = both
            rc_copy(off).start()
        else:
            rc[z] = both

    edges.wait_recv()
    ga = jnp.zeros((ROWS, CH), F32)
    for t in range(TAPS):
        lo = (TAPS - 1 - t) * GAP
        ga = ga + dot_nt(bext[lo : lo + ROWS, :], cwv[t])
    x = x_ref[...].astype(F32)
    th = gelu_tanh(x)
    slope = 0.5 * (1.0 + th) + 0.5 * x * (1.0 - th * th) * GELU_A * (1.0 + 3.0 * GELU_B * x * x)
    gi_ref[...] = (hid_s[...] + slope * ga).astype(BF)

    def pair(n, zz):
        return cfin.at[n, pl.ds(2 * zz, 2)]

    def fin_copy(i):
        to = (d + i) % DP
        return rcopy(pair(xl, z), pair(xl, z), fzs.at[to], fzr.at[xl, z], {"dp": to})

    cfin[xl, pl.ds(2 * z, 2)] = take(rc, rcs, rcr)
    for i in (8, 7, 9, 6, 10, 5, 11, 4, 12, 3, 13, 2, 14, 1, 15):
        fin_copy(i).start()

    def o_wait(chip):
        @pl.when(2 * chip + home != j)
        def _():
            lanes = pl.ds(pl.multiple_of(chip * HD, HD), HD)
            rcopy(obuf.at[0], att_ref.at[:, lanes], os_.at[0], or_.at[chip], mate).wait_recv()

    loop(CHIPS, o_wait)

    def land_q(row):
        u = 3 * j + row // 8
        hc = 8 * (u // SEQ) + row % 8

        @pl.when((u % SEQ != j) | (hc // 3 != z))
        def _():
            rcopy(red.at[0], gfin.at[row], gus.at[0, 0], gur.at[row], mate).wait_recv()

    loop(24, land_q)
    def land_c(i):
        n = i // ZS
        zz = i % ZS

        @pl.when((n != xl) | (zz != z))
        def _():
            rcopy(pair(n, zz), pair(n, zz), fzs.at[0], fzr.at[n, zz], partner).wait_recv()

    loop(DP, land_c)

    for g in range(GROUPS):
        if g == GROUPS - 1:
            x_left(g)
        pl.when(home != k)(lambda g=g: x_copy(g, 4).wait_send())
        for e in range(2):
            pass_copy(g, e, flip_x, 0).wait_send()
            pl.when(inside)(lambda g=g, e=e: pass_copy(g, e, flip_x, 1).wait_send())
    edge_copy.wait_send()
    to_worker_done(do_copy)
    to_worker_done(b_copy)
    pl.when(k == c // 4)(lambda: hd_copy.wait_send())
    edges.wait_send()

    def mates(p):
        kv_copy(p).wait_send()
        pr_copy(p).wait_send()

    loop(TILES, mates)

    def given(b):
        @pl.when(owner_of(b) != j)
        def _():
            o_copy(b).wait_send()
            kv_back(b).wait_send()
            dq_copy(b).wait_send()

    loop(CHIPS, given)
    gp_copy.wait_send()

    rp_copy.wait_send()
    for i in range(3):
        for off in FAR:
            red_copy(i, off)[0].wait_send()
        cp, owner, _ = red_copy(i, 0)
        pl.when(owner != j)(cp.wait_send)
    for o in range(2):
        cp_copy(o).wait_send()
    for off in FAR:
        rq_copy(off).wait_send()
        rc_copy(off).wait_send()
    for off in range(ZS):
        px_copy(off).wait_send()
    loop(15, lambda i: fin_copy(i + 1).wait_send())


def finish(att_ref, gi_ref, cfin, gfin, att_out, gi_out, cw_out, w_out, cbuf, gbuf, sem):
    copies = [pltpu.make_async_copy(att_ref, att_out, sem.at[0]), pltpu.make_async_copy(gi_ref, gi_out, sem.at[1])]
    for cp in copies:
        cp.start()
    for r in range(3):
        for h in range(2):
            piece = gfin[8 * r + 4 * h : 8 * r + 4 * h + 4].astype(F32).reshape(64, PART)
            gbuf[64 * r : 64 * r + 64, h * PART : (h + 1) * PART] = piece
    copies.append(pltpu.make_async_copy(gbuf, w_out, sem.at[2]))
    copies[-1].start()
    for n in range(2):
        cbuf[:, n * PART : (n + 1) * PART] = cfin[n, :15].astype(F32).reshape(240, PART)
    copies.append(pltpu.make_async_copy(cbuf, cw_out, sem.at[3]))
    copies[-1].start()
    for cp in copies:
        cp.wait()


def body(inputs, convolution_weight, w_qkv, gain, out_grad):
    vm = pl.BlockSpec(memory_space=pltpu.VMEM)
    hbm = pl.BlockSpec(memory_space=pl.ANY)
    V = pltpu.VMEM

    def sem(*n):
        return pltpu.SemaphoreType.DMA(n)

    scratch = [
        V((ROWS, CH), BF),
        V((CH,), F32),
        V((ROWS, INNER), BF),
        V((TAPS, CH, CH), BF),
        V((CH, 3 * INNER), BF),
        V((CH, 3 * HD), BF),
        V((GROUPS, CHIPS, ROWS, WIDE), BF),
        V((HALF + 2 * HALO, CH), BF),
        V((TILES, TILE + 2 * PAD, CH), BF),
        V((HALO + 2 * PAD, CH), BF),
        V((HALF + 2 * HALO, CH), F32),
        V((ROWS, CH), F32),
        V((ROWS, CH), F32),
        V((TILES, TILE, CH), BF),
        V((CHIPS, ROWS, HD), BF),
        V((TILES, HD, TILE), BF),
        V((HALF, HD), BF),
        V((TILES, HD, TILE), BF),
        V((2, TILES, TILE, 2 * HD), BF),
        V((2 * TILES, HD, TILE), BF),
        V((2 * TILES, TILE, HALF), BF),
        V((2, 8, HALF), F32),
        V((TILES, HD, TILE), BF),
        V((HALF, HD), BF),
        V((HD, HALF), F32),
        V((TILES, 2, TILE, HD), F32),
        V((TILES, 2, TILE, HD), F32),
        V((CHIPS, ROWS, HD), BF),
        V((CHIPS, ROWS, HD), BF),
        V((CHIPS, 2, ROWS, HD), BF),
        V((TILES, 3 * HD, TILE), BF),
        V((HEADS, 3, ROWS, HD), BF),
        V((3 * HD, CH), F32),
        V((12, 16, CH), BF),
        V((12, 16, CH), BF),
        V((24, 16, PART), BF),
        V((ZS, 3, 16, PART), BF),
        V((3, 16, PART), BF),
        V((3, 16, PART), BF),
        V((3, 16, PART), BF),
        V((ROWS + 2 * HALO, CH), BF),
        V((CHIPS, 96, ROWS), BF),
        V((CHIPS, 96, ROWS), BF),
        V((96, HALF), BF),
        V((2, TAPS * 96, PART), F32),
        V((2, 15, 16, PART), BF),
        V((2, 15, 16, PART), BF),
        V((16, 16, PART), BF),
        V((16, 16, PART), F32),
        V((ZS, 2, 16, PART), BF),
        V((ZS, 2, 16, PART), BF),
        V((ZS, 2, 16, PART), BF),
        sem(12),
        sem(3, 5), sem(3, 8), sem(3, 2, 2), sem(1), sem(1),
        sem(8), sem(8), sem(1), sem(1),
        sem(4), sem(4), sem(8), sem(8), sem(8), sem(8), sem(8), sem(8), sem(4), sem(4),
        sem(1), sem(1), sem(8), sem(8), sem(1), sem(1), sem(3, 8), sem(24),
        sem(2), sem(2), sem(8), sem(8), sem(2), sem(2),
        sem(8), sem(8), sem(8), sem(8), sem(16), sem(2, 8),
    ]
    att, gi, cfin, gfin = pl.pallas_call(
        kernel,
        out_shape=[
            jax.ShapeDtypeStruct((ROWS, INNER), BF),
            jax.ShapeDtypeStruct((ROWS, CH), BF),
            jax.ShapeDtypeStruct((2, 16, 16, PART), BF),
            jax.ShapeDtypeStruct((24, 16, PART), BF),
        ],
        in_specs=[hbm] * 5,
        out_specs=[vm, vm, vm, vm],
        scratch_shapes=scratch,
        compiler_params=pltpu.CompilerParams(
            collective_id=0, has_side_effects=True, vmem_limit_bytes=58 * 1024 * 1024
        ),
        cost_estimate=pl.CostEstimate(flops=14_000_000_000, bytes_accessed=15_000_000, transcendentals=3_000_000),
    )(inputs[0], gain, out_grad[0], convolution_weight, w_qkv)
    att, gi, conv, qkv = pl.pallas_call(
        finish,
        out_shape=[
            jax.ShapeDtypeStruct((ROWS, INNER), BF),
            jax.ShapeDtypeStruct((ROWS, CH), BF),
            jax.ShapeDtypeStruct((240, CH), F32),
            jax.ShapeDtypeStruct((192, CH), F32),
        ],
        in_specs=[vm, vm, vm, vm],
        out_specs=[hbm, hbm, hbm, hbm],
        scratch_shapes=[V((240, CH), F32), V((192, CH), F32), sem(4)],
    )(att, gi, cfin, gfin)
    return att[None], gi[None], conv.reshape(TAPS, 48, CH).transpose(0, 2, 1), qkv.T


def solution(mesh):
    in_specs = (P("dp", "seq", None), P(), P(), P(), P("dp", "seq", None))
    out_specs = (P("dp", "seq", None), P("dp", "seq", None), P(None, None, "seq"), P(None, "seq"))
    return jax.shard_map(body, mesh=mesh, in_specs=in_specs, out_specs=out_specs, check_vma=False)
```

```python
import jax
import jax.numpy as jnp
from jax import lax
from jax.experimental import pallas as pl
from jax.experimental.pallas import tpu as pltpu
from jax.sharding import PartitionSpec as P

CH = 768
HEADS = 8
HD = 128
INNER = HEADS * HD
TAPS = 5
GAP = 16
HALO = 32
PAD = 2 * HALO
ROWS = 128
SEQ = 16
DP = 16
ZS = 8
CHIPS = 8
HALF = CHIPS * ROWS
TILE = 256
TILES = HALF // TILE
PART = 384
GROUPS = 3
WIDE = CH // GROUPS
TEMPER = HD ** (-0.5)
LOG2E = 1.4426950408889634
GELU_A = 0.7978845608028654
GELU_B = 0.044715
BF = jnp.bfloat16
F32 = jnp.float32
MESH = pl.DeviceIdType.MESH


def rcopy(src, dst, ss, rs, dev):
    return pltpu.make_async_remote_copy(
        src_ref=src, dst_ref=dst, send_sem=ss, recv_sem=rs, device_id=dev, device_id_type=MESH
    )


def dot(a, b):
    return jnp.dot(a, b, preferred_element_type=F32)


def dot_nt(a, b):
    return lax.dot_general(a, b, (((1,), (1,)), ((), ())), preferred_element_type=F32)


def flip(a):
    return a.astype(F32).T


def gelu_tanh(x):
    return jnp.tanh(GELU_A * (x + GELU_B * x * x * x))


def gelu(x):
    x = x.astype(F32)
    return (0.5 * x * (1.0 + gelu_tanh(x))).astype(BF)


def loop(n, step):
    lax.fori_loop(0, n, lambda i, carry: (step(i), carry)[1], 0)


def kernel(
    x_hbm, gain_hbm, og_hbm, cw_hbm, w_hbm,
    att_out, gi_out, ct_out, gq_out,
    att_ref, gi_ref, cfin, gfin, ctf, gqf, x_ref, gain_ref, og_ref, cwv, wfull, wh, xg, ag, apad, epad, acc_s, gn_s, hid_s, nh, doh, dot_s, qd, qt_s, kv, vt_s,
    wts, stat_s, ot_s, dor_s, dqt, dkvp, pr, obuf, dqb, gsrc, gt, res, gtf, gst, grcv, gown,
    rq, redp, redr, red, bext, bst, bh, bt, cg, cst, crcv, give_c, keep_c, px, zs, rc,
    wsem, xs, xr, xps, xhs, xhr, dos, dor, hds, hdr, kvs, kvr, os_, or_, dqs, dqr, ks, kr, prs, prr,
    gps, gpr, rqs, rqr, rps, rpr, gus, gur, h2s, h2r, bs, br, cps, cpr,
    pxs, pxr, rcs, rcr, fzs, fzr, fxs, fxr,
):
    j = lax.axis_index("seq")
    d = lax.axis_index("dp")
    c = j // 2
    k = j % 2
    mate = {"seq": j + 1 - 2 * k}
    home = j // CHIPS
    slot = j % CHIPS
    col = pl.multiple_of(c * HD, HD)

    barrier = pltpu.get_barrier_semaphore()

    def hello(i):
        pl.semaphore_signal(barrier, inc=1, device_id={"seq": (j + i + 1) % SEQ}, device_id_type=MESH)
        pl.semaphore_signal(barrier, inc=1, device_id={"dp": (d + i + 1) % DP}, device_id_type=MESH)

    loop(15, hello)
    x_in = pltpu.make_async_copy(x_hbm, x_ref, wsem.at[9])
    og_in = pltpu.make_async_copy(og_hbm, og_ref, wsem.at[10])
    gain_in = pltpu.make_async_copy(gain_hbm, gain_ref, wsem.at[11])
    x_in.start()
    og_in.start()
    gain_in.start()
    for t in range(TAPS):
        pltpu.make_async_copy(cw_hbm.at[t], cwv.at[t], wsem.at[t]).start()
    for p in range(3):
        pltpu.make_async_copy(
            w_hbm.at[:, pl.ds(p * INNER + col, HD)], wh.at[:, pl.ds(p * HD, HD)], wsem.at[5 + p]
        ).start()
    wf_copy = pltpu.make_async_copy(w_hbm, wfull, wsem.at[8])
    wf_copy.start()

    dqt[...] = jnp.zeros_like(dqt)
    acc_s[...] = jnp.zeros_like(acc_s)
    for p in range(TILES):
        apad[p, :PAD, :] = jnp.zeros((PAD, CH), BF)
        apad[p, PAD + TILE :, :] = jnp.zeros((PAD, CH), BF)
    epad[:PAD, :] = jnp.zeros((PAD, CH), BF)
    epad[PAD + HALO :, :] = jnp.zeros((PAD, CH), BF)

    @pl.when(k == 0)
    def _():
        ag[0:HALO, :] = jnp.zeros((HALO, CH), BF)

    @pl.when(k == 1)
    def _():
        ag[HALO + HALF :, :] = jnp.zeros((HALO, CH), BF)

    pl.semaphore_wait(barrier, 30)

    def to_worker(copy, local):
        def step(i):
            chip = (c + CHIPS - 1 - i) % CHIPS
            dev = 2 * chip + home

            @pl.when(dev != j)
            def _():
                copy(chip, {"seq": dev}).start()

            if local is not None:
                pl.when(dev == j)(lambda: local(chip))

        loop(CHIPS, step)

    def to_worker_done(copy):
        def step(chip):
            dev = 2 * chip + home

            @pl.when(dev != j)
            def _():
                copy(chip, {"seq": dev}).wait_send()

        loop(CHIPS, step)

    def owner_of(b):
        return CHIPS * k + b

    flip_x = c + 1 - 2 * (c % 2)
    near = (flip_x, (c + 2) % CHIPS, (c + 6) % CHIPS, (c + 4) % CHIPS, c)

    def x_copy(g, i):
        src = x_ref.at[:, g * WIDE : (g + 1) * WIDE]
        return rcopy(src, xg.at[g, slot], xs.at[g, i], xr.at[g, slot], {"seq": 2 * near[i] + home})

    def x_left(g):
        for i in range(4):
            x_copy(g, i).wait_send()

    def send_x(g):
        for i in range(4):
            x_copy(g, i).start()
        pl.when(home != k)(lambda: x_copy(g, 4).start())

        @pl.when(home == k)
        def _():
            xg[g, slot] = x_ref[:, g * WIDE : (g + 1) * WIDE]

    x_in.wait()
    send_x(0)
    x_left(0)
    send_x(1)

    inside = c // 4 == k
    passed = jnp.where(inside, flip_x, (c + 4) % CHIPS) - 4 * k

    def pass_copy(g, e, chip, i):
        b = 2 * passed + e
        return rcopy(xg.at[g, b], xg.at[g, b], xps.at[g, e, i], xr.at[g, b], {"seq": 2 * chip + k})

    def hand_on(g, e):
        b = 2 * passed + e
        rcopy(xg.at[g, b], xg.at[g, b], xps.at[g, e, 0], xr.at[g, b], mate).wait_recv()

        @pl.when(inside)
        def _():
            pass_copy(g, e, near[1], 0).start()
            pass_copy(g, e, near[2], 1).start()

        pl.when(c // 4 != k)(lambda: pass_copy(g, e, flip_x, 0).start())

    def relay(g):
        hand_on(g, 0)
        hand_on(g, 1)

    def wait_slot(buf, ss, rs, b):
        @pl.when(owner_of(b) != j)
        def _():
            rcopy(buf.at[b], buf.at[b], ss.at[0], rs.at[b], mate).wait_recv()

    def kv_copy(p):
        return rcopy(kv.at[k, p], kv.at[k, p], kvs.at[p], kvr.at[p], mate)

    def do_copy(chip, dev):
        src = og_ref.at[:, pl.ds(pl.multiple_of(chip * HD, HD), HD)]
        return rcopy(src, doh.at[slot], dos.at[chip], dor.at[slot], dev)

    def do_local(chip):
        doh[slot] = og_ref[:, pl.ds(pl.multiple_of(chip * HD, HD), HD)]

    edge_copy = rcopy(
        apad.at[3 - 3 * k, pl.ds(pl.multiple_of(PAD + (TILE - HALO) * (1 - k), HALO), HALO)],
        epad.at[pl.ds(PAD, HALO)], xhs.at[0], xhr.at[0], mate,
    )
    def unit(g, direct):
        lanes = slice(g * WIDE, (g + 1) * WIDE)
        low = c % 2 if direct else 1 - c % 2
        for q in range(2):
            p = low + 2 * q
            for e in range(2):
                b = 2 * p + e

                @pl.when((owner_of(b) != j) & (p != passed))
                def _(b=b):
                    rcopy(xg.at[g, b], xg.at[g, b], xps.at[g, 0, 0], xr.at[g, b], mate).wait_recv()

            rows = gelu(xg[g, pl.ds(2 * p, 2)].reshape(TILE, WIDE))
            apad[p, PAD : PAD + TILE, lanes] = rows
            ag[pl.ds(pl.multiple_of(HALO + p * TILE, HALO), TILE), lanes] = rows
        if g == GROUPS - 1 and not direct:
            edge_copy.start()
        weights = cwv[:, lanes, :].reshape(TAPS * WIDE, CH)
        for q in range(2):
            p = low + 2 * q
            windows = [apad[p, t * GAP : t * GAP + TILE + PAD, lanes] for t in range(TAPS)]
            rows = pl.ds(pl.multiple_of(p * TILE, TILE), TILE + PAD)
            acc_s[rows, :] = acc_s[rows, :] + dot(jnp.concatenate(windows, axis=1), weights)

    for t in range(TAPS):
        pltpu.make_async_copy(cw_hbm.at[t], cwv.at[t], wsem.at[t]).wait()
    relay(0)
    unit(0, True)
    x_left(1)
    send_x(2)
    relay(1)
    unit(1, True)
    unit(0, False)
    relay(2)
    og_in.wait()
    to_worker(do_copy, do_local)
    unit(2, True)
    unit(1, False)
    gain_in.wait()
    unit(2, False)

    for p in range(3):
        pltpu.make_async_copy(
            w_hbm.at[:, pl.ds(p * INNER + col, HD)], wh.at[:, pl.ds(p * HD, HD)], wsem.at[5 + p]
        ).wait()

    def finish_rows(p):
        rows = pl.ds(pl.multiple_of(HALO + p * 2 * TILE, HALO), 2 * TILE)
        x = jnp.concatenate([xg[g, pl.ds(4 * p, 4)].reshape(2 * TILE, WIDE) for g in range(GROUPS)], axis=1)
        acc = acc_s[rows, :] + x.astype(F32)
        acc_s[rows, :] = acc
        inv = lax.rsqrt(jnp.mean(acc * acc, -1, keepdims=True) + 1e-6)
        rows_bf = (acc * inv * gain_ref[...].reshape(1, CH)).astype(BF)
        nh[pl.ds(2 * p, 2)] = rows_bf.reshape(2, TILE, CH)
        outb = dot(rows_bf, wh[...]).astype(BF)
        kv[k, pl.ds(2 * p, 2)] = outb[:, HD:].reshape(2, TILE, 2 * HD)
        qd[pl.ds(pl.multiple_of(p * 2 * TILE, TILE), 2 * TILE), :] = outb[:, :HD]
        for e in range(2):
            qt_s[2 * p + e] = outb[e * TILE : (e + 1) * TILE, :HD].T
            vt_s[k * TILES + 2 * p + e] = outb[e * TILE : (e + 1) * TILE, 2 * HD :].T
        kv_copy(2 * p).start()
        kv_copy(2 * p + 1).start()

    finish_rows(k)
    edge_copy.wait_recv()
    ag[pl.ds(pl.multiple_of((HALF + HALO) * (1 - k), HALO), HALO), :] = epad[PAD : PAD + HALO, :]
    windows = [epad[pl.ds(pl.multiple_of((3 + k + q) * GAP, GAP), HALO), :] for q in range(2)]
    part = dot(jnp.concatenate(windows, axis=1), cwv[pl.ds(3 - 3 * k, 2)].reshape(2 * CH, CH))
    rows = pl.ds(pl.multiple_of(HALF - (HALF - HALO) * k, HALO), HALO)
    acc_s[rows, :] = acc_s[rows, :] + part
    finish_rows(1 - k)

    def hidden_rows(core):
        return acc_s.at[pl.ds(pl.multiple_of(HALO + (c % 4) * TILE + core * ROWS, HALO), ROWS)]

    hd_copy = rcopy(hidden_rows(1 - k), hid_s, hds.at[0], hdr.at[0], mate)

    @pl.when(k == c // 4)
    def _():
        hd_copy.start()
        hid_s[...] = hidden_rows(k)[...]

    def other_keys(p):
        rcopy(kv.at[1 - k, p], kv.at[1 - k, p], kvs.at[p], kvr.at[p], mate).wait_recv()
        vt_s[(1 - k) * TILES + p] = kv[1 - k, p, :, HD:].T

    loop(TILES, other_keys)

    def give(copy, local, p):
        for e in range(2):
            b = 2 * p + e
            pl.when(owner_of(b) != j)(lambda b=b: copy(b).start())
            pl.when(owner_of(b) == j)(lambda b=b: local(b))

    def o_copy(b):
        return rcopy(
            obuf.at[b], att_ref.at[:, pl.ds(col, HD)], os_.at[b], or_.at[c], {"seq": owner_of(b)}
        )

    def o_local(b):
        att_ref[:, pl.ds(col, HD)] = obuf[b]

    def forward(t):
        qt = qt_s[t]
        top = None
        for i in range(2 * TILES):
            s = dot(kv[i // TILES, i % TILES, :, :HD], qt)
            part = jnp.max(s.reshape(TILE // 8, 8, TILE), axis=0)
            top = part if top is None else jnp.maximum(top, part)
        top = jnp.max(top, axis=0, keepdims=True) * (TEMPER * LOG2E)
        total = jnp.zeros((8, TILE), F32)
        ot = jnp.zeros((HD, TILE), F32)
        lanes = pl.ds(pl.multiple_of(t * TILE, TILE), TILE)
        for i in range(2 * TILES):
            s = dot(kv[i // TILES, i % TILES, :, :HD], qt)
            p = jnp.exp2(s * (TEMPER * LOG2E) - top)
            total = total + jnp.sum(p.reshape(TILE // 8, 8, TILE), axis=0)
            pb = p.astype(BF)
            wts[i, :, lanes] = pb
            ot = ot + dot(vt_s[i], pb)
        rec = 1.0 / jnp.sum(total, axis=0, keepdims=True)
        otb = (ot * rec).astype(BF)
        ot_s[t] = otb
        stat_s[0, :, lanes] = jnp.broadcast_to(rec, (8, TILE))
        obuf[pl.ds(2 * t, 2)] = otb.T.reshape(2, ROWS, HD)

    def turn(i, core):
        return (c + i + core) % TILES

    def forward_two(i):
        forward(turn(2 * i, k))
        forward(turn(2 * i + 1, k))
        give(o_copy, o_local, turn(2 * i, k))
        give(o_copy, o_local, turn(2 * i + 1, k))

    loop(TILES // 2, forward_two)

    loop(CHIPS, lambda b: wait_slot(doh, dos, dor, b))
    for t in range(TILES):
        lanes = slice(t * TILE, (t + 1) * TILE)
        got = doh[2 * t : 2 * t + 2].reshape(TILE, HD).T
        dot_s[t] = got
        go = got.astype(F32)
        dots = jnp.sum(go * ot_s[t].astype(F32), axis=0, keepdims=True)
        stat_s[1, :, lanes] = jnp.broadcast_to(dots, (8, TILE))
        dor_s[lanes, :] = (go * stat_s[0, 0:1, lanes]).T.astype(BF)

    def backward(h, m):
        g = h * TILES + m
        vc = kv[h, m, :, HD:]
        w = wts[g]
        parts = []
        for t in range(TILES):
            lanes = slice(t * TILE, (t + 1) * TILE)
            gw = dot(vc, dot_s[t])
            slope = (gw - stat_s[1, 0:1, lanes]) * stat_s[0, 0:1, lanes]
            parts.append((w[:, lanes].astype(F32) * slope).astype(BF))
        ds = jnp.concatenate(parts, axis=1)
        return dot(ds, qd[...]) * TEMPER, dot(w, dor_s[...]), kv[h, m, :, :HD].T, ds

    def add_queries(*parts):
        keys = jnp.concatenate([part[2] for part in parts], axis=1)
        dqt[...] = dqt[...] + dot(keys, jnp.concatenate([part[3] for part in parts], axis=0))

    def pr_copy(m):
        return rcopy(dkvp.at[m], pr.at[m], prs.at[m], prr.at[m], mate)

    def hand_over(m, part):
        dkvp[m, 0] = part[0]
        dkvp[m, 1] = part[1]
        pr_copy(m).start()

    early = backward(1 - k, turn(0, 1 - k))
    hand_over(turn(0, 1 - k), early)
    add_queries(early)

    def kv_back(b):
        return rcopy(
            gsrc.at[b], res.at[c, 1:3], ks.at[b], kr.at[c], {"seq": owner_of(b)}
        )

    def kv_local(b):
        res[c, 1:3] = gsrc[b]

    def complete(m, part):
        pr_copy(m).wait_recv()
        dk = part[0] + pr[m, 0]
        dv = part[1] + pr[m, 1]
        for e in range(2):
            gsrc[2 * m + e, 0] = dk[e * ROWS : (e + 1) * ROWS].astype(BF)
            gsrc[2 * m + e, 1] = dv[e * ROWS : (e + 1) * ROWS].astype(BF)
        give(kv_back, kv_local, m)
        gt[m, HD : 2 * HD, :] = dk.T.astype(BF)
        gt[m, 2 * HD :, :] = dv.T.astype(BF)

    def halves(i):
        ahead = backward(1 - k, turn(i + 1, 1 - k))
        own = backward(k, turn(i, k))
        add_queries(ahead, own)
        hand_over(turn(i + 1, 1 - k), ahead)
        complete(turn(i, k), own)

    loop(TILES - 1, halves)
    last = backward(k, turn(TILES - 1, k))
    add_queries(last)
    complete(turn(TILES - 1, k), last)

    def dq_copy(b):
        return rcopy(
            dqb.at[b], res.at[c, 0], dqs.at[b], dqr.at[c], {"seq": owner_of(b)}
        )

    def dq_local(b):
        res[c, 0] = dqb[b]

    def query_back(i):
        t = turn(i, k)
        dq = dqt[:, pl.ds(pl.multiple_of(t * TILE, TILE), TILE)] * TEMPER
        dqb[pl.ds(2 * t, 2)] = dq.T.astype(BF).reshape(2, ROWS, HD)
        give(dq_copy, dq_local, t)
        gt[t, :HD, :] = dq.astype(BF)

    loop(TILES, query_back)

    gtf[...] = dot(jnp.concatenate([gt[t] for t in range(TILES)], axis=1), nh[...].reshape(HALF, CH))
    for p in range(3):
        rows = pl.ds(pl.multiple_of(p * HD + (1 - k) * 64, 64), 64)
        gst[p * 4 : p * 4 + 4] = gtf[rows, :].astype(BF).reshape(4, 16, CH)
    gp_copy = rcopy(gst, grcv, gps.at[0], gpr.at[0], mate)
    gp_copy.start()
    gp_copy.wait_recv()
    for p in range(3):
        rows = pl.ds(pl.multiple_of(p * HD + k * 64, 64), 64)
        own = gtf[rows, :].reshape(4, 16, CH)
        both = own + grcv[p * 4 : p * 4 + 4].astype(F32)
        for h in range(2):
            gown[8 * p + 4 * h : 8 * p + 4 * h + 4] = both[:, :, h * PART : (h + 1) * PART].astype(BF)

    z = d // 2
    xl = d % 2
    partner = {"dp": d + 1 - 2 * xl}

    def ring(off):
        zz = (z + off) % ZS
        return zz, {"dp": 2 * zz + xl}

    FAR = (4, 3, 5, 2, 6, 1, 7)

    def rq_copy(off):
        zz, dev = ring(off)
        return rcopy(gown.at[pl.ds(3 * zz, 3)], rq.at[z], rqs.at[zz], rqr.at[z], dev)

    for off in FAR:
        rq_copy(off).start()

    def back(copy):
        def step(i):
            chip = (c + i) % CHIPS
            pl.when(2 * chip + home != j)(lambda: copy(chip).wait_recv())

        loop(CHIPS, step)

    @pl.when(k != c // 4)
    def _():
        hd_copy.wait_recv()

    wf_copy.wait()

    def heads(i):
        return jnp.concatenate([res[h, i] for h in range(HEADS)], axis=1)

    back(lambda chip: rcopy(gsrc.at[0], res.at[chip, 1:3], ks.at[0], kr.at[chip], mate))
    gn_s[...] = dot_nt(jnp.concatenate([heads(1), heads(2)], axis=1), wfull[:, INNER:])
    back(lambda chip: rcopy(dqb.at[0], res.at[chip, 0], dqs.at[0], dqr.at[chip], mate))
    gn = gn_s[...] + dot_nt(heads(0), wfull[:, :INNER])
    hidden = hid_s[...]
    inv = lax.rsqrt(jnp.mean(hidden * hidden, -1, keepdims=True) + 1e-6)
    normed = hidden * inv
    scaled = gn * gain_ref[...].reshape(1, CH)
    gh = inv * (scaled - normed * jnp.mean(scaled * normed, -1, keepdims=True))
    hid_s[...] = gh
    ghb = gh.astype(BF)
    bext[HALO : HALO + ROWS, :] = ghb

    bst[...] = gh.T.astype(BF).reshape(CHIPS, 96, ROWS)

    def b_copy(chip, dev):
        return rcopy(bst.at[chip], bh.at[slot], bs.at[chip], br.at[slot], dev)

    def b_local(chip):
        bh[slot] = bst[chip]

    to_worker(b_copy, b_local)

    class Edges:
        def __init__(self, buf, ss, rs):
            self.up = rcopy(
                buf.at[ROWS : ROWS + HALO], buf.at[0:HALO], ss.at[0], rs.at[0], {"seq": (j + 1) % SEQ}
            )
            self.down = rcopy(
                buf.at[HALO : 2 * HALO], buf.at[HALO + ROWS :], ss.at[1], rs.at[1], {"seq": (j + SEQ - 1) % SEQ}
            )

        def start(self):
            pl.when(j < SEQ - 1)(lambda: self.up.start())
            pl.when(j > 0)(lambda: self.down.start())

        def wait_recv(self):
            pl.when(j > 0)(lambda: self.up.wait_recv())
            pl.when(j < SEQ - 1)(lambda: self.down.wait_recv())

        def wait_send(self):
            pl.when(j < SEQ - 1)(lambda: self.up.wait_send())
            pl.when(j > 0)(lambda: self.down.wait_send())

    edges = Edges(bext, h2s, h2r)
    edges.start()

    @pl.when(j == 0)
    def _():
        bext[0:HALO, :] = jnp.zeros((HALO, CH), BF)

    @pl.when(j == SEQ - 1)
    def _():
        bext[HALO + ROWS :, :] = jnp.zeros((HALO, CH), BF)

    def take(buf, ss, rs):
        for off in reversed(FAR):
            zz, dev = ring(off)
            rcopy(buf.at[zz], buf.at[zz], ss.at[zz], rs.at[zz], dev).wait_recv()
        total = buf[0].astype(F32)
        for i in range(1, ZS):
            total = total + buf[i].astype(F32)
        return total.astype(BF)

    rq[z] = gown[pl.ds(3 * z, 3)]
    redp[...] = take(rq, rqs, rqr)
    rp_copy = rcopy(redp, redr, rps.at[0], rpr.at[0], partner)
    rp_copy.start()

    rp_copy.wait_recv()
    red[...] = (redp[...].astype(F32) + redr[...].astype(F32)).astype(BF)

    def red_copy(i, off):
        hc = 3 * z + i
        unit = SEQ * (hc // 8) + j
        row = (unit % 3) * 8 + hc % 8
        zz = (z + off) % ZS
        dev = {"dp": 2 * zz + xl, "seq": unit // 3}
        return rcopy(red.at[i], gfin.at[row], gus.at[i, zz], gur.at[row], dev), unit // 3, row

    for i in range(3):
        for off in FAR:
            red_copy(i, off)[0].start()
        cp, owner, row = red_copy(i, 0)
        pl.when(owner != j)(cp.start)

        @pl.when(owner == j)
        def _(i=i, row=row):
            gfin[row] = red[i]

    def b_wait(b):
        wait_slot(bh, bs, br, b)

    loop(CHIPS, b_wait)
    for b in range(CHIPS):
        bt[:, b * ROWS : (b + 1) * ROWS] = bh[b]

    def cp_copy(o):
        return rcopy(cst.at[o], crcv.at[o], cps.at[o], cpr.at[o], mate)

    for o in range(2):
        n = 1 - xl if o == 0 else xl
        lanes = pl.ds(pl.multiple_of(n * PART, PART), PART)
        for t in range(TAPS):
            cg[o, t * 96 : t * 96 + 96, :] = dot(bt[...], ag[t * GAP : t * GAP + HALF, lanes])
        for t in range(TAPS):
            rows = pl.ds(pl.multiple_of(t * 96 + (1 - k) * 48, 48), 48)
            cst[o, t * 3 : t * 3 + 3] = cg[o, rows, :].astype(BF).reshape(3, 16, PART)
        cp_copy(o).start()

    give_c[15] = jnp.zeros((16, PART), BF)
    keep_c[15] = jnp.zeros((16, PART), F32)

    def with_mate(o):
        cp_copy(o).wait_recv()
        for t in range(TAPS):
            rows = pl.ds(pl.multiple_of(t * 96 + k * 48, 48), 48)
            own = cg[o, rows, :].reshape(3, 16, PART)
            both = own + crcv[o, t * 3 : t * 3 + 3].astype(F32)
            if o == 0:
                give_c[t * 3 : t * 3 + 3] = both.astype(BF)
            else:
                keep_c[t * 3 : t * 3 + 3] = both

    def px_copy(h, off):
        zz, _ = ring(off)
        return rcopy(give_c.at[2 * zz + h], px.at[h, zz], pxs.at[h, zz], pxr.at[h, zz], partner)

    with_mate(0)
    for h in range(2):
        for off in FAR + (0,):
            px_copy(h, off).start()
    with_mate(1)

    def rc_copy(h, off):
        zz, dev = ring(off)
        return rcopy(zs.at[h, zz], rc.at[h, z], rcs.at[h, zz], rcr.at[h, z], dev)

    for h in range(2):
        for off in FAR + (0,):
            zz, _ = ring(off)
            px_copy(h, off).wait_recv()
            both = (keep_c[2 * zz + h] + px[h, zz].astype(F32)).astype(BF)
            if off:
                zs[h, zz] = both
                rc_copy(h, off).start()
            else:
                rc[h, z] = both

    def piece(n, h, zz):
        return cfin.at[n, 2 * zz + h]

    def fz_copy(h, off):
        zz, dev = ring(off)
        return rcopy(piece(xl, h, z), piece(xl, h, z), fzs.at[h, zz], fzr.at[h, z], dev)

    def fx_copy(h, zz):
        return rcopy(piece(xl, h, zz), piece(xl, h, zz), fxs.at[h, zz], fxr.at[h, zz], partner)

    for h in range(2):
        cfin[xl, 2 * z + h] = take(rc.at[h], rcs.at[h], rcr.at[h])
        for off in FAR:
            fz_copy(h, off).start()
        fx_copy(h, z).start()
    edges.wait_recv()
    ga = jnp.zeros((ROWS, CH), F32)
    for t in range(TAPS):
        lo = (TAPS - 1 - t) * GAP
        ga = ga + dot_nt(bext[lo : lo + ROWS, :], cwv[t])
    x = x_ref[...].astype(F32)
    th = gelu_tanh(x)
    slope = 0.5 * (1.0 + th) + 0.5 * x * (1.0 - th * th) * GELU_A * (1.0 + 3.0 * GELU_B * x * x)
    gi_ref[...] = (hid_s[...] + slope * ga).astype(BF)

    for h in range(2):
        for off in reversed(FAR):
            zz, _ = ring(off)
            here = piece(xl, h, zz)
            rcopy(here, here, fzs.at[0, 0], fzr.at[h, zz], partner).wait_recv()
            fx_copy(h, zz).start()

    def o_wait(chip):
        @pl.when(2 * chip + home != j)
        def _():
            lanes = pl.ds(pl.multiple_of(chip * HD, HD), HD)
            rcopy(obuf.at[0], att_ref.at[:, lanes], os_.at[0], or_.at[chip], mate).wait_recv()

    loop(CHIPS, o_wait)
    att_copy = pltpu.make_async_copy(att_ref, att_out, wsem.at[12])
    gi_copy = pltpu.make_async_copy(gi_ref, gi_out, wsem.at[13])
    att_copy.start()
    gi_copy.start()

    def land_q(row):
        u = 3 * j + row // 8
        hc = 8 * (u // SEQ) + row % 8

        @pl.when((u % SEQ != j) | (hc // 3 != z))
        def _():
            rcopy(red.at[0], gfin.at[row], gus.at[0, 0], gur.at[row], mate).wait_recv()

    loop(24, land_q)
    for r in range(3):
        for h in range(2):
            block = gfin[8 * r + 4 * h : 8 * r + 4 * h + 4].astype(F32).reshape(64, PART)
            gqf[64 * r : 64 * r + 64, h * PART : (h + 1) * PART] = block
    gq_copy = pltpu.make_async_copy(gqf, gq_out, wsem.at[14])
    gq_copy.start()
    def land_c(i):
        here = piece(1 - xl, i // ZS, i % ZS)
        rcopy(here, here, fzs.at[0, 0], fxr.at[i // ZS, i % ZS], partner).wait_recv()

    loop(2 * ZS, land_c)
    for n in range(2):
        ctf[:, n * PART : (n + 1) * PART] = cfin[n, :15].astype(F32).reshape(240, PART)
    ct_copy = pltpu.make_async_copy(ctf, ct_out, wsem.at[15])
    ct_copy.start()

    for g in range(GROUPS):
        if g == GROUPS - 1:
            x_left(g)
        pl.when(home != k)(lambda g=g: x_copy(g, 4).wait_send())
        for e in range(2):
            pass_copy(g, e, flip_x, 0).wait_send()
            pl.when(inside)(lambda g=g, e=e: pass_copy(g, e, flip_x, 1).wait_send())
    edge_copy.wait_send()
    to_worker_done(do_copy)
    to_worker_done(b_copy)
    pl.when(k == c // 4)(lambda: hd_copy.wait_send())
    edges.wait_send()

    def mates(p):
        kv_copy(p).wait_send()
        pr_copy(p).wait_send()

    loop(TILES, mates)

    def given(b):
        @pl.when(owner_of(b) != j)
        def _():
            o_copy(b).wait_send()
            kv_back(b).wait_send()
            dq_copy(b).wait_send()

    loop(CHIPS, given)
    gp_copy.wait_send()

    rp_copy.wait_send()
    for i in range(3):
        for off in FAR:
            red_copy(i, off)[0].wait_send()
        cp, owner, _ = red_copy(i, 0)
        pl.when(owner != j)(cp.wait_send)
    for o in range(2):
        cp_copy(o).wait_send()
    for off in FAR:
        rq_copy(off).wait_send()
        rc_copy(0, off).wait_send()
        rc_copy(1, off).wait_send()
    for off in range(ZS):
        px_copy(0, off).wait_send()
        px_copy(1, off).wait_send()
        for h in range(2):
            fx_copy(h, ring(off)[0]).wait_send()
            if off:
                fz_copy(h, off).wait_send()

    for copy in (att_copy, gi_copy, gq_copy, ct_copy):
        copy.wait()


def finish(a, b, c, d, a_out, b_out, c_out, d_out, a_buf, b_buf, c_buf, d_buf, sem):
    parts = ((a, a_buf, a_out), (b, b_buf, b_out), (c, c_buf, c_out), (d, d_buf, d_out))
    reads = [pltpu.make_async_copy(src, buf, sem.at[i]) for i, (src, buf, _) in enumerate(parts)]
    writes = [pltpu.make_async_copy(buf, dst, sem.at[4 + i]) for i, (_, buf, dst) in enumerate(parts)]
    for copy in reads:
        copy.start()
    for i in range(4):
        reads[i].wait()
        writes[i].start()
    for copy in writes:
        copy.wait()


def body(inputs, convolution_weight, w_qkv, gain, out_grad):
    hbm = pl.BlockSpec(memory_space=pl.ANY)
    V = pltpu.VMEM

    def sem(*n):
        return pltpu.SemaphoreType.DMA(n)

    scratch = [
        V((ROWS, INNER), BF),
        V((ROWS, CH), BF),
        V((2, 16, 16, PART), BF),
        V((24, 16, PART), BF),
        V((240, CH), F32),
        V((192, CH), F32),
        V((ROWS, CH), BF),
        V((CH,), F32),
        V((ROWS, INNER), BF),
        V((TAPS, CH, CH), BF),
        V((CH, 3 * INNER), BF),
        V((CH, 3 * HD), BF),
        V((GROUPS, CHIPS, ROWS, WIDE), BF),
        V((HALF + 2 * HALO, CH), BF),
        V((TILES, TILE + 2 * PAD, CH), BF),
        V((HALO + 2 * PAD, CH), BF),
        V((HALF + 2 * HALO, CH), F32),
        V((ROWS, CH), F32),
        V((ROWS, CH), F32),
        V((TILES, TILE, CH), BF),
        V((CHIPS, ROWS, HD), BF),
        V((TILES, HD, TILE), BF),
        V((HALF, HD), BF),
        V((TILES, HD, TILE), BF),
        V((2, TILES, TILE, 2 * HD), BF),
        V((2 * TILES, HD, TILE), BF),
        V((2 * TILES, TILE, HALF), BF),
        V((2, 8, HALF), F32),
        V((TILES, HD, TILE), BF),
        V((HALF, HD), BF),
        V((HD, HALF), F32),
        V((TILES, 2, TILE, HD), F32),
        V((TILES, 2, TILE, HD), F32),
        V((CHIPS, ROWS, HD), BF),
        V((CHIPS, ROWS, HD), BF),
        V((CHIPS, 2, ROWS, HD), BF),
        V((TILES, 3 * HD, TILE), BF),
        V((HEADS, 3, ROWS, HD), BF),
        V((3 * HD, CH), F32),
        V((12, 16, CH), BF),
        V((12, 16, CH), BF),
        V((24, 16, PART), BF),
        V((ZS, 3, 16, PART), BF),
        V((3, 16, PART), BF),
        V((3, 16, PART), BF),
        V((3, 16, PART), BF),
        V((ROWS + 2 * HALO, CH), BF),
        V((CHIPS, 96, ROWS), BF),
        V((CHIPS, 96, ROWS), BF),
        V((96, HALF), BF),
        V((2, TAPS * 96, PART), F32),
        V((2, 15, 16, PART), BF),
        V((2, 15, 16, PART), BF),
        V((16, 16, PART), BF),
        V((16, 16, PART), F32),
        V((2, ZS, 16, PART), BF),
        V((2, ZS, 16, PART), BF),
        V((2, ZS, 16, PART), BF),
        sem(16),
        sem(3, 5), sem(3, 8), sem(3, 2, 2), sem(1), sem(1),
        sem(8), sem(8), sem(1), sem(1),
        sem(4), sem(4), sem(8), sem(8), sem(8), sem(8), sem(8), sem(8), sem(4), sem(4),
        sem(1), sem(1), sem(8), sem(8), sem(1), sem(1), sem(3, 8), sem(24),
        sem(2), sem(2), sem(8), sem(8), sem(2), sem(2),
        sem(2, 8), sem(2, 8), sem(2, 8), sem(2, 8), sem(2, 8), sem(2, 8),
        sem(2, 8), sem(2, 8),
    ]
    att, gi, cfin, gfin = pl.pallas_call(
        kernel,
        out_shape=[
            jax.ShapeDtypeStruct((ROWS, INNER), BF),
            jax.ShapeDtypeStruct((ROWS, CH), BF),
            jax.ShapeDtypeStruct((240, CH), F32),
            jax.ShapeDtypeStruct((192, CH), F32),
        ],
        in_specs=[hbm] * 5,
        out_specs=[hbm] * 4,
        scratch_shapes=scratch,
        compiler_params=pltpu.CompilerParams(
            collective_id=0, has_side_effects=True, vmem_limit_bytes=58 * 1024 * 1024
        ),
        cost_estimate=pl.CostEstimate(flops=14_000_000_000, bytes_accessed=15_000_000, transcendentals=3_000_000),
    )(inputs[0], gain, out_grad[0], convolution_weight, w_qkv)
    att, gi, conv, qkv = pl.pallas_call(
        finish,
        out_shape=[
            jax.ShapeDtypeStruct((ROWS, INNER), BF),
            jax.ShapeDtypeStruct((ROWS, CH), BF),
            jax.ShapeDtypeStruct((240, CH), F32),
            jax.ShapeDtypeStruct((192, CH), F32),
        ],
        in_specs=[hbm] * 4,
        out_specs=[hbm] * 4,
        scratch_shapes=[V((ROWS, INNER), BF), V((ROWS, CH), BF), V((240, CH), F32), V((192, CH), F32), sem(8)],
    )(att, gi, cfin, gfin)
    return att[None], gi[None], conv.reshape(TAPS, 48, CH).transpose(0, 2, 1), qkv.T


def solution(mesh):
    in_specs = (P("dp", "seq", None), P(), P(), P(), P("dp", "seq", None))
    out_specs = (P("dp", "seq", None), P("dp", "seq", None), P(None, None, "seq"), P(None, "seq"))
    return jax.shard_map(body, mesh=mesh, in_specs=in_specs, out_specs=out_specs, check_vma=False)
```

```python
import jax
import jax.numpy as jnp
from jax import lax
from jax.experimental import pallas as pl
from jax.experimental.pallas import tpu as pltpu
from jax.sharding import PartitionSpec as P

CH = 768
HEADS = 8
HD = 128
INNER = HEADS * HD
TAPS = 5
GAP = 16
HALO = 32
PAD = 2 * HALO
ROWS = 128
SEQ = 16
DP = 16
ZS = 8
CHIPS = 8
HALF = CHIPS * ROWS
TILE = 256
TILES = HALF // TILE
PART = 384
GROUPS = 3
WIDE = CH // GROUPS
TEMPER = HD ** (-0.5)
LOG2E = 1.4426950408889634
GELU_A = 0.7978845608028654
GELU_B = 0.044715
BF = jnp.bfloat16
F32 = jnp.float32
MESH = pl.DeviceIdType.MESH


def rcopy(src, dst, ss, rs, dev):
    return pltpu.make_async_remote_copy(
        src_ref=src, dst_ref=dst, send_sem=ss, recv_sem=rs, device_id=dev, device_id_type=MESH
    )


def dot(a, b):
    return jnp.dot(a, b, preferred_element_type=F32)


def dot_nt(a, b):
    return lax.dot_general(a, b, (((1,), (1,)), ((), ())), preferred_element_type=F32)


def flip(a):
    return a.astype(F32).T


def gelu_tanh(x):
    return jnp.tanh(GELU_A * (x + GELU_B * x * x * x))


def gelu(x):
    x = x.astype(F32)
    return (0.5 * x * (1.0 + gelu_tanh(x))).astype(BF)


def loop(n, step):
    lax.fori_loop(0, n, lambda i, carry: (step(i), carry)[1], 0)


def kernel(
    x_hbm, gain_hbm, og_hbm, cw_hbm, w_hbm,
    att_out, gi_out, ct_out, gq_out,
    att_ref, gi_ref, cfin, gfin, ctf, gqf, x_ref, gain_ref, og_ref, cwv, wfull, wh, xg, ag, apad, epad, acc_s, gn_s, hid_s, nh, doh, dot_s, qd, qt_s, kv, vt_s,
    wts, stat_s, ot_s, dor_s, dqt, dkvp, pr, obuf, dqb, gsrc, gt, res, gtf, gst, grcv, gown,
    rq, redp, redr, red, bext, bst, bh, bt, cg, cst, crcv, give_c, keep_c, px, zs, rc,
    wsem, xs, xr, xps, xhs, xhr, dos, dor, hds, hdr, kvs, kvr, os_, or_, dqs, dqr, ks, kr, prs, prr,
    gps, gpr, rqs, rqr, rps, rpr, gus, gur, h2s, h2r, bs, br, cps, cpr,
    pxs, pxr, rcs, rcr, fzs, fzr, fxs, fxr,
):
    j = lax.axis_index("seq")
    d = lax.axis_index("dp")
    c = j // 2
    k = j % 2
    mate = {"seq": j + 1 - 2 * k}
    home = j // CHIPS
    slot = j % CHIPS
    col = pl.multiple_of(c * HD, HD)

    barrier = pltpu.get_barrier_semaphore()

    def hello(i):
        pl.semaphore_signal(barrier, inc=1, device_id={"seq": (j + i + 1) % SEQ}, device_id_type=MESH)
        pl.semaphore_signal(barrier, inc=1, device_id={"dp": (d + i + 1) % DP}, device_id_type=MESH)

    loop(15, hello)
    x_in = pltpu.make_async_copy(x_hbm, x_ref, wsem.at[9])
    og_in = pltpu.make_async_copy(og_hbm, og_ref, wsem.at[10])
    gain_in = pltpu.make_async_copy(gain_hbm, gain_ref, wsem.at[11])
    x_in.start()
    og_in.start()
    gain_in.start()
    for t in range(TAPS):
        pltpu.make_async_copy(cw_hbm.at[t], cwv.at[t], wsem.at[t]).start()
    for p in range(3):
        pltpu.make_async_copy(
            w_hbm.at[:, pl.ds(p * INNER + col, HD)], wh.at[:, pl.ds(p * HD, HD)], wsem.at[5 + p]
        ).start()
    wf_copy = pltpu.make_async_copy(w_hbm, wfull, wsem.at[8])
    wf_copy.start()

    dqt[...] = jnp.zeros_like(dqt)
    acc_s[...] = jnp.zeros_like(acc_s)
    for p in range(TILES):
        apad[p, :PAD, :] = jnp.zeros((PAD, CH), BF)
        apad[p, PAD + TILE :, :] = jnp.zeros((PAD, CH), BF)
    epad[:PAD, :] = jnp.zeros((PAD, CH), BF)
    epad[PAD + HALO :, :] = jnp.zeros((PAD, CH), BF)

    @pl.when(k == 0)
    def _():
        ag[0:HALO, :] = jnp.zeros((HALO, CH), BF)

    @pl.when(k == 1)
    def _():
        ag[HALO + HALF :, :] = jnp.zeros((HALO, CH), BF)

    pl.semaphore_wait(barrier, 30)

    def to_worker(copy, local):
        def step(i):
            chip = (c + CHIPS - 1 - i) % CHIPS
            dev = 2 * chip + home

            @pl.when(dev != j)
            def _():
                copy(chip, {"seq": dev}).start()

            if local is not None:
                pl.when(dev == j)(lambda: local(chip))

        loop(CHIPS, step)

    def to_worker_done(copy):
        def step(chip):
            dev = 2 * chip + home

            @pl.when(dev != j)
            def _():
                copy(chip, {"seq": dev}).wait_send()

        loop(CHIPS, step)

    def owner_of(b):
        return CHIPS * k + b

    flip_x = c + 1 - 2 * (c % 2)
    near = (flip_x, (c + 2) % CHIPS, (c + 6) % CHIPS, (c + 4) % CHIPS, c)

    def x_copy(g, i):
        src = x_ref.at[:, g * WIDE : (g + 1) * WIDE]
        return rcopy(src, xg.at[g, slot], xs.at[g, i], xr.at[g, slot], {"seq": 2 * near[i] + home})

    def x_left(g):
        for i in range(4):
            x_copy(g, i).wait_send()

    def send_x(g):
        for i in range(4):
            x_copy(g, i).start()
        pl.when(home != k)(lambda: x_copy(g, 4).start())

        @pl.when(home == k)
        def _():
            xg[g, slot] = x_ref[:, g * WIDE : (g + 1) * WIDE]

    x_in.wait()
    send_x(0)
    send_x(1)

    inside = c // 4 == k
    passed = jnp.where(inside, flip_x, (c + 4) % CHIPS) - 4 * k

    def pass_copy(g, e, chip, i):
        b = 2 * passed + e
        return rcopy(xg.at[g, b], xg.at[g, b], xps.at[g, e, i], xr.at[g, b], {"seq": 2 * chip + k})

    def hand_on(g, e):
        b = 2 * passed + e
        rcopy(xg.at[g, b], xg.at[g, b], xps.at[g, e, 0], xr.at[g, b], mate).wait_recv()

        @pl.when(inside)
        def _():
            pass_copy(g, e, near[1], 0).start()
            pass_copy(g, e, near[2], 1).start()

        pl.when(c // 4 != k)(lambda: pass_copy(g, e, flip_x, 0).start())

    def relay(g):
        hand_on(g, 0)
        hand_on(g, 1)

    def wait_slot(buf, ss, rs, b):
        @pl.when(owner_of(b) != j)
        def _():
            rcopy(buf.at[b], buf.at[b], ss.at[0], rs.at[b], mate).wait_recv()

    def kv_copy(p):
        return rcopy(kv.at[k, p], kv.at[k, p], kvs.at[p], kvr.at[p], mate)

    def do_copy(chip, dev):
        src = og_ref.at[:, pl.ds(pl.multiple_of(chip * HD, HD), HD)]
        return rcopy(src, doh.at[slot], dos.at[chip], dor.at[slot], dev)

    def do_local(chip):
        doh[slot] = og_ref[:, pl.ds(pl.multiple_of(chip * HD, HD), HD)]

    edge_copy = rcopy(
        apad.at[3 - 3 * k, pl.ds(pl.multiple_of(PAD + (TILE - HALO) * (1 - k), HALO), HALO)],
        epad.at[pl.ds(PAD, HALO)], xhs.at[0], xhr.at[0], mate,
    )
    def unit(g, direct):
        lanes = slice(g * WIDE, (g + 1) * WIDE)
        low = c % 2 if direct else 1 - c % 2
        for q in range(2):
            p = low + 2 * q
            for e in range(2):
                b = 2 * p + e

                @pl.when((owner_of(b) != j) & (p != passed))
                def _(b=b):
                    rcopy(xg.at[g, b], xg.at[g, b], xps.at[g, 0, 0], xr.at[g, b], mate).wait_recv()

            rows = gelu(xg[g, pl.ds(2 * p, 2)].reshape(TILE, WIDE))
            apad[p, PAD : PAD + TILE, lanes] = rows
            ag[pl.ds(pl.multiple_of(HALO + p * TILE, HALO), TILE), lanes] = rows
        if g == GROUPS - 1 and not direct:
            edge_copy.start()
        weights = cwv[:, lanes, :].reshape(TAPS * WIDE, CH)
        for q in range(2):
            p = low + 2 * q
            windows = [apad[p, t * GAP : t * GAP + TILE + PAD, lanes] for t in range(TAPS)]
            rows = pl.ds(pl.multiple_of(p * TILE, TILE), TILE + PAD)
            acc_s[rows, :] = acc_s[rows, :] + dot(jnp.concatenate(windows, axis=1), weights)

    for t in range(TAPS):
        pltpu.make_async_copy(cw_hbm.at[t], cwv.at[t], wsem.at[t]).wait()
    relay(0)
    send_x(2)
    unit(0, True)
    relay(1)
    unit(1, True)
    unit(0, False)
    relay(2)
    og_in.wait()
    to_worker(do_copy, do_local)
    unit(2, True)
    unit(1, False)
    gain_in.wait()
    unit(2, False)

    for p in range(3):
        pltpu.make_async_copy(
            w_hbm.at[:, pl.ds(p * INNER + col, HD)], wh.at[:, pl.ds(p * HD, HD)], wsem.at[5 + p]
        ).wait()

    def finish_rows(p):
        rows = pl.ds(pl.multiple_of(HALO + p * 2 * TILE, HALO), 2 * TILE)
        x = jnp.concatenate([xg[g, pl.ds(4 * p, 4)].reshape(2 * TILE, WIDE) for g in range(GROUPS)], axis=1)
        acc = acc_s[rows, :] + x.astype(F32)
        acc_s[rows, :] = acc
        inv = lax.rsqrt(jnp.mean(acc * acc, -1, keepdims=True) + 1e-6)
        rows_bf = (acc * inv * gain_ref[...].reshape(1, CH)).astype(BF)
        nh[pl.ds(2 * p, 2)] = rows_bf.reshape(2, TILE, CH)
        outb = dot(rows_bf, wh[...]).astype(BF)
        kv[k, pl.ds(2 * p, 2)] = outb[:, HD:].reshape(2, TILE, 2 * HD)
        qd[pl.ds(pl.multiple_of(p * 2 * TILE, TILE), 2 * TILE), :] = outb[:, :HD]
        for e in range(2):
            qt_s[2 * p + e] = outb[e * TILE : (e + 1) * TILE, :HD].T
            vt_s[k * TILES + 2 * p + e] = outb[e * TILE : (e + 1) * TILE, 2 * HD :].T
        kv_copy(2 * p).start()
        kv_copy(2 * p + 1).start()

    finish_rows(k)
    edge_copy.wait_recv()
    ag[pl.ds(pl.multiple_of((HALF + HALO) * (1 - k), HALO), HALO), :] = epad[PAD : PAD + HALO, :]
    windows = [epad[pl.ds(pl.multiple_of((3 + k + q) * GAP, GAP), HALO), :] for q in range(2)]
    part = dot(jnp.concatenate(windows, axis=1), cwv[pl.ds(3 - 3 * k, 2)].reshape(2 * CH, CH))
    rows = pl.ds(pl.multiple_of(HALF - (HALF - HALO) * k, HALO), HALO)
    acc_s[rows, :] = acc_s[rows, :] + part
    finish_rows(1 - k)

    def hidden_rows(core):
        return acc_s.at[pl.ds(pl.multiple_of(HALO + (c % 4) * TILE + core * ROWS, HALO), ROWS)]

    hd_copy = rcopy(hidden_rows(1 - k), hid_s, hds.at[0], hdr.at[0], mate)

    @pl.when(k == c // 4)
    def _():
        hd_copy.start()
        hid_s[...] = hidden_rows(k)[...]

    def other_keys(p):
        rcopy(kv.at[1 - k, p], kv.at[1 - k, p], kvs.at[p], kvr.at[p], mate).wait_recv()
        vt_s[(1 - k) * TILES + p] = kv[1 - k, p, :, HD:].T

    loop(TILES, other_keys)

    def give(copy, local, p):
        for e in range(2):
            b = 2 * p + e
            pl.when(owner_of(b) != j)(lambda b=b: copy(b).start())
            pl.when(owner_of(b) == j)(lambda b=b: local(b))

    def o_copy(b):
        return rcopy(
            obuf.at[b], att_ref.at[:, pl.ds(col, HD)], os_.at[b], or_.at[c], {"seq": owner_of(b)}
        )

    def o_local(b):
        att_ref[:, pl.ds(col, HD)] = obuf[b]

    def forward(t):
        qt = qt_s[t]
        top = None
        for i in range(2 * TILES):
            s = dot(kv[i // TILES, i % TILES, :, :HD], qt)
            part = jnp.max(s.reshape(TILE // 8, 8, TILE), axis=0)
            top = part if top is None else jnp.maximum(top, part)
        top = jnp.max(top, axis=0, keepdims=True) * (TEMPER * LOG2E)
        total = jnp.zeros((8, TILE), F32)
        ot = jnp.zeros((HD, TILE), F32)
        lanes = pl.ds(pl.multiple_of(t * TILE, TILE), TILE)
        for i in range(2 * TILES):
            s = dot(kv[i // TILES, i % TILES, :, :HD], qt)
            p = jnp.exp2(s * (TEMPER * LOG2E) - top)
            total = total + jnp.sum(p.reshape(TILE // 8, 8, TILE), axis=0)
            pb = p.astype(BF)
            wts[i, :, lanes] = pb
            ot = ot + dot(vt_s[i], pb)
        rec = 1.0 / jnp.sum(total, axis=0, keepdims=True)
        otb = (ot * rec).astype(BF)
        ot_s[t] = otb
        stat_s[0, :, lanes] = jnp.broadcast_to(rec, (8, TILE))
        obuf[pl.ds(2 * t, 2)] = otb.T.reshape(2, ROWS, HD)

    def turn(i, core):
        return (c + i + core) % TILES

    def forward_two(i):
        forward(turn(2 * i, k))
        forward(turn(2 * i + 1, k))
        give(o_copy, o_local, turn(2 * i, k))
        give(o_copy, o_local, turn(2 * i + 1, k))

    loop(TILES // 2, forward_two)

    loop(CHIPS, lambda b: wait_slot(doh, dos, dor, b))
    for t in range(TILES):
        lanes = slice(t * TILE, (t + 1) * TILE)
        got = doh[2 * t : 2 * t + 2].reshape(TILE, HD).T
        dot_s[t] = got
        go = got.astype(F32)
        dots = jnp.sum(go * ot_s[t].astype(F32), axis=0, keepdims=True)
        stat_s[1, :, lanes] = jnp.broadcast_to(dots, (8, TILE))
        dor_s[lanes, :] = (go * stat_s[0, 0:1, lanes]).T.astype(BF)

    def backward(h, m):
        g = h * TILES + m
        vc = kv[h, m, :, HD:]
        w = wts[g]
        parts = []
        for t in range(TILES):
            lanes = slice(t * TILE, (t + 1) * TILE)
            gw = dot(vc, dot_s[t])
            slope = (gw - stat_s[1, 0:1, lanes]) * stat_s[0, 0:1, lanes]
            parts.append((w[:, lanes].astype(F32) * slope).astype(BF))
        ds = jnp.concatenate(parts, axis=1)
        return dot(ds, qd[...]) * TEMPER, dot(w, dor_s[...]), kv[h, m, :, :HD].T, ds

    def add_queries(*parts):
        keys = jnp.concatenate([part[2] for part in parts], axis=1)
        dqt[...] = dqt[...] + dot(keys, jnp.concatenate([part[3] for part in parts], axis=0))

    def pr_copy(m):
        return rcopy(dkvp.at[m], pr.at[m], prs.at[m], prr.at[m], mate)

    def hand_over(m, part):
        dkvp[m, 0] = part[0]
        dkvp[m, 1] = part[1]
        pr_copy(m).start()

    early = backward(1 - k, turn(0, 1 - k))
    hand_over(turn(0, 1 - k), early)
    add_queries(early)

    def kv_back(b):
        return rcopy(
            gsrc.at[b], res.at[c, 1:3], ks.at[b], kr.at[c], {"seq": owner_of(b)}
        )

    def kv_local(b):
        res[c, 1:3] = gsrc[b]

    def complete(m, part):
        pr_copy(m).wait_recv()
        dk = part[0] + pr[m, 0]
        dv = part[1] + pr[m, 1]
        for e in range(2):
            gsrc[2 * m + e, 0] = dk[e * ROWS : (e + 1) * ROWS].astype(BF)
            gsrc[2 * m + e, 1] = dv[e * ROWS : (e + 1) * ROWS].astype(BF)
        give(kv_back, kv_local, m)
        gt[m, HD : 2 * HD, :] = dk.T.astype(BF)
        gt[m, 2 * HD :, :] = dv.T.astype(BF)

    def halves(i):
        ahead = backward(1 - k, turn(i + 1, 1 - k))
        own = backward(k, turn(i, k))
        add_queries(ahead, own)
        hand_over(turn(i + 1, 1 - k), ahead)
        complete(turn(i, k), own)

    loop(TILES - 1, halves)
    last = backward(k, turn(TILES - 1, k))
    add_queries(last)
    complete(turn(TILES - 1, k), last)

    def dq_copy(b):
        return rcopy(
            dqb.at[b], res.at[c, 0], dqs.at[b], dqr.at[c], {"seq": owner_of(b)}
        )

    def dq_local(b):
        res[c, 0] = dqb[b]

    def query_back(i):
        t = turn(i, k)
        dq = dqt[:, pl.ds(pl.multiple_of(t * TILE, TILE), TILE)] * TEMPER
        dqb[pl.ds(2 * t, 2)] = dq.T.astype(BF).reshape(2, ROWS, HD)
        give(dq_copy, dq_local, t)
        gt[t, :HD, :] = dq.astype(BF)

    loop(TILES, query_back)

    gtf[...] = dot(jnp.concatenate([gt[t] for t in range(TILES)], axis=1), nh[...].reshape(HALF, CH))
    for p in range(3):
        rows = pl.ds(pl.multiple_of(p * HD + (1 - k) * 64, 64), 64)
        gst[p * 4 : p * 4 + 4] = gtf[rows, :].astype(BF).reshape(4, 16, CH)
    gp_copy = rcopy(gst, grcv, gps.at[0], gpr.at[0], mate)
    gp_copy.start()
    gp_copy.wait_recv()
    for p in range(3):
        rows = pl.ds(pl.multiple_of(p * HD + k * 64, 64), 64)
        own = gtf[rows, :].reshape(4, 16, CH)
        both = own + grcv[p * 4 : p * 4 + 4].astype(F32)
        for h in range(2):
            gown[8 * p + 4 * h : 8 * p + 4 * h + 4] = both[:, :, h * PART : (h + 1) * PART].astype(BF)

    z = d // 2
    xl = d % 2
    partner = {"dp": d + 1 - 2 * xl}

    def ring(off):
        zz = (z + off) % ZS
        return zz, {"dp": 2 * zz + xl}

    FAR = (4, 3, 5, 2, 6, 1, 7)

    def rq_copy(off):
        zz, dev = ring(off)
        return rcopy(gown.at[pl.ds(3 * zz, 3)], rq.at[z], rqs.at[zz], rqr.at[z], dev)

    for off in FAR:
        rq_copy(off).start()

    def back(copy):
        def step(i):
            chip = (c + i) % CHIPS
            pl.when(2 * chip + home != j)(lambda: copy(chip).wait_recv())

        loop(CHIPS, step)

    @pl.when(k != c // 4)
    def _():
        hd_copy.wait_recv()

    wf_copy.wait()

    def heads(i):
        return jnp.concatenate([res[h, i] for h in range(HEADS)], axis=1)

    back(lambda chip: rcopy(gsrc.at[0], res.at[chip, 1:3], ks.at[0], kr.at[chip], mate))
    gn_s[...] = dot_nt(jnp.concatenate([heads(1), heads(2)], axis=1), wfull[:, INNER:])
    back(lambda chip: rcopy(dqb.at[0], res.at[chip, 0], dqs.at[0], dqr.at[chip], mate))
    gn = gn_s[...] + dot_nt(heads(0), wfull[:, :INNER])
    hidden = hid_s[...]
    inv = lax.rsqrt(jnp.mean(hidden * hidden, -1, keepdims=True) + 1e-6)
    normed = hidden * inv
    scaled = gn * gain_ref[...].reshape(1, CH)
    gh = inv * (scaled - normed * jnp.mean(scaled * normed, -1, keepdims=True))
    hid_s[...] = gh
    ghb = gh.astype(BF)
    bext[HALO : HALO + ROWS, :] = ghb

    bst[...] = gh.T.astype(BF).reshape(CHIPS, 96, ROWS)

    def b_copy(chip, dev):
        return rcopy(bst.at[chip], bh.at[slot], bs.at[chip], br.at[slot], dev)

    def b_local(chip):
        bh[slot] = bst[chip]

    to_worker(b_copy, b_local)

    class Edges:
        def __init__(self, buf, ss, rs):
            self.up = rcopy(
                buf.at[ROWS : ROWS + HALO], buf.at[0:HALO], ss.at[0], rs.at[0], {"seq": (j + 1) % SEQ}
            )
            self.down = rcopy(
                buf.at[HALO : 2 * HALO], buf.at[HALO + ROWS :], ss.at[1], rs.at[1], {"seq": (j + SEQ - 1) % SEQ}
            )

        def start(self):
            pl.when(j < SEQ - 1)(lambda: self.up.start())
            pl.when(j > 0)(lambda: self.down.start())

        def wait_recv(self):
            pl.when(j > 0)(lambda: self.up.wait_recv())
            pl.when(j < SEQ - 1)(lambda: self.down.wait_recv())

        def wait_send(self):
            pl.when(j < SEQ - 1)(lambda: self.up.wait_send())
            pl.when(j > 0)(lambda: self.down.wait_send())

    edges = Edges(bext, h2s, h2r)
    edges.start()

    @pl.when(j == 0)
    def _():
        bext[0:HALO, :] = jnp.zeros((HALO, CH), BF)

    @pl.when(j == SEQ - 1)
    def _():
        bext[HALO + ROWS :, :] = jnp.zeros((HALO, CH), BF)

    def take(buf, ss, rs):
        for off in reversed(FAR):
            zz, dev = ring(off)
            rcopy(buf.at[zz], buf.at[zz], ss.at[zz], rs.at[zz], dev).wait_recv()
        total = buf[0].astype(F32)
        for i in range(1, ZS):
            total = total + buf[i].astype(F32)
        return total.astype(BF)

    rq[z] = gown[pl.ds(3 * z, 3)]
    redp[...] = take(rq, rqs, rqr)
    rp_copy = rcopy(redp, redr, rps.at[0], rpr.at[0], partner)
    rp_copy.start()

    rp_copy.wait_recv()
    red[...] = (redp[...].astype(F32) + redr[...].astype(F32)).astype(BF)

    def red_copy(i, off):
        hc = 3 * z + i
        unit = SEQ * (hc // 8) + j
        row = (unit % 3) * 8 + hc % 8
        zz = (z + off) % ZS
        dev = {"dp": 2 * zz + xl, "seq": unit // 3}
        return rcopy(red.at[i], gfin.at[row], gus.at[i, zz], gur.at[row], dev), unit // 3, row

    for i in range(3):
        for off in FAR:
            red_copy(i, off)[0].start()
        cp, owner, row = red_copy(i, 0)
        pl.when(owner != j)(cp.start)

        @pl.when(owner == j)
        def _(i=i, row=row):
            gfin[row] = red[i]

    def b_wait(b):
        wait_slot(bh, bs, br, b)

    loop(CHIPS, b_wait)
    for b in range(CHIPS):
        bt[:, b * ROWS : (b + 1) * ROWS] = bh[b]

    def cp_copy(o):
        return rcopy(cst.at[o], crcv.at[o], cps.at[o], cpr.at[o], mate)

    for o in range(2):
        n = 1 - xl if o == 0 else xl
        lanes = pl.ds(pl.multiple_of(n * PART, PART), PART)
        for t in range(TAPS):
            cg[o, t * 96 : t * 96 + 96, :] = dot(bt[...], ag[t * GAP : t * GAP + HALF, lanes])
        for t in range(TAPS):
            rows = pl.ds(pl.multiple_of(t * 96 + (1 - k) * 48, 48), 48)
            cst[o, t * 3 : t * 3 + 3] = cg[o, rows, :].astype(BF).reshape(3, 16, PART)
        cp_copy(o).start()

    give_c[15] = jnp.zeros((16, PART), BF)
    keep_c[15] = jnp.zeros((16, PART), F32)

    def with_mate(o):
        cp_copy(o).wait_recv()
        for t in range(TAPS):
            rows = pl.ds(pl.multiple_of(t * 96 + k * 48, 48), 48)
            own = cg[o, rows, :].reshape(3, 16, PART)
            both = own + crcv[o, t * 3 : t * 3 + 3].astype(F32)
            if o == 0:
                give_c[t * 3 : t * 3 + 3] = both.astype(BF)
            else:
                keep_c[t * 3 : t * 3 + 3] = both

    def px_copy(h, off):
        zz, _ = ring(off)
        return rcopy(give_c.at[2 * zz + h], px.at[h, zz], pxs.at[h, zz], pxr.at[h, zz], partner)

    with_mate(0)
    for h in range(2):
        for off in FAR + (0,):
            px_copy(h, off).start()
    with_mate(1)

    def rc_copy(h, off):
        zz, dev = ring(off)
        return rcopy(zs.at[h, zz], rc.at[h, z], rcs.at[h, zz], rcr.at[h, z], dev)

    for h in range(2):
        for off in FAR + (0,):
            zz, _ = ring(off)
            px_copy(h, off).wait_recv()
            both = (keep_c[2 * zz + h] + px[h, zz].astype(F32)).astype(BF)
            if off:
                zs[h, zz] = both
                rc_copy(h, off).start()
            else:
                rc[h, z] = both

    def piece(n, h, zz):
        return cfin.at[n, 2 * zz + h]

    def fz_copy(h, off):
        zz, dev = ring(off)
        return rcopy(piece(xl, h, z), piece(xl, h, z), fzs.at[h, zz], fzr.at[h, z], dev)

    def fx_copy(h, zz):
        return rcopy(piece(xl, h, zz), piece(xl, h, zz), fxs.at[h, zz], fxr.at[h, zz], partner)

    for h in range(2):
        cfin[xl, 2 * z + h] = take(rc.at[h], rcs.at[h], rcr.at[h])
        for off in FAR:
            fz_copy(h, off).start()
        fx_copy(h, z).start()
    edges.wait_recv()
    ga = jnp.zeros((ROWS, CH), F32)
    for t in range(TAPS):
        lo = (TAPS - 1 - t) * GAP
        ga = ga + dot_nt(bext[lo : lo + ROWS, :], cwv[t])
    x = x_ref[...].astype(F32)
    th = gelu_tanh(x)
    slope = 0.5 * (1.0 + th) + 0.5 * x * (1.0 - th * th) * GELU_A * (1.0 + 3.0 * GELU_B * x * x)
    gi_ref[...] = (hid_s[...] + slope * ga).astype(BF)

    for h in range(2):
        for off in reversed(FAR):
            zz, _ = ring(off)
            here = piece(xl, h, zz)
            rcopy(here, here, fzs.at[0, 0], fzr.at[h, zz], partner).wait_recv()
            fx_copy(h, zz).start()

    def o_wait(chip):
        @pl.when(2 * chip + home != j)
        def _():
            lanes = pl.ds(pl.multiple_of(chip * HD, HD), HD)
            rcopy(obuf.at[0], att_ref.at[:, lanes], os_.at[0], or_.at[chip], mate).wait_recv()

    loop(CHIPS, o_wait)
    att_copy = pltpu.make_async_copy(att_ref, att_out, wsem.at[12])
    gi_copy = pltpu.make_async_copy(gi_ref, gi_out, wsem.at[13])
    att_copy.start()
    gi_copy.start()

    def land_q(row):
        u = 3 * j + row // 8
        hc = 8 * (u // SEQ) + row % 8

        @pl.when((u % SEQ != j) | (hc // 3 != z))
        def _():
            rcopy(red.at[0], gfin.at[row], gus.at[0, 0], gur.at[row], mate).wait_recv()

    loop(24, land_q)
    for r in range(3):
        for h in range(2):
            block = gfin[8 * r + 4 * h : 8 * r + 4 * h + 4].astype(F32).reshape(64, PART)
            gqf[64 * r : 64 * r + 64, h * PART : (h + 1) * PART] = block
    gq_copy = pltpu.make_async_copy(gqf, gq_out, wsem.at[14])
    gq_copy.start()
    def land_c(i):
        here = piece(1 - xl, i // ZS, i % ZS)
        rcopy(here, here, fzs.at[0, 0], fxr.at[i // ZS, i % ZS], partner).wait_recv()

    def write_taps(n):
        ctf[n] = cfin[n, :15].astype(F32).reshape(240, PART)
        lanes = pl.ds(pl.multiple_of(n * PART, PART), PART)
        copy = pltpu.make_async_copy(ctf.at[n], ct_out.at[:, lanes], wsem.at[15 + n])
        copy.start()
        return copy

    ct_own = write_taps(xl)
    loop(2 * ZS, land_c)
    ct_other = write_taps(1 - xl)

    for g in range(GROUPS):
        x_left(g)
        pl.when(home != k)(lambda g=g: x_copy(g, 4).wait_send())
        for e in range(2):
            pass_copy(g, e, flip_x, 0).wait_send()
            pl.when(inside)(lambda g=g, e=e: pass_copy(g, e, flip_x, 1).wait_send())
    edge_copy.wait_send()
    to_worker_done(do_copy)
    to_worker_done(b_copy)
    pl.when(k == c // 4)(lambda: hd_copy.wait_send())
    edges.wait_send()

    def mates(p):
        kv_copy(p).wait_send()
        pr_copy(p).wait_send()

    loop(TILES, mates)

    def given(b):
        @pl.when(owner_of(b) != j)
        def _():
            o_copy(b).wait_send()
            kv_back(b).wait_send()
            dq_copy(b).wait_send()

    loop(CHIPS, given)
    gp_copy.wait_send()

    rp_copy.wait_send()
    for i in range(3):
        for off in FAR:
            red_copy(i, off)[0].wait_send()
        cp, owner, _ = red_copy(i, 0)
        pl.when(owner != j)(cp.wait_send)
    for o in range(2):
        cp_copy(o).wait_send()
    for off in FAR:
        rq_copy(off).wait_send()
        rc_copy(0, off).wait_send()
        rc_copy(1, off).wait_send()
    for off in range(ZS):
        px_copy(0, off).wait_send()
        px_copy(1, off).wait_send()
        for h in range(2):
            fx_copy(h, ring(off)[0]).wait_send()
            if off:
                fz_copy(h, off).wait_send()

    for copy in (att_copy, gi_copy, gq_copy, ct_own, ct_other):
        copy.wait()


def finish(a, b, c, d, a_out, b_out, c_out, d_out, a_buf, b_buf, c_buf, d_buf, sem):
    parts = ((a, a_buf, a_out), (b, b_buf, b_out), (c, c_buf, c_out), (d, d_buf, d_out))
    reads = [pltpu.make_async_copy(src, buf, sem.at[i]) for i, (src, buf, _) in enumerate(parts)]
    writes = [pltpu.make_async_copy(buf, dst, sem.at[4 + i]) for i, (_, buf, dst) in enumerate(parts)]
    for copy in reads:
        copy.start()
    for i in range(4):
        reads[i].wait()
        writes[i].start()
    for copy in writes:
        copy.wait()


def body(inputs, convolution_weight, w_qkv, gain, out_grad):
    hbm = pl.BlockSpec(memory_space=pl.ANY)
    V = pltpu.VMEM

    def sem(*n):
        return pltpu.SemaphoreType.DMA(n)

    scratch = [
        V((ROWS, INNER), BF),
        V((ROWS, CH), BF),
        V((2, 16, 16, PART), BF),
        V((24, 16, PART), BF),
        V((2, 240, PART), F32),
        V((192, CH), F32),
        V((ROWS, CH), BF),
        V((CH,), F32),
        V((ROWS, INNER), BF),
        V((TAPS, CH, CH), BF),
        V((CH, 3 * INNER), BF),
        V((CH, 3 * HD), BF),
        V((GROUPS, CHIPS, ROWS, WIDE), BF),
        V((HALF + 2 * HALO, CH), BF),
        V((TILES, TILE + 2 * PAD, CH), BF),
        V((HALO + 2 * PAD, CH), BF),
        V((HALF + 2 * HALO, CH), F32),
        V((ROWS, CH), F32),
        V((ROWS, CH), F32),
        V((TILES, TILE, CH), BF),
        V((CHIPS, ROWS, HD), BF),
        V((TILES, HD, TILE), BF),
        V((HALF, HD), BF),
        V((TILES, HD, TILE), BF),
        V((2, TILES, TILE, 2 * HD), BF),
        V((2 * TILES, HD, TILE), BF),
        V((2 * TILES, TILE, HALF), BF),
        V((2, 8, HALF), F32),
        V((TILES, HD, TILE), BF),
        V((HALF, HD), BF),
        V((HD, HALF), F32),
        V((TILES, 2, TILE, HD), F32),
        V((TILES, 2, TILE, HD), F32),
        V((CHIPS, ROWS, HD), BF),
        V((CHIPS, ROWS, HD), BF),
        V((CHIPS, 2, ROWS, HD), BF),
        V((TILES, 3 * HD, TILE), BF),
        V((HEADS, 3, ROWS, HD), BF),
        V((3 * HD, CH), F32),
        V((12, 16, CH), BF),
        V((12, 16, CH), BF),
        V((24, 16, PART), BF),
        V((ZS, 3, 16, PART), BF),
        V((3, 16, PART), BF),
        V((3, 16, PART), BF),
        V((3, 16, PART), BF),
        V((ROWS + 2 * HALO, CH), BF),
        V((CHIPS, 96, ROWS), BF),
        V((CHIPS, 96, ROWS), BF),
        V((96, HALF), BF),
        V((2, TAPS * 96, PART), F32),
        V((2, 15, 16, PART), BF),
        V((2, 15, 16, PART), BF),
        V((16, 16, PART), BF),
        V((16, 16, PART), F32),
        V((2, ZS, 16, PART), BF),
        V((2, ZS, 16, PART), BF),
        V((2, ZS, 16, PART), BF),
        sem(17),
        sem(3, 5), sem(3, 8), sem(3, 2, 2), sem(1), sem(1),
        sem(8), sem(8), sem(1), sem(1),
        sem(4), sem(4), sem(8), sem(8), sem(8), sem(8), sem(8), sem(8), sem(4), sem(4),
        sem(1), sem(1), sem(8), sem(8), sem(1), sem(1), sem(3, 8), sem(24),
        sem(2), sem(2), sem(8), sem(8), sem(2), sem(2),
        sem(2, 8), sem(2, 8), sem(2, 8), sem(2, 8), sem(2, 8), sem(2, 8),
        sem(2, 8), sem(2, 8),
    ]
    att, gi, cfin, gfin = pl.pallas_call(
        kernel,
        out_shape=[
            jax.ShapeDtypeStruct((ROWS, INNER), BF),
            jax.ShapeDtypeStruct((ROWS, CH), BF),
            jax.ShapeDtypeStruct((240, CH), F32),
            jax.ShapeDtypeStruct((192, CH), F32),
        ],
        in_specs=[hbm] * 5,
        out_specs=[hbm] * 4,
        scratch_shapes=scratch,
        compiler_params=pltpu.CompilerParams(
            collective_id=0, has_side_effects=True, vmem_limit_bytes=58 * 1024 * 1024
        ),
        cost_estimate=pl.CostEstimate(flops=14_000_000_000, bytes_accessed=15_000_000, transcendentals=3_000_000),
    )(inputs[0], gain, out_grad[0], convolution_weight, w_qkv)
    att, gi, conv, qkv = pl.pallas_call(
        finish,
        out_shape=[
            jax.ShapeDtypeStruct((ROWS, INNER), BF),
            jax.ShapeDtypeStruct((ROWS, CH), BF),
            jax.ShapeDtypeStruct((240, CH), F32),
            jax.ShapeDtypeStruct((192, CH), F32),
        ],
        in_specs=[hbm] * 4,
        out_specs=[hbm] * 4,
        scratch_shapes=[V((ROWS, INNER), BF), V((ROWS, CH), BF), V((240, CH), F32), V((192, CH), F32), sem(8)],
    )(att, gi, cfin, gfin)
    return att[None], gi[None], conv.reshape(TAPS, 48, CH).transpose(0, 2, 1), qkv.T


def solution(mesh):
    in_specs = (P("dp", "seq", None), P(), P(), P(), P("dp", "seq", None))
    out_specs = (P("dp", "seq", None), P("dp", "seq", None), P(None, None, "seq"), P(None, "seq"))
    return jax.shard_map(body, mesh=mesh, in_specs=in_specs, out_specs=out_specs, check_vma=False)
```

```python
import jax
import jax.numpy as jnp
from jax import lax
from jax.experimental import pallas as pl
from jax.experimental.pallas import tpu as pltpu
from jax.sharding import PartitionSpec as P

CH = 768
HEADS = 8
HD = 128
INNER = HEADS * HD
TAPS = 5
GAP = 16
HALO = 32
PAD = 2 * HALO
ROWS = 128
SEQ = 16
DP = 16
ZS = 8
CHIPS = 8
HALF = CHIPS * ROWS
TILE = 256
TILES = HALF // TILE
PART = 384
GROUPS = 3
WIDE = CH // GROUPS
TEMPER = HD ** (-0.5)
LOG2E = 1.4426950408889634
GELU_A = 0.7978845608028654
GELU_B = 0.044715
BF = jnp.bfloat16
F32 = jnp.float32
MESH = pl.DeviceIdType.MESH


def rcopy(src, dst, ss, rs, dev):
    return pltpu.make_async_remote_copy(
        src_ref=src, dst_ref=dst, send_sem=ss, recv_sem=rs, device_id=dev, device_id_type=MESH
    )


def dot(a, b):
    return jnp.dot(a, b, preferred_element_type=F32)


def dot_nt(a, b):
    return lax.dot_general(a, b, (((1,), (1,)), ((), ())), preferred_element_type=F32)


def flip(a):
    return a.astype(F32).T


def gelu_tanh(x):
    return jnp.tanh(GELU_A * (x + GELU_B * x * x * x))


def gelu(x):
    x = x.astype(F32)
    return (0.5 * x * (1.0 + gelu_tanh(x))).astype(BF)


def loop(n, step):
    lax.fori_loop(0, n, lambda i, carry: (step(i), carry)[1], 0)


def kernel(
    x_hbm, gain_hbm, og_hbm, cw_hbm, w_hbm,
    att_out, gi_out, ct_out, gq_out,
    att_ref, gi_ref, cfin, gfin, ctf, gqf, x_ref, gain_ref, og_ref, cwv, wfull, wh, xg, ag, apad, epad, acc_s, gn_s, hid_s, nh, doh, dot_s, qd, qt_s, kv, vt_s,
    wts, stat_s, ot_s, dor_s, dqt, dkvp, pr, obuf, dqb, gsrc, gt, res, gtf, gst, grcv, gown,
    rq, redp, redr, red, bext, bst, bh, bt, cg, cst, crcv, give_c, keep_c, px, zs, rc,
    wsem, xs, xr, xps, xhs, xhr, dos, dor, hds, hdr, kvs, kvr, os_, or_, dqs, dqr, ks, kr, prs, prr,
    gps, gpr, rqs, rqr, rps, rpr, gus, gur, h2s, h2r, bs, br, cps, cpr,
    pxs, pxr, rcs, rcr, fzs, fzr, fxs, fxr,
):
    j = lax.axis_index("seq")
    d = lax.axis_index("dp")
    c = j // 2
    k = j % 2
    mate = {"seq": j + 1 - 2 * k}
    home = j // CHIPS
    slot = j % CHIPS
    col = pl.multiple_of(c * HD, HD)

    barrier = pltpu.get_barrier_semaphore()

    def hello(i):
        pl.semaphore_signal(barrier, inc=1, device_id={"seq": (j + i + 1) % SEQ}, device_id_type=MESH)
        pl.semaphore_signal(barrier, inc=1, device_id={"dp": (d + i + 1) % DP}, device_id_type=MESH)

    loop(15, hello)
    x_in = pltpu.make_async_copy(x_hbm, x_ref, wsem.at[9])
    og_in = pltpu.make_async_copy(og_hbm, og_ref, wsem.at[10])
    gain_in = pltpu.make_async_copy(gain_hbm, gain_ref, wsem.at[11])
    x_in.start()
    og_in.start()
    gain_in.start()
    for t in range(TAPS):
        pltpu.make_async_copy(cw_hbm.at[t], cwv.at[t], wsem.at[t]).start()
    for p in range(3):
        pltpu.make_async_copy(
            w_hbm.at[:, pl.ds(p * INNER + col, HD)], wh.at[:, pl.ds(p * HD, HD)], wsem.at[5 + p]
        ).start()
    wf_copy = pltpu.make_async_copy(w_hbm, wfull, wsem.at[8])
    wf_copy.start()

    dqt[...] = jnp.zeros_like(dqt)
    acc_s[...] = jnp.zeros_like(acc_s)
    for p in range(TILES):
        apad[p, :PAD, :] = jnp.zeros((PAD, CH), BF)
        apad[p, PAD + TILE :, :] = jnp.zeros((PAD, CH), BF)
    epad[:PAD, :] = jnp.zeros((PAD, CH), BF)
    epad[PAD + HALO :, :] = jnp.zeros((PAD, CH), BF)

    @pl.when(k == 0)
    def _():
        ag[0:HALO, :] = jnp.zeros((HALO, CH), BF)

    @pl.when(k == 1)
    def _():
        ag[HALO + HALF :, :] = jnp.zeros((HALO, CH), BF)

    pl.semaphore_wait(barrier, 30)

    def to_worker(copy, local):
        def step(i):
            chip = (c + CHIPS - 1 - i) % CHIPS
            dev = 2 * chip + home

            @pl.when(dev != j)
            def _():
                copy(chip, {"seq": dev}).start()

            if local is not None:
                pl.when(dev == j)(lambda: local(chip))

        loop(CHIPS, step)

    def to_worker_done(copy):
        def step(chip):
            dev = 2 * chip + home

            @pl.when(dev != j)
            def _():
                copy(chip, {"seq": dev}).wait_send()

        loop(CHIPS, step)

    def owner_of(b):
        return CHIPS * k + b

    flip_x = c + 1 - 2 * (c % 2)
    near = (flip_x, (c + 2) % CHIPS, (c + 6) % CHIPS, (c + 4) % CHIPS, c)

    def x_copy(g, i):
        src = x_ref.at[:, g * WIDE : (g + 1) * WIDE]
        return rcopy(src, xg.at[g, slot], xs.at[g, i], xr.at[g, slot], {"seq": 2 * near[i] + home})

    def x_left(g):
        for i in range(4):
            x_copy(g, i).wait_send()

    def send_x(g):
        for i in range(4):
            x_copy(g, i).start()
        pl.when(home != k)(lambda: x_copy(g, 4).start())

        @pl.when(home == k)
        def _():
            xg[g, slot] = x_ref[:, g * WIDE : (g + 1) * WIDE]

    x_in.wait()
    send_x(0)
    x_left(0)
    send_x(1)

    inside = c // 4 == k
    passed = jnp.where(inside, flip_x, (c + 4) % CHIPS) - 4 * k

    def pass_copy(g, e, chip, i):
        b = 2 * passed + e
        return rcopy(xg.at[g, b], xg.at[g, b], xps.at[g, e, i], xr.at[g, b], {"seq": 2 * chip + k})

    def hand_on(g, e):
        b = 2 * passed + e
        rcopy(xg.at[g, b], xg.at[g, b], xps.at[g, e, 0], xr.at[g, b], mate).wait_recv()

        @pl.when(inside)
        def _():
            pass_copy(g, e, near[1], 0).start()
            pass_copy(g, e, near[2], 1).start()

        pl.when(c // 4 != k)(lambda: pass_copy(g, e, flip_x, 0).start())

    def relay(g):
        hand_on(g, 0)
        hand_on(g, 1)

    def wait_slot(buf, ss, rs, b):
        @pl.when(owner_of(b) != j)
        def _():
            rcopy(buf.at[b], buf.at[b], ss.at[0], rs.at[b], mate).wait_recv()

    def kv_copy(p):
        return rcopy(kv.at[k, p], kv.at[k, p], kvs.at[p], kvr.at[p], mate)

    def do_copy(chip, dev):
        src = og_ref.at[:, pl.ds(pl.multiple_of(chip * HD, HD), HD)]
        return rcopy(src, doh.at[slot], dos.at[chip], dor.at[slot], dev)

    def do_local(chip):
        doh[slot] = og_ref[:, pl.ds(pl.multiple_of(chip * HD, HD), HD)]

    edge_copy = rcopy(
        apad.at[3 - 3 * k, pl.ds(pl.multiple_of(PAD + (TILE - HALO) * (1 - k), HALO), HALO)],
        epad.at[pl.ds(PAD, HALO)], xhs.at[0], xhr.at[0], mate,
    )
    def unit(g, direct):
        lanes = slice(g * WIDE, (g + 1) * WIDE)
        low = c % 2 if direct else 1 - c % 2
        for q in range(2):
            p = low + 2 * q
            for e in range(2):
                b = 2 * p + e

                @pl.when((owner_of(b) != j) & (p != passed))
                def _(b=b):
                    rcopy(xg.at[g, b], xg.at[g, b], xps.at[g, 0, 0], xr.at[g, b], mate).wait_recv()

            rows = gelu(xg[g, pl.ds(2 * p, 2)].reshape(TILE, WIDE))
            apad[p, PAD : PAD + TILE, lanes] = rows
            ag[pl.ds(pl.multiple_of(HALO + p * TILE, HALO), TILE), lanes] = rows
        if g == GROUPS - 1 and not direct:
            edge_copy.start()
        weights = cwv[:, lanes, :].reshape(TAPS * WIDE, CH)
        for q in range(2):
            p = low + 2 * q
            windows = [apad[p, t * GAP : t * GAP + TILE + PAD, lanes] for t in range(TAPS)]
            rows = pl.ds(pl.multiple_of(p * TILE, TILE), TILE + PAD)
            acc_s[rows, :] = acc_s[rows, :] + dot(jnp.concatenate(windows, axis=1), weights)

    for t in range(TAPS):
        pltpu.make_async_copy(cw_hbm.at[t], cwv.at[t], wsem.at[t]).wait()
    relay(0)
    unit(0, True)
    x_left(1)
    send_x(2)
    relay(1)
    unit(1, True)
    unit(0, False)
    relay(2)
    og_in.wait()
    to_worker(do_copy, do_local)
    unit(2, True)
    unit(1, False)
    gain_in.wait()
    unit(2, False)

    for p in range(3):
        pltpu.make_async_copy(
            w_hbm.at[:, pl.ds(p * INNER + col, HD)], wh.at[:, pl.ds(p * HD, HD)], wsem.at[5 + p]
        ).wait()

    def finish_rows(p):
        rows = pl.ds(pl.multiple_of(HALO + p * 2 * TILE, HALO), 2 * TILE)
        x = jnp.concatenate([xg[g, pl.ds(4 * p, 4)].reshape(2 * TILE, WIDE) for g in range(GROUPS)], axis=1)
        acc = acc_s[rows, :] + x.astype(F32)
        acc_s[rows, :] = acc
        inv = lax.rsqrt(jnp.mean(acc * acc, -1, keepdims=True) + 1e-6)
        rows_bf = (acc * inv * gain_ref[...].reshape(1, CH)).astype(BF)
        nh[pl.ds(2 * p, 2)] = rows_bf.reshape(2, TILE, CH)
        outb = dot(rows_bf, wh[...]).astype(BF)
        kv[k, pl.ds(2 * p, 2)] = outb[:, HD:].reshape(2, TILE, 2 * HD)
        qd[pl.ds(pl.multiple_of(p * 2 * TILE, TILE), 2 * TILE), :] = outb[:, :HD]
        for e in range(2):
            qt_s[2 * p + e] = outb[e * TILE : (e + 1) * TILE, :HD].T
            vt_s[k * TILES + 2 * p + e] = outb[e * TILE : (e + 1) * TILE, 2 * HD :].T
        kv_copy(2 * p).start()
        kv_copy(2 * p + 1).start()

    finish_rows(k)
    edge_copy.wait_recv()
    ag[pl.ds(pl.multiple_of((HALF + HALO) * (1 - k), HALO), HALO), :] = epad[PAD : PAD + HALO, :]
    windows = [epad[pl.ds(pl.multiple_of((3 + k + q) * GAP, GAP), HALO), :] for q in range(2)]
    part = dot(jnp.concatenate(windows, axis=1), cwv[pl.ds(3 - 3 * k, 2)].reshape(2 * CH, CH))
    rows = pl.ds(pl.multiple_of(HALF - (HALF - HALO) * k, HALO), HALO)
    acc_s[rows, :] = acc_s[rows, :] + part
    finish_rows(1 - k)

    def hidden_rows(core):
        return acc_s.at[pl.ds(pl.multiple_of(HALO + (c % 4) * TILE + core * ROWS, HALO), ROWS)]

    hd_copy = rcopy(hidden_rows(1 - k), hid_s, hds.at[0], hdr.at[0], mate)

    @pl.when(k == c // 4)
    def _():
        hd_copy.start()
        hid_s[...] = hidden_rows(k)[...]

    def other_keys(p):
        rcopy(kv.at[1 - k, p], kv.at[1 - k, p], kvs.at[p], kvr.at[p], mate).wait_recv()
        vt_s[(1 - k) * TILES + p] = kv[1 - k, p, :, HD:].T

    loop(TILES, other_keys)

    def give(copy, local, p):
        for e in range(2):
            b = 2 * p + e
            pl.when(owner_of(b) != j)(lambda b=b: copy(b).start())
            pl.when(owner_of(b) == j)(lambda b=b: local(b))

    def o_copy(b):
        return rcopy(
            obuf.at[b], att_ref.at[:, pl.ds(col, HD)], os_.at[b], or_.at[c], {"seq": owner_of(b)}
        )

    def o_local(b):
        att_ref[:, pl.ds(col, HD)] = obuf[b]

    def forward(t):
        qt = qt_s[t]
        top = None
        for i in range(2 * TILES):
            s = dot(kv[i // TILES, i % TILES, :, :HD], qt)
            part = jnp.max(s.reshape(TILE // 8, 8, TILE), axis=0)
            top = part if top is None else jnp.maximum(top, part)
        top = jnp.max(top, axis=0, keepdims=True) * (TEMPER * LOG2E)
        total = jnp.zeros((8, TILE), F32)
        ot = jnp.zeros((HD, TILE), F32)
        lanes = pl.ds(pl.multiple_of(t * TILE, TILE), TILE)
        for i in range(2 * TILES):
            s = dot(kv[i // TILES, i % TILES, :, :HD], qt)
            p = jnp.exp2(s * (TEMPER * LOG2E) - top)
            total = total + jnp.sum(p.reshape(TILE // 8, 8, TILE), axis=0)
            pb = p.astype(BF)
            wts[i, :, lanes] = pb
            ot = ot + dot(vt_s[i], pb)
        rec = 1.0 / jnp.sum(total, axis=0, keepdims=True)
        otb = (ot * rec).astype(BF)
        ot_s[t] = otb
        stat_s[0, :, lanes] = jnp.broadcast_to(rec, (8, TILE))
        obuf[pl.ds(2 * t, 2)] = otb.T.reshape(2, ROWS, HD)

    def turn(i, core):
        return (c + i + core) % TILES

    def forward_two(i):
        forward(turn(2 * i, k))
        forward(turn(2 * i + 1, k))
        give(o_copy, o_local, turn(2 * i, k))
        give(o_copy, o_local, turn(2 * i + 1, k))

    loop(TILES // 2, forward_two)

    loop(CHIPS, lambda b: wait_slot(doh, dos, dor, b))
    for t in range(TILES):
        lanes = slice(t * TILE, (t + 1) * TILE)
        got = doh[2 * t : 2 * t + 2].reshape(TILE, HD).T
        dot_s[t] = got
        go = got.astype(F32)
        dots = jnp.sum(go * ot_s[t].astype(F32), axis=0, keepdims=True)
        stat_s[1, :, lanes] = jnp.broadcast_to(dots, (8, TILE))
        dor_s[lanes, :] = (go * stat_s[0, 0:1, lanes]).T.astype(BF)

    def backward(h, m):
        g = h * TILES + m
        vc = kv[h, m, :, HD:]
        w = wts[g]
        parts = []
        for t in range(TILES):
            lanes = slice(t * TILE, (t + 1) * TILE)
            gw = dot(vc, dot_s[t])
            slope = (gw - stat_s[1, 0:1, lanes]) * stat_s[0, 0:1, lanes]
            parts.append((w[:, lanes].astype(F32) * slope).astype(BF))
        ds = jnp.concatenate(parts, axis=1)
        return dot(ds, qd[...]) * TEMPER, dot(w, dor_s[...]), kv[h, m, :, :HD].T, ds

    def add_queries(*parts):
        keys = jnp.concatenate([part[2] for part in parts], axis=1)
        dqt[...] = dqt[...] + dot(keys, jnp.concatenate([part[3] for part in parts], axis=0))

    def pr_copy(m):
        return rcopy(dkvp.at[m], pr.at[m], prs.at[m], prr.at[m], mate)

    def hand_over(m, part):
        dkvp[m, 0] = part[0]
        dkvp[m, 1] = part[1]
        pr_copy(m).start()

    early = backward(1 - k, turn(0, 1 - k))
    hand_over(turn(0, 1 - k), early)
    add_queries(early)

    def kv_back(b):
        return rcopy(
            gsrc.at[b], res.at[c, 1:3], ks.at[b], kr.at[c], {"seq": owner_of(b)}
        )

    def kv_local(b):
        res[c, 1:3] = gsrc[b]

    def complete(m, part):
        pr_copy(m).wait_recv()
        dk = part[0] + pr[m, 0]
        dv = part[1] + pr[m, 1]
        for e in range(2):
            gsrc[2 * m + e, 0] = dk[e * ROWS : (e + 1) * ROWS].astype(BF)
            gsrc[2 * m + e, 1] = dv[e * ROWS : (e + 1) * ROWS].astype(BF)
        give(kv_back, kv_local, m)
        gt[m, HD : 2 * HD, :] = dk.T.astype(BF)
        gt[m, 2 * HD :, :] = dv.T.astype(BF)

    def halves(i):
        ahead = backward(1 - k, turn(i + 1, 1 - k))
        own = backward(k, turn(i, k))
        add_queries(ahead, own)
        hand_over(turn(i + 1, 1 - k), ahead)
        complete(turn(i, k), own)

    loop(TILES - 1, halves)
    last = backward(k, turn(TILES - 1, k))
    add_queries(last)
    complete(turn(TILES - 1, k), last)

    def dq_copy(b):
        return rcopy(
            dqb.at[b], res.at[c, 0], dqs.at[b], dqr.at[c], {"seq": owner_of(b)}
        )

    def dq_local(b):
        res[c, 0] = dqb[b]

    def query_back(i):
        t = turn(i, k)
        dq = dqt[:, pl.ds(pl.multiple_of(t * TILE, TILE), TILE)] * TEMPER
        dqb[pl.ds(2 * t, 2)] = dq.T.astype(BF).reshape(2, ROWS, HD)
        give(dq_copy, dq_local, t)
        gt[t, :HD, :] = dq.astype(BF)

    loop(TILES, query_back)

    gtf[...] = dot(jnp.concatenate([gt[t] for t in range(TILES)], axis=1), nh[...].reshape(HALF, CH))
    for p in range(3):
        rows = pl.ds(pl.multiple_of(p * HD + (1 - k) * 64, 64), 64)
        gst[p * 4 : p * 4 + 4] = gtf[rows, :].astype(BF).reshape(4, 16, CH)
    gp_copy = rcopy(gst, grcv, gps.at[0], gpr.at[0], mate)
    gp_copy.start()
    gp_copy.wait_recv()
    for p in range(3):
        rows = pl.ds(pl.multiple_of(p * HD + k * 64, 64), 64)
        own = gtf[rows, :].reshape(4, 16, CH)
        both = own + grcv[p * 4 : p * 4 + 4].astype(F32)
        for h in range(2):
            gown[8 * p + 4 * h : 8 * p + 4 * h + 4] = both[:, :, h * PART : (h + 1) * PART].astype(BF)

    z = d // 2
    xl = d % 2
    partner = {"dp": d + 1 - 2 * xl}

    def ring(off):
        zz = (z + off) % ZS
        return zz, {"dp": 2 * zz + xl}

    FAR = (4, 3, 5, 2, 6, 1, 7)

    def rq_copy(off):
        zz, dev = ring(off)
        return rcopy(gown.at[pl.ds(3 * zz, 3)], rq.at[z], rqs.at[zz], rqr.at[z], dev)

    for off in FAR:
        rq_copy(off).start()

    def back(copy):
        def step(i):
            chip = (c + i) % CHIPS
            pl.when(2 * chip + home != j)(lambda: copy(chip).wait_recv())

        loop(CHIPS, step)

    @pl.when(k != c // 4)
    def _():
        hd_copy.wait_recv()

    wf_copy.wait()

    def heads(i):
        return jnp.concatenate([res[h, i] for h in range(HEADS)], axis=1)

    back(lambda chip: rcopy(gsrc.at[0], res.at[chip, 1:3], ks.at[0], kr.at[chip], mate))
    gn_s[...] = dot_nt(jnp.concatenate([heads(1), heads(2)], axis=1), wfull[:, INNER:])
    back(lambda chip: rcopy(dqb.at[0], res.at[chip, 0], dqs.at[0], dqr.at[chip], mate))
    gn = gn_s[...] + dot_nt(heads(0), wfull[:, :INNER])
    hidden = hid_s[...]
    inv = lax.rsqrt(jnp.mean(hidden * hidden, -1, keepdims=True) + 1e-6)
    normed = hidden * inv
    scaled = gn * gain_ref[...].reshape(1, CH)
    gh = inv * (scaled - normed * jnp.mean(scaled * normed, -1, keepdims=True))
    hid_s[...] = gh
    ghb = gh.astype(BF)
    bext[HALO : HALO + ROWS, :] = ghb

    bst[...] = gh.T.astype(BF).reshape(CHIPS, 96, ROWS)

    def b_copy(chip, dev):
        return rcopy(bst.at[chip], bh.at[slot], bs.at[chip], br.at[slot], dev)

    def b_local(chip):
        bh[slot] = bst[chip]

    to_worker(b_copy, b_local)

    class Edges:
        def __init__(self, buf, ss, rs):
            self.up = rcopy(
                buf.at[ROWS : ROWS + HALO], buf.at[0:HALO], ss.at[0], rs.at[0], {"seq": (j + 1) % SEQ}
            )
            self.down = rcopy(
                buf.at[HALO : 2 * HALO], buf.at[HALO + ROWS :], ss.at[1], rs.at[1], {"seq": (j + SEQ - 1) % SEQ}
            )

        def start(self):
            pl.when(j < SEQ - 1)(lambda: self.up.start())
            pl.when(j > 0)(lambda: self.down.start())

        def wait_recv(self):
            pl.when(j > 0)(lambda: self.up.wait_recv())
            pl.when(j < SEQ - 1)(lambda: self.down.wait_recv())

        def wait_send(self):
            pl.when(j < SEQ - 1)(lambda: self.up.wait_send())
            pl.when(j > 0)(lambda: self.down.wait_send())

    edges = Edges(bext, h2s, h2r)
    edges.start()

    @pl.when(j == 0)
    def _():
        bext[0:HALO, :] = jnp.zeros((HALO, CH), BF)

    @pl.when(j == SEQ - 1)
    def _():
        bext[HALO + ROWS :, :] = jnp.zeros((HALO, CH), BF)

    def take(buf, ss, rs):
        for off in reversed(FAR):
            zz, dev = ring(off)
            rcopy(buf.at[zz], buf.at[zz], ss.at[zz], rs.at[zz], dev).wait_recv()
        total = buf[0].astype(F32)
        for i in range(1, ZS):
            total = total + buf[i].astype(F32)
        return total.astype(BF)

    rq[z] = gown[pl.ds(3 * z, 3)]
    redp[...] = take(rq, rqs, rqr)
    rp_copy = rcopy(redp, redr, rps.at[0], rpr.at[0], partner)
    rp_copy.start()

    rp_copy.wait_recv()
    red[...] = (redp[...].astype(F32) + redr[...].astype(F32)).astype(BF)

    def red_copy(i, off):
        hc = 3 * z + i
        unit = SEQ * (hc // 8) + j
        row = (unit % 3) * 8 + hc % 8
        zz = (z + off) % ZS
        dev = {"dp": 2 * zz + xl, "seq": unit // 3}
        return rcopy(red.at[i], gfin.at[row], gus.at[i, zz], gur.at[row], dev), unit // 3, row

    for i in range(3):
        for off in FAR:
            red_copy(i, off)[0].start()
        cp, owner, row = red_copy(i, 0)
        pl.when(owner != j)(cp.start)

        @pl.when(owner == j)
        def _(i=i, row=row):
            gfin[row] = red[i]

    def b_wait(b):
        wait_slot(bh, bs, br, b)

    loop(CHIPS, b_wait)
    for b in range(CHIPS):
        bt[:, b * ROWS : (b + 1) * ROWS] = bh[b]

    def cp_copy(o):
        return rcopy(cst.at[o], crcv.at[o], cps.at[o], cpr.at[o], mate)

    for o in range(2):
        n = 1 - xl if o == 0 else xl
        lanes = pl.ds(pl.multiple_of(n * PART, PART), PART)
        for t in range(TAPS):
            cg[o, t * 96 : t * 96 + 96, :] = dot(bt[...], ag[t * GAP : t * GAP + HALF, lanes])
        for t in range(TAPS):
            rows = pl.ds(pl.multiple_of(t * 96 + (1 - k) * 48, 48), 48)
            cst[o, t * 3 : t * 3 + 3] = cg[o, rows, :].astype(BF).reshape(3, 16, PART)
        cp_copy(o).start()

    give_c[15] = jnp.zeros((16, PART), BF)
    keep_c[15] = jnp.zeros((16, PART), F32)

    def with_mate(o):
        cp_copy(o).wait_recv()
        for t in range(TAPS):
            rows = pl.ds(pl.multiple_of(t * 96 + k * 48, 48), 48)
            own = cg[o, rows, :].reshape(3, 16, PART)
            both = own + crcv[o, t * 3 : t * 3 + 3].astype(F32)
            if o == 0:
                give_c[t * 3 : t * 3 + 3] = both.astype(BF)
            else:
                keep_c[t * 3 : t * 3 + 3] = both

    def px_copy(h, off):
        zz, _ = ring(off)
        return rcopy(give_c.at[2 * zz + h], px.at[h, zz], pxs.at[h, zz], pxr.at[h, zz], partner)

    with_mate(0)
    for h in range(2):
        for off in FAR + (0,):
            px_copy(h, off).start()
    with_mate(1)

    def rc_copy(h, off):
        zz, dev = ring(off)
        return rcopy(zs.at[h, zz], rc.at[h, z], rcs.at[h, zz], rcr.at[h, z], dev)

    for h in range(2):
        for off in FAR + (0,):
            zz, _ = ring(off)
            px_copy(h, off).wait_recv()
            both = (keep_c[2 * zz + h] + px[h, zz].astype(F32)).astype(BF)
            if off:
                zs[h, zz] = both
                rc_copy(h, off).start()
            else:
                rc[h, z] = both

    def piece(n, h, zz):
        return cfin.at[n, 2 * zz + h]

    def fz_copy(h, off):
        zz, dev = ring(off)
        return rcopy(piece(xl, h, z), piece(xl, h, z), fzs.at[h, zz], fzr.at[h, z], dev)

    def fx_copy(h, zz):
        return rcopy(piece(xl, h, zz), piece(xl, h, zz), fxs.at[h, zz], fxr.at[h, zz], partner)

    for h in range(2):
        cfin[xl, 2 * z + h] = take(rc.at[h], rcs.at[h], rcr.at[h])
        for off in FAR:
            fz_copy(h, off).start()
        fx_copy(h, z).start()
    edges.wait_recv()
    ga = jnp.zeros((ROWS, CH), F32)
    for t in range(TAPS):
        lo = (TAPS - 1 - t) * GAP
        ga = ga + dot_nt(bext[lo : lo + ROWS, :], cwv[t])
    x = x_ref[...].astype(F32)
    th = gelu_tanh(x)
    slope = 0.5 * (1.0 + th) + 0.5 * x * (1.0 - th * th) * GELU_A * (1.0 + 3.0 * GELU_B * x * x)
    gi_ref[...] = (hid_s[...] + slope * ga).astype(BF)

    for h in range(2):
        for off in reversed(FAR):
            zz, _ = ring(off)
            here = piece(xl, h, zz)
            rcopy(here, here, fzs.at[0, 0], fzr.at[h, zz], partner).wait_recv()
            fx_copy(h, zz).start()

    def o_wait(chip):
        @pl.when(2 * chip + home != j)
        def _():
            lanes = pl.ds(pl.multiple_of(chip * HD, HD), HD)
            rcopy(obuf.at[0], att_ref.at[:, lanes], os_.at[0], or_.at[chip], mate).wait_recv()

    loop(CHIPS, o_wait)
    att_copy = pltpu.make_async_copy(att_ref, att_out, wsem.at[12])
    gi_copy = pltpu.make_async_copy(gi_ref, gi_out, wsem.at[13])
    att_copy.start()
    gi_copy.start()

    def land_q(row):
        u = 3 * j + row // 8
        hc = 8 * (u // SEQ) + row % 8

        @pl.when((u % SEQ != j) | (hc // 3 != z))
        def _():
            rcopy(red.at[0], gfin.at[row], gus.at[0, 0], gur.at[row], mate).wait_recv()

    loop(24, land_q)
    for r in range(3):
        for h in range(2):
            block = gfin[8 * r + 4 * h : 8 * r + 4 * h + 4].astype(F32).reshape(64, PART)
            gqf[64 * r : 64 * r + 64, h * PART : (h + 1) * PART] = block
    gq_copy = pltpu.make_async_copy(gqf, gq_out, wsem.at[14])
    gq_copy.start()
    def land_c(i):
        here = piece(1 - xl, i // ZS, i % ZS)
        rcopy(here, here, fzs.at[0, 0], fxr.at[i // ZS, i % ZS], partner).wait_recv()

    def write_taps(n):
        ctf[n] = cfin[n, :15].astype(F32).reshape(240, PART)
        lanes = pl.ds(pl.multiple_of(n * PART, PART), PART)
        copy = pltpu.make_async_copy(ctf.at[n], ct_out.at[:, lanes], wsem.at[15 + n])
        copy.start()
        return copy

    ct_own = write_taps(xl)
    loop(2 * ZS, land_c)
    ct_other = write_taps(1 - xl)

    for g in range(GROUPS):
        if g == GROUPS - 1:
            x_left(g)
        pl.when(home != k)(lambda g=g: x_copy(g, 4).wait_send())
        for e in range(2):
            pass_copy(g, e, flip_x, 0).wait_send()
            pl.when(inside)(lambda g=g, e=e: pass_copy(g, e, flip_x, 1).wait_send())
    edge_copy.wait_send()
    to_worker_done(do_copy)
    to_worker_done(b_copy)
    pl.when(k == c // 4)(lambda: hd_copy.wait_send())
    edges.wait_send()

    def mates(p):
        kv_copy(p).wait_send()
        pr_copy(p).wait_send()

    loop(TILES, mates)

    def given(b):
        @pl.when(owner_of(b) != j)
        def _():
            o_copy(b).wait_send()
            kv_back(b).wait_send()
            dq_copy(b).wait_send()

    loop(CHIPS, given)
    gp_copy.wait_send()

    rp_copy.wait_send()
    for i in range(3):
        for off in FAR:
            red_copy(i, off)[0].wait_send()
        cp, owner, _ = red_copy(i, 0)
        pl.when(owner != j)(cp.wait_send)
    for o in range(2):
        cp_copy(o).wait_send()
    for off in FAR:
        rq_copy(off).wait_send()
        rc_copy(0, off).wait_send()
        rc_copy(1, off).wait_send()
    for off in range(ZS):
        px_copy(0, off).wait_send()
        px_copy(1, off).wait_send()
        for h in range(2):
            fx_copy(h, ring(off)[0]).wait_send()
            if off:
                fz_copy(h, off).wait_send()

    for copy in (att_copy, gi_copy, gq_copy, ct_own, ct_other):
        copy.wait()


def finish(a, b, c, d, a_out, b_out, c_out, d_out, a_buf, b_buf, c_buf, d_buf, sem):
    parts = ((a, a_buf, a_out), (b, b_buf, b_out), (c, c_buf, c_out), (d, d_buf, d_out))
    reads = [pltpu.make_async_copy(src, buf, sem.at[i]) for i, (src, buf, _) in enumerate(parts)]
    writes = [pltpu.make_async_copy(buf, dst, sem.at[4 + i]) for i, (_, buf, dst) in enumerate(parts)]
    for copy in reads:
        copy.start()
    for i in range(4):
        reads[i].wait()
        writes[i].start()
    for copy in writes:
        copy.wait()


def body(inputs, convolution_weight, w_qkv, gain, out_grad):
    hbm = pl.BlockSpec(memory_space=pl.ANY)
    V = pltpu.VMEM

    def sem(*n):
        return pltpu.SemaphoreType.DMA(n)

    scratch = [
        V((ROWS, INNER), BF),
        V((ROWS, CH), BF),
        V((2, 16, 16, PART), BF),
        V((24, 16, PART), BF),
        V((2, 240, PART), F32),
        V((192, CH), F32),
        V((ROWS, CH), BF),
        V((CH,), F32),
        V((ROWS, INNER), BF),
        V((TAPS, CH, CH), BF),
        V((CH, 3 * INNER), BF),
        V((CH, 3 * HD), BF),
        V((GROUPS, CHIPS, ROWS, WIDE), BF),
        V((HALF + 2 * HALO, CH), BF),
        V((TILES, TILE + 2 * PAD, CH), BF),
        V((HALO + 2 * PAD, CH), BF),
        V((HALF + 2 * HALO, CH), F32),
        V((ROWS, CH), F32),
        V((ROWS, CH), F32),
        V((TILES, TILE, CH), BF),
        V((CHIPS, ROWS, HD), BF),
        V((TILES, HD, TILE), BF),
        V((HALF, HD), BF),
        V((TILES, HD, TILE), BF),
        V((2, TILES, TILE, 2 * HD), BF),
        V((2 * TILES, HD, TILE), BF),
        V((2 * TILES, TILE, HALF), BF),
        V((2, 8, HALF), F32),
        V((TILES, HD, TILE), BF),
        V((HALF, HD), BF),
        V((HD, HALF), F32),
        V((TILES, 2, TILE, HD), F32),
        V((TILES, 2, TILE, HD), F32),
        V((CHIPS, ROWS, HD), BF),
        V((CHIPS, ROWS, HD), BF),
        V((CHIPS, 2, ROWS, HD), BF),
        V((TILES, 3 * HD, TILE), BF),
        V((HEADS, 3, ROWS, HD), BF),
        V((3 * HD, CH), F32),
        V((12, 16, CH), BF),
        V((12, 16, CH), BF),
        V((24, 16, PART), BF),
        V((ZS, 3, 16, PART), BF),
        V((3, 16, PART), BF),
        V((3, 16, PART), BF),
        V((3, 16, PART), BF),
        V((ROWS + 2 * HALO, CH), BF),
        V((CHIPS, 96, ROWS), BF),
        V((CHIPS, 96, ROWS), BF),
        V((96, HALF), BF),
        V((2, TAPS * 96, PART), F32),
        V((2, 15, 16, PART), BF),
        V((2, 15, 16, PART), BF),
        V((16, 16, PART), BF),
        V((16, 16, PART), F32),
        V((2, ZS, 16, PART), BF),
        V((2, ZS, 16, PART), BF),
        V((2, ZS, 16, PART), BF),
        sem(17),
        sem(3, 5), sem(3, 8), sem(3, 2, 2), sem(1), sem(1),
        sem(8), sem(8), sem(1), sem(1),
        sem(4), sem(4), sem(8), sem(8), sem(8), sem(8), sem(8), sem(8), sem(4), sem(4),
        sem(1), sem(1), sem(8), sem(8), sem(1), sem(1), sem(3, 8), sem(24),
        sem(2), sem(2), sem(8), sem(8), sem(2), sem(2),
        sem(2, 8), sem(2, 8), sem(2, 8), sem(2, 8), sem(2, 8), sem(2, 8),
        sem(2, 8), sem(2, 8),
    ]
    att, gi, cfin, gfin = pl.pallas_call(
        kernel,
        out_shape=[
            jax.ShapeDtypeStruct((ROWS, INNER), BF),
            jax.ShapeDtypeStruct((ROWS, CH), BF),
            jax.ShapeDtypeStruct((240, CH), F32),
            jax.ShapeDtypeStruct((192, CH), F32),
        ],
        in_specs=[hbm] * 5,
        out_specs=[hbm] * 4,
        scratch_shapes=scratch,
        compiler_params=pltpu.CompilerParams(
            collective_id=0, has_side_effects=True, vmem_limit_bytes=58 * 1024 * 1024
        ),
        cost_estimate=pl.CostEstimate(flops=14_000_000_000, bytes_accessed=15_000_000, transcendentals=3_000_000),
    )(inputs[0], gain, out_grad[0], convolution_weight, w_qkv)
    att, gi, conv, qkv = pl.pallas_call(
        finish,
        out_shape=[
            jax.ShapeDtypeStruct((ROWS, INNER), BF),
            jax.ShapeDtypeStruct((ROWS, CH), BF),
            jax.ShapeDtypeStruct((240, CH), F32),
            jax.ShapeDtypeStruct((192, CH), F32),
        ],
        in_specs=[hbm] * 4,
        out_specs=[hbm] * 4,
        scratch_shapes=[V((ROWS, INNER), BF), V((ROWS, CH), BF), V((240, CH), F32), V((192, CH), F32), sem(8)],
    )(att, gi, cfin, gfin)
    return att[None], gi[None], conv.reshape(TAPS, 48, CH).transpose(0, 2, 1), qkv.T


def solution(mesh):
    in_specs = (P("dp", "seq", None), P(), P(), P(), P("dp", "seq", None))
    out_specs = (P("dp", "seq", None), P("dp", "seq", None), P(None, None, "seq"), P(None, "seq"))
    return jax.shard_map(body, mesh=mesh, in_specs=in_specs, out_specs=out_specs, check_vma=False)
```
